256 devices in a mesh: dp: 32 (over x_hi, z, core), fsdp: 8 (over y, x_lo).
Axes of the slice: x: 4 (x_hi: 2, x_lo: 2; x = x_hi * 2 + x_lo), y: 4, z: 8, core: 2. Of those that a mesh axis runs over, the one named last changes fastest.
Arguments:
- tokens: bfloat16 [49152, 6144], P(('dp', 'fsdp')), may hold values from -6 to 6
- cotangent: bfloat16 [49152, 6144], P(('dp', 'fsdp')), may hold values from -24 to 24
- lengths: int32 [256, 3], P(('dp', 'fsdp')), may hold values from 0 to 80, as said below
- positions: int32 [2, 49152], P(None, ('dp', 'fsdp')), may hold values from 0 to 63, as said below
- weights: bfloat16 [4, 6144, 256], P(None, 'fsdp'), may hold values from -0.078125 to 0.078125
Outputs:
- grad_tokens: bfloat16 [49152, 6144], P(('dp', 'fsdp'))
- weight_grads: float32 [4, 6144, 256], P(None, 'fsdp')
The draws below stay inside these ranges and needn't reach their ends.
Inputs may be any that keep to these rules, and one draw needn't show every extreme that they name: Devices pair up: dp indices i and i + 16 with the same fsdp index. In every pair exactly one device holds more than 112 live patches; its third image is not empty, its first two images together hold at most 112 patches, and its partner's live patches plus that third image are at most 112. No device holds more than 192 live patches; the first pair's heavy device holds exactly 192. Every non-empty image has at least 10 patches; lengths are 0 only in the light device's third slot. `positions`: each image is laid out row by row with a width w of 2 to 64 patches (exactly 64 for images of 80 patches): its patch number k has row k // w and column k % w; padding rows hold 0.
All inputs are finite; a program needn't handle non-finite values.
Results may differ from the reference program's by a relative error of at most 0.015.
Values may be sent and summed in bfloat16 or wider, within the bound.
No kernel may reach another device: no remote copies, remote signals or barrier semaphores. Data moves between devices by JAX's collectives and lax.ppermute only.
A program may use at most 128 MiB of HBM per device.

```python
import math
import jax
import jax.numpy as jnp
from jax import lax

D = 6144
HD = 128
H = 2
TOK_DEV = 112
MAXLEN = 80
GRID = 64
MINLEN = 10
CAP = 192
TOTAL = 49152
DEVICES = 256


def make_lengths(key):
    key = jax.random.fold_in(key, 11)
    pair_count = DEVICES // 2
    subkeys = jax.random.split(key, 6)
    moved = jax.random.randint(subkeys[0], (pair_count,), MAXLEN // 2, MAXLEN + 1)
    moved = moved.at[0].set(MAXLEN)
    heavy_rest = jax.random.randint(subkeys[1], (pair_count,), TOK_DEV + 1 - moved, TOK_DEV + 1)
    heavy_rest = heavy_rest.at[0].set(TOK_DEV)
    low_first = jnp.maximum(MINLEN, heavy_rest - MAXLEN)
    high_first = jnp.minimum(MAXLEN, heavy_rest - MINLEN) + 1
    heavy_first = jax.random.randint(subkeys[2], (pair_count,), low_first, high_first)
    heavy_rows = jnp.stack([heavy_first, heavy_rest - heavy_first, moved], axis=1)
    room_left = TOK_DEV - moved
    light_first = jax.random.randint(subkeys[3], (pair_count,), MINLEN, jnp.minimum(MAXLEN, room_left - MINLEN) + 1)
    light_second = jax.random.randint(subkeys[4], (pair_count,), MINLEN, jnp.minimum(MAXLEN, room_left - light_first) + 1)
    light_rows = jnp.stack([light_first, light_second, jnp.zeros_like(light_first)], axis=1)
    upper_heavy = jax.random.randint(subkeys[5], (pair_count,), 0, 2)
    lower_member = jnp.where(upper_heavy[:, None] == 0, heavy_rows, light_rows)
    upper_member = jnp.where(upper_heavy[:, None] == 0, light_rows, heavy_rows)
    both_members = jnp.stack([lower_member, upper_member], axis=0)
    return both_members.reshape(DEVICES, 3).astype(jnp.int32)


def draw_lengths(key, part):
    return make_lengths(key)


def draw_positions(key, part):
    image_lengths = make_lengths(key)
    key = jax.random.fold_in(key, 23)
    width_top = jnp.maximum(jnp.minimum(GRID, image_lengths), 2) + 1
    widths = jax.random.randint(key, (DEVICES, 3), 2, width_top)
    widths = jnp.where(image_lengths == MAXLEN, GRID, widths)
    image_ends = jnp.cumsum(image_lengths, axis=1)
    image_starts = image_ends - image_lengths
    row_number = jnp.arange(CAP, dtype=jnp.int32)
    slot_number = jnp.sum((row_number[None, :, None] >= image_ends[:, None, :]).astype(jnp.int32), axis=2)
    live = slot_number < 3
    safe_slot = jnp.minimum(slot_number, 2)
    start_of = jnp.take_along_axis(image_starts, safe_slot, axis=1)
    width_of = jnp.take_along_axis(widths, safe_slot, axis=1)
    inside = row_number[None, :] - start_of
    row_place = jnp.where(live, inside // width_of, 0)
    col_place = jnp.where(live, inside % width_of, 0)
    return jnp.stack([row_place.reshape(-1), col_place.reshape(-1)], axis=0).astype(jnp.int32)


def with_spikes(entries, key, source, target, shards_of, factor):
    owner, partner = [(jnp.arange(entries.shape[axis_at]) // (entries.shape[axis_at] // shards_of)).reshape([-1 if axis == axis_at else 1 for axis in range(entries.ndim)]) for axis_at in (source, target)]
    chosen = jax.random.permutation(key, shards_of)[partner]
    strong = (owner == chosen) | (owner == (partner + shards_of // 2) % shards_of)
    return jnp.where(strong, factor * entries, entries)


def steps_of(rng, extent, cuts, smallest, largest):
    gain = 1.0
    for position, parts in cuts:
        steps = jax.random.uniform(jax.random.fold_in(jax.random.fold_in(rng, 6), position), (parts,), jnp.float32, smallest / len(cuts), largest / len(cuts))
        gain = gain * jnp.repeat(jnp.exp(steps), extent[position] // parts).reshape((-1,) + (1,) * (len(extent) - 1 - position))
    return gain


def noise(own_key, shape, scale, most, shards=(), kind=jnp.bfloat16):
    result = scale * jax.random.normal(own_key, shape, jnp.float32)
    if shards:
        result = result * steps_of(own_key, shape, shards, -0.22, 0.18)
    return jnp.clip(result, -most, most).astype(kind)


def noise_with(own_key, extent, scale, limit, shards, heavy, kind=jnp.bfloat16):
    array = scale * jax.random.normal(own_key, extent, jnp.float32)
    if shards:
        array = array * steps_of(own_key, extent, shards, -0.22, 0.18)
    return jnp.clip(with_spikes(array, jax.random.fold_in(own_key, 3), *heavy), -limit, limit).astype(kind)


def setup_inputs(seed: int = 0) -> dict:
    seeds = jax.random.split(jax.random.key(seed), 6)
    tokens = noise(seeds[0], (TOTAL, D), 1.0, 6.0, ((0, 256),))
    cotangent = noise_with(seeds[1], (TOTAL, D), 1.0, 24.0, ((0, 256),), (0, 1, 256, 6.0))
    lengths = draw_lengths(jax.random.fold_in(seeds[5], 71), 0)
    positions = draw_positions(jax.random.fold_in(seeds[5], 71), 0)
    weights = noise(seeds[4], (4, D, H * HD), D ** -0.5, 0.078125, ((1, 8),))
    return {"tokens": tokens, "cotangent": cotangent, "lengths": lengths, "positions": positions, "weights": weights}


rope_base = 100.0

def layer_norm(values):
    center = values - lax.optimization_barrier(jnp.mean(values, axis=-1, keepdims=True))
    return center * lax.rsqrt(lax.optimization_barrier(jnp.mean(center * center, axis=-1, keepdims=True)) + 1e-06)

def rotate(values, row_index, col_index):
    quarter = values.shape[-1] // 4
    frequency = rope_base ** (-jnp.arange(quarter, dtype=jnp.float32) / quarter)
    pieces = []
    for offset, where_at in ((0, row_index), (2 * quarter, col_index)):
        angles = where_at.astype(jnp.float32)[:, None, None] * frequency[None, None, :]
        cosine = jnp.cos(angles)
        sine_part = jnp.sin(angles)
        first_half = values[..., offset:offset + quarter]
        second = values[..., offset + quarter:offset + 2 * quarter]
        pieces.append(first_half * cosine - second * sine_part)
        pieces.append(second * cosine + first_half * sine_part)
    return jnp.concatenate(pieces, axis=-1)

def segment_ids(image_lengths, row_count):
    image_ends = jnp.cumsum(image_lengths)
    row_index = jnp.arange(row_count, dtype=jnp.int32)
    slot_number = lax.optimization_barrier(jnp.sum((row_index[:, None] >= image_ends[None, :]).astype(jnp.int32), axis=1))
    return jnp.where(slot_number < image_lengths.shape[0], slot_number, -1).astype(jnp.int32)

def attend(query_lin, key_lin, value_lin, row_index, col_index, segment):
    row_count = query_lin.shape[0]
    score_scale = 1.0 / math.sqrt(HD)
    queries = rotate(layer_norm(query_lin.reshape(row_count, -1, HD)), row_index, col_index).astype(jnp.bfloat16)
    keys_rot = rotate(layer_norm(key_lin.reshape(row_count, -1, HD)), row_index, col_index).astype(jnp.bfloat16)
    values = value_lin.reshape(row_count, -1, HD).astype(jnp.bfloat16)
    scores = jnp.einsum('qhd,khd->hqk', queries.astype(jnp.float32), keys_rot.astype(jnp.float32)) * score_scale
    same = (segment[:, None] == segment[None, :])[None, :, :]
    exponent = jnp.where(same, jnp.exp(scores), jnp.float32(0.0))
    probabilities = (exponent / lax.optimization_barrier(jnp.sum(exponent, axis=-1, keepdims=True))).astype(jnp.bfloat16)
    attended = jnp.einsum('hqk,khd->qhd', probabilities.astype(jnp.float32), values.astype(jnp.float32)).astype(jnp.bfloat16)
    return attended.reshape(row_count, -1)

def one_device(tokens, cotangent, image_lengths, row_index, col_index, weights):
    head_size = weights.shape[-1]
    model_width = weights.shape[1]
    segment = segment_ids(image_lengths, tokens.shape[0])
    grad_out = jnp.where((segment >= 0)[:, None], cotangent, jnp.zeros_like(cotangent))
    source = tokens.astype(jnp.float32)
    normed = layer_norm(source).astype(jnp.bfloat16)
    merged = jnp.transpose(weights[:3], (1, 0, 2)).reshape(model_width, 3 * head_size)
    linear = jnp.dot(normed, merged, preferred_element_type=jnp.float32)
    grad_attn = jnp.dot(grad_out, weights[3], preferred_element_type=jnp.float32).astype(jnp.bfloat16)

    def core(query_in, key_in, value_in):
        return attend(query_in, key_in, value_in, row_index, col_index, segment)
    attended, pullback = jax.vjp(core, linear[:, :head_size], linear[:, head_size:2 * head_size], linear[:, 2 * head_size:])
    grad_query, grad_key, grad_value = pullback(grad_attn)
    grad_linear = jnp.concatenate([grad_query, grad_key, grad_value], axis=1).astype(jnp.bfloat16)
    grad_normed = lax.dot_general(grad_linear, merged, (((1,), (1,)), ((), ())), preferred_element_type=jnp.float32)
    grad_proj = lax.dot_general(normed, grad_linear, (((0,), (0,)), ((), ())), preferred_element_type=jnp.float32)
    grad_output_w = lax.dot_general(grad_out, attended, (((0,), (0,)), ((), ())), preferred_element_type=jnp.float32)
    term_rows = jnp.concatenate([grad_proj, grad_output_w], axis=1)
    unused, norm_pull = jax.vjp(layer_norm, source)
    grad_tokens = norm_pull(grad_normed)[0].astype(jnp.bfloat16)
    return (grad_tokens, term_rows)

def reference(tokens, cotangent, lengths, positions, weights):
    head_size = weights.shape[-1]
    token_blocks = tokens.reshape(DEVICES, CAP, D)
    grad_blocks = cotangent.reshape(DEVICES, CAP, D)
    place_blocks = jnp.transpose(positions.reshape(2, DEVICES, CAP), (1, 0, 2))

    def step(carried, item):
        block_tokens, block_grads, block_lengths, block_places = item
        grad_tokens, term_rows = one_device(block_tokens, block_grads, block_lengths, block_places[0], block_places[1], weights)
        return (carried + term_rows, grad_tokens)
    start_sum = jnp.zeros((D, 4 * head_size), jnp.float32)
    total_sum, grad_all = lax.scan(step, start_sum, (token_blocks, grad_blocks, lengths, place_blocks))
    weight_grads = jnp.transpose(total_sum.reshape(D, 4, head_size), (1, 0, 2))
    return (grad_all.reshape(DEVICES * CAP, D), weight_grads)
```

```python
import functools
import math

import jax
import jax.numpy as jnp
from jax import lax
from jax.experimental import pallas as pl
from jax.experimental.pallas import tpu as pltpu
from jax.sharding import PartitionSpec as P

HD = 128
HEADS = 2
ROPE_BASE = 100.0
EPS = 1e-6
NX, NY, NZ = 4, 4, 8
REL = [(dy, dx) for dy in range(NY) for dx in range(2)]
BF16, F32 = jnp.bfloat16, jnp.float32


def flat_index(x, y, z, core):
    return ((x // 2) * 16 + z * 2 + core) * 8 + y * 2 + x % 2


def shift(values, dx=0, dy=0, dz=0, dc=0):
    pairs = []
    for x in range(NX):
        for y in range(NY):
            for z in range(NZ):
                for core in range(2):
                    target = flat_index((x + dx) % NX, (y + dy) % NY, (z + dz) % NZ, core ^ dc)
                    pairs.append((flat_index(x, y, z, core), target))
    return lax.ppermute(values, ("dp", "fsdp"), pairs)


def call(body, out_shapes, operands, scalars=0, scratch=(), flops=0, nbytes=0, name=None):
    specs = [
        pl.BlockSpec(memory_space=pltpu.SMEM if i < scalars else pltpu.VMEM) for i in range(len(operands))
    ]
    return pl.pallas_call(
        body,
        out_shape=out_shapes,
        in_specs=specs,
        out_specs=jax.tree.map(lambda _: pl.BlockSpec(memory_space=pltpu.VMEM), out_shapes),
        scratch_shapes=list(scratch),
        compiler_params=pltpu.CompilerParams(vmem_limit_bytes=56 * 1024 * 1024),
        cost_estimate=pl.CostEstimate(flops=flops, bytes_accessed=nbytes, transcendentals=0),
        name=name,
    )(*operands)


def shape(dims, dtype=BF16):
    return jax.ShapeDtypeStruct(dims, dtype)


def prep_kernel(width, offs, tokens, cot, x_own, x_send, c_own, c_send, normed):
    rows, model = tokens.shape
    step = 16

    def body(i, carry):
        at = pl.ds(pl.multiple_of(i * step, step), step)
        x = tokens[at, :].astype(F32)
        center = x - jnp.sum(x, axis=1, keepdims=True) / model
        var = jnp.sum(center * center, axis=1, keepdims=True) / model
        normed[at, :] = (center * lax.rsqrt(var + EPS)).astype(BF16)
        return carry

    lax.fori_loop(0, rows // step, body, 0)
    for j in range(8):
        own = pl.ds(pl.multiple_of(offs[j], 128), width)
        other = pl.ds(pl.multiple_of(offs[8 + j], 128), width)
        to = slice(j * width, (j + 1) * width)
        x_own[:, to] = normed[:, own]
        x_send[:, to] = normed[:, other]
        c_own[:, to] = cot[:, own]
        c_send[:, to] = cot[:, other]


def linear_kernel(width, x_own, x_peer, c_own, c_peer, *refs):
    shards, (lin_own, lin_peer) = refs[:-2], refs[-2:]
    rows = x_own.shape[0]
    cols = shards[0].shape[2]
    for m in range(4):
        a, b = (x_own, x_peer) if m < 3 else (c_own, c_peer)
        total = None
        for j in range(8):
            at = slice(j * width, (j + 1) * width)
            left = jnp.concatenate([a[:, at], b[:, at]], axis=0)
            term = jnp.dot(left, shards[2 * j + m // 2][m % 2], preferred_element_type=F32)
            total = term if total is None else total + term
        lin_own[:, m * cols : (m + 1) * cols] = total[:rows]
        lin_peer[:, m * cols : (m + 1) * cols] = total[rows:]


def swap_quarters(x):
    lane = lax.broadcasted_iota(jnp.int32, x.shape, 1)
    quarter = HD // 4
    up = pltpu.roll(x, HD - quarter, 1)
    down = pltpu.roll(x, quarter, 1)
    return jnp.where(lane % (2 * quarter) < quarter, up, down)


def mean_of(x):
    return jnp.sum(x, axis=1, keepdims=True) * (1.0 / HD)


def norm_rows(x):
    center = x - mean_of(x)
    scale = lax.rsqrt(mean_of(center * center) + EPS)
    return center * scale, scale


def norm_rows_back(g, hat, scale):
    return scale * (g - mean_of(g) - hat * mean_of(g * hat))


def dot_t(a, b, dims):
    return lax.dot_general(a, b, ((dims[0], dims[1]), ((), ())), preferred_element_type=F32)


def attend_kernel(ends, mine, theirs, cos_t, sin_t, out):
    rows = mine.shape[0]
    cols = HEADS * HD
    row_id = lax.broadcasted_iota(jnp.int32, (rows, 1), 0)
    col_id = lax.broadcasted_iota(jnp.int32, (1, rows), 1)

    def slot(ids):
        count = jnp.zeros(ids.shape, jnp.int32)
        for k in range(3):
            count = count + (ids >= ends[k]).astype(jnp.int32)
        return count

    row_slot, col_slot = slot(row_id), slot(col_id)
    same = row_slot == col_slot
    live = row_slot < 3
    cosine, sine = cos_t[...], sin_t[...]
    score_scale = 1.0 / math.sqrt(HD)
    for h in range(HEADS):

        def part(m):
            at = slice(m * cols + h * HD, m * cols + (h + 1) * HD)
            return mine[:, at] + theirs[:, at]

        q_hat, q_scale = norm_rows(part(0))
        k_hat, k_scale = norm_rows(part(1))
        q = (q_hat * cosine + swap_quarters(q_hat) * sine).astype(BF16)
        k = (k_hat * cosine + swap_quarters(k_hat) * sine).astype(BF16)
        v = part(2).astype(BF16)
        ga = jnp.where(live, part(3), 0.0).astype(BF16)
        scores = dot_t(q, k, ((1,), (1,))) * score_scale
        e = jnp.where(same, jnp.exp(scores), 0.0)
        p32 = e / jnp.sum(e, axis=1, keepdims=True)
        p = p32.astype(BF16)
        att = jnp.dot(p, v, preferred_element_type=F32).astype(BF16)
        gv = dot_t(p, ga, ((0,), (0,)))
        gp = dot_t(ga, v, ((1,), (1,))).astype(BF16).astype(F32)
        gs = p32 * (gp - jnp.sum(gp * p32, axis=1, keepdims=True)) * score_scale
        gs = gs.astype(BF16)
        gq = jnp.dot(gs, k, preferred_element_type=F32).astype(BF16).astype(F32)
        gk = dot_t(gs, q, ((0,), (0,))).astype(BF16).astype(F32)
        gq = norm_rows_back(gq * cosine + swap_quarters(gq * sine), q_hat, q_scale)
        gk = norm_rows_back(gk * cosine + swap_quarters(gk * sine), k_hat, k_scale)
        at = lambda m: slice(m * cols + h * HD, m * cols + (h + 1) * HD)
        out[:, at(0)] = gq.astype(BF16)
        out[:, at(1)] = gk.astype(BF16)
        out[:, at(2)] = gv.astype(BF16)
        out[:, at(3)] = jnp.where(live, att.astype(F32), 0.0).astype(BF16)


def terms_kernel(width, place, x_own, x_peer, c_own, c_peer, y_own, y_peer, *refs):
    first, second, acc = refs[:4], refs[4:8], refs[8]
    half = width // 2
    x_at, z_at = place[0], place[1]
    y_all = jnp.concatenate([y_own[...], y_peer[...]], axis=0)
    proj = 3 * HEADS * HD
    for j, (dy, dx) in enumerate(REL):
        at = slice(j * width, (j + 1) * width)
        left = jnp.concatenate([x_own[:, at], x_peer[:, at]], axis=0)
        value = dot_t(left, y_all[:, :proj], ((0,), (0,)))
        for n in range(6):
            acc[n] = value[:, n * 128 : (n + 1) * 128]
        left = jnp.concatenate([c_own[:, at], c_peer[:, at]], axis=0)
        value = dot_t(left, y_all[:, proj:], ((0,), (0,)))
        for n in range(2):
            acc[6 + n] = value[:, n * 128 : (n + 1) * 128]
        for dxx in (dx, dx + 2):
            start = pl.multiple_of(lax.rem(x_at + dxx, 4) // 2 * half, half)
            for n in range(8):
                block = acc[lax.rem(z_at + n, 8), pl.ds(start, half), :].astype(BF16)
                if n < 4:
                    first[dy][dxx, n] = block
                else:
                    second[dxx][dy, n - 4] = block


def sum_split_kernel(count, *refs):
    ins, outs = refs[:count], refs[count:]
    for k, out in enumerate(outs):
        total = ins[0][k].astype(F32)
        for ref in ins[1:]:
            total = total + ref[k].astype(F32)
        out[...] = total.astype(BF16)


def sum_split(arrays):
    lead, rest = arrays[0].shape[0], arrays[0].shape[1:]
    size = math.prod(arrays[0].shape)
    return call(
        functools.partial(sum_split_kernel, len(arrays)),
        [shape(rest)] * lead,
        arrays,
        flops=len(arrays) * size,
        nbytes=2 * size * (len(arrays) + 1),
    )


def sum_whole_kernel(*refs):
    total = refs[0][...].astype(F32)
    for ref in refs[1:-1]:
        total = total + ref[...].astype(F32)
    refs[-1][...] = total.astype(BF16)


def sum_whole(arrays):
    size = math.prod(arrays[0].shape)
    return call(
        sum_whole_kernel,
        shape(arrays[0].shape),
        arrays,
        flops=len(arrays) * size,
        nbytes=2 * size * (len(arrays) + 1),
    )


def token_grad_kernel(width, offs, tokens, y_own, *refs):
    own, other, (out, g) = refs[:16], refs[16:32], refs[32:]
    rows, model = tokens.shape
    cols = HEADS * HD
    gl = [y_own[:, m * cols : (m + 1) * cols] for m in range(3)]
    for side, shards in ((0, own), (1, other)):
        for j in range(8):
            total = None
            for m in range(3):
                term = dot_t(gl[m], shards[2 * j + m // 2][m % 2], ((1,), (1,)))
                total = term if total is None else total + term
            g[:, pl.ds(pl.multiple_of(offs[8 * side + j], 128), width)] = total
    step = 16

    def body(i, carry):
        at = pl.ds(pl.multiple_of(i * step, step), step)
        x = tokens[at, :].astype(F32)
        center = x - jnp.sum(x, axis=1, keepdims=True) / model
        scale = lax.rsqrt(jnp.sum(center * center, axis=1, keepdims=True) / model + EPS)
        hat = center * scale
        grad = g[at, :]
        mean_g = jnp.sum(grad, axis=1, keepdims=True) / model
        mean_gh = jnp.sum(grad * hat, axis=1, keepdims=True) / model
        out[at, :] = (scale * (grad - mean_g - hat * mean_gh)).astype(BF16)
        return carry

    lax.fori_loop(0, rows // step, body, 0)


def place_kernel(place, *refs):
    blocks, out = refs[:4], refs[4]
    half = blocks[0].shape[1]
    core, x_hi, z_at = place[0], place[1], place[2]
    for k, ref in enumerate(blocks):
        c = core if k < 2 else 1 - core
        h = x_hi if k % 2 == 0 else 1 - x_hi
        rows = pl.ds(pl.multiple_of((2 * c + h) * half, half), half)
        for d in range(8):
            n = lax.rem(z_at - d + 8, 8)
            cols = pl.ds(pl.multiple_of(lax.rem(n, 2) * 128, 128), 128)
            out[n // 2, rows, cols] = ref[d].astype(F32)


def per_device(tokens, cotangent, lengths, positions, weights):
    rows, model = tokens.shape
    shard_rows, cols = weights.shape[1], weights.shape[2]
    width = shard_rows // 2
    dp, fs = lax.axis_index("dp"), lax.axis_index("fsdp")
    core, z_at, x_hi = dp % 2, (dp // 2) % NZ, dp // 16
    y_at, x_lo = fs // 2, fs % 2
    x_at = x_hi * 2 + x_lo
    shard_of = [((y_at + dy) % NY) * 2 + (x_lo + dx) % 2 for dy, dx in REL]
    offs = jnp.stack(
        [s * shard_rows + core * width for s in shard_of]
        + [s * shard_rows + (1 - core) * width for s in shard_of]
    ).astype(jnp.int32)
    half = width // 2

    mine = lax.dynamic_slice(weights, (0, core * width, 0), (4, width, cols))
    halves = {(0, 0): (mine[:2], mine[2:])}
    a0, b0 = halves[(0, 0)]
    a3, b3 = shift(a0, dy=1), shift(b0, dy=1)
    a1, b1 = shift(a0, dy=-1), shift(b0, dy=-1)
    a2, b2 = shift(a3, dy=1), shift(b1, dy=-1)
    halves.update({(1, 0): (a1, b1), (2, 0): (a2, b2), (3, 0): (a3, b3)})
    for dy in range(NY):
        a, b = halves[(dy, 0)]
        halves[(dy, 1)] = (shift(a, dx=1), shift(b, dx=-1))
    shards = [part for rel in REL for part in halves[rel]]

    half_shape = shape((rows, model // 2))
    x_own, x_send, c_own, c_send = call(
        functools.partial(prep_kernel, width),
        [half_shape] * 4,
        [offs, tokens, cotangent],
        scalars=1,
        scratch=[pltpu.VMEM((rows, model), BF16)],
        flops=8 * rows * model,
        nbytes=8 * rows * model,
        name="prep",
    )
    x_peer, c_peer = shift(x_send, dc=1), shift(c_send, dc=1)

    quarter = HD // 4
    frequency = ROPE_BASE ** (-jnp.arange(quarter, dtype=F32) / quarter)
    angle_r = positions[0].astype(F32)[:, None] * frequency[None, :]
    angle_c = positions[1].astype(F32)[:, None] * frequency[None, :]
    cos_r, sin_r, cos_c, sin_c = jnp.cos(angle_r), jnp.sin(angle_r), jnp.cos(angle_c), jnp.sin(angle_c)
    cos_t = jnp.concatenate([cos_r, cos_r, cos_c, cos_c], axis=1)
    sin_t = jnp.concatenate([-sin_r, sin_r, -sin_c, sin_c], axis=1)
    l0, l1, l2 = lengths[0, 0], lengths[0, 1], lengths[0, 2]
    ends = jnp.stack([l0, l0 + l1, l0 + l1 + l2]).astype(jnp.int32)

    lin_shape = shape((rows, 4 * cols), F32)
    lin_own, lin_send = call(
        functools.partial(linear_kernel, width),
        [lin_shape] * 2,
        [x_own, x_peer, c_own, c_peer] + shards,
        flops=2 * 2 * rows * (model // 2) * 4 * cols,
        nbytes=4 * model * cols + 8 * rows * model,
        name="linear",
    )
    lin_peer = shift(lin_send, dc=1)
    y_own = call(
        attend_kernel,
        shape((rows, 4 * cols)),
        [ends, lin_own, lin_peer, cos_t, sin_t],
        scalars=1,
        flops=HEADS * 10 * rows * rows * HD * 2,
        nbytes=10 * rows * 4 * cols,
        name="attend",
    )
    y_peer = shift(y_own, dc=1)

    piece = shape((4, 4, half, 128))
    pieces = call(
        functools.partial(terms_kernel, width),
        [piece] * 8,
        [jnp.stack([x_at, z_at]).astype(jnp.int32), x_own, x_peer, c_own, c_peer, y_own, y_peer],
        scalars=1,
        scratch=[pltpu.VMEM((8, width, 128), F32)],
        flops=2 * 2 * rows * (model // 2) * 4 * cols,
        nbytes=4 * model * cols + 8 * rows * model,
        name="terms",
    )
    first, second = pieces[:4], pieces[4:]
    got_y = [shift(first[d], dy=d) for d in range(1, 4)]
    got_x = [shift(second[d], dx=d) for d in range(1, 4)]
    by_x = sum_split([first[0]] + got_y)
    by_y = sum_split([second[0]] + got_x)
    got_yx = [shift(by_x[d], dx=d) for d in range(1, 4)]
    got_xy = [shift(by_y[d], dy=d) for d in range(1, 4)]
    by_z = sum_split([by_x[0]] + got_yx) + sum_split([by_y[0]] + got_xy)
    got_z = [shift(by_z[d], dz=d) for d in range(1, NZ)]
    total = sum_whole([by_z[0]] + got_z)
    stack = jnp.stack([total] + [shift(total, dz=d) for d in range(1, NZ)])
    stack_x = shift(stack, dx=2)
    stack_c = shift(stack, dc=1)
    stack_cx = shift(stack_x, dc=1)
    weight_grads = call(
        place_kernel,
        shape((4, shard_rows, cols), F32),
        [jnp.stack([core, x_hi, z_at]).astype(jnp.int32), stack, stack_x, stack_c, stack_cx],
        scalars=1,
        flops=4 * shard_rows * cols,
        nbytes=24 * shard_rows * cols,
        name="place",
    )

    late = lax.optimization_barrier((tuple(shards), y_own))[0]
    others = [shift(part, dc=1) for part in late]
    grad_tokens = call(
        functools.partial(token_grad_kernel, width),
        shape((rows, model)),
        [offs, tokens, y_own] + shards + others,
        scalars=1,
        scratch=[pltpu.VMEM((rows, model), F32)],
        flops=2 * rows * model * 3 * cols,
        nbytes=8 * model * cols + 8 * rows * model,
        name="token_grad",
    )
    return (grad_tokens, weight_grads)


def solution(mesh):
    return jax.shard_map(
        per_device,
        mesh=mesh,
        in_specs=(
            P(("dp", "fsdp"), None),
            P(("dp", "fsdp"), None),
            P(("dp", "fsdp"), None),
            P(None, ("dp", "fsdp")),
            P(None, "fsdp", None),
        ),
        out_specs=(P(("dp", "fsdp"), None), P(None, "fsdp", None)),
        check_vma=False,
    )
```

```python
import functools
import math

import jax
import jax.numpy as jnp
from jax import lax
from jax.experimental import pallas as pl
from jax.experimental.pallas import tpu as pltpu
from jax.sharding import PartitionSpec as P

HD = 128
HEADS = 2
ROPE_BASE = 100.0
EPS = 1e-6
NX, NY, NZ = 4, 4, 8
ORDER = [(0, 0), (0, 1), (1, 0), (1, 1), (3, 0), (2, 0), (3, 1), (2, 1)]
X_AT, X_LO, CORE, SIGN = 16, 17, 18, 19
BF16, F32 = jnp.bfloat16, jnp.float32


def flat_index(x, y, z, core):
    return ((x // 2) * 16 + z * 2 + core) * 8 + y * 2 + x % 2


DEVICES = [(x, y, z, core) for x in range(NX) for y in range(NY) for z in range(NZ) for core in range(2)]


def permute(values, target):
    pairs = []
    for x, y, z, core in DEVICES:
        tx, ty, tz, tcore = target(x, y, z, core)
        pairs.append((flat_index(x, y, z, core), flat_index(tx % NX, ty % NY, tz % NZ, tcore)))
    return lax.ppermute(values, ("dp", "fsdp"), pairs)


def shift(values, dx=0, dy=0, dc=0):
    def target(x, y, z, core):
        s = 1 - 2 * core
        return x + s * dx, y + s * dy, z, core ^ dc

    return permute(values, target)


def along(values, first=0, second=0):
    def target(x, y, z, core):
        dx, dy = (second, first) if core == 0 else (first, second)
        return x + dx, y + dy, z, core

    return permute(values, target)


def call(body, out_shapes, operands, scalars=0, scratch=(), flops=0, nbytes=0, name=None, after=()):
    count, last = len(operands), len(operands) + len(after)
    specs = [pl.BlockSpec(memory_space=pltpu.SMEM if i < scalars else pltpu.VMEM) for i in range(count)]
    specs += [pl.BlockSpec(memory_space=pl.ANY) for _ in after]
    kernel = (lambda *refs: body(*refs[:count], *refs[last:])) if after else body
    return pl.pallas_call(
        kernel,
        out_shape=out_shapes,
        in_specs=specs,
        out_specs=jax.tree.map(lambda _: pl.BlockSpec(memory_space=pltpu.VMEM), out_shapes),
        scratch_shapes=list(scratch),
        compiler_params=pltpu.CompilerParams(vmem_limit_bytes=56 * 1024 * 1024),
        cost_estimate=pl.CostEstimate(flops=flops, bytes_accessed=nbytes, transcendentals=0),
        name=name,
    )(*operands, *after)


def gate(value, after):
    return pl.pallas_call(
        lambda *refs: None,
        out_shape=shape(value.shape, value.dtype),
        in_specs=[pl.BlockSpec(memory_space=pl.ANY)] * (1 + len(after)),
        out_specs=pl.BlockSpec(memory_space=pl.ANY),
        input_output_aliases={0: 0},
        cost_estimate=pl.CostEstimate(flops=1, bytes_accessed=1, transcendentals=0),
        name="gate",
    )(value, *after)


def shape(dims, dtype=BF16):
    return jax.ShapeDtypeStruct(dims, dtype)


def prep_kernel(width, info, tokens, cot, own, send, normed):
    rows, model = tokens.shape
    step = 16

    def body(i, carry):
        at = pl.ds(pl.multiple_of(i * step, step), step)
        x = tokens[at, :].astype(F32)
        center = x - jnp.sum(x, axis=1, keepdims=True) / model
        var = jnp.sum(center * center, axis=1, keepdims=True) / model
        normed[at, :] = (center * lax.rsqrt(var + EPS)).astype(BF16)
        return carry

    lax.fori_loop(0, rows // step, body, 0)
    for j in range(8):
        to = slice(j * width, (j + 1) * width)
        for out, first in ((own, 0), (send, 8)):
            cols = pl.ds(pl.multiple_of(info[first + j], 128), width)
            out[0, :, to] = normed[:, cols]
            out[1, :, to] = cot[:, cols]


def flip_kernel(width, info, own, peer, out):
    half = width // 2
    quarter = half // 2
    core, sign, x_at = info[CORE], info[SIGN], info[X_AT]
    for j, (k, dx) in enumerate(ORDER):
        at = slice(j * width, (j + 1) * width)
        y_steps = lax.rem(4 - sign * k, 4)
        for i in range(2):
            turned = jnp.concatenate([own[i, :, at], peer[i, :, at]], axis=0).T
            for x_hi in range(2):
                x_to = 2 * x_hi + lax.rem(info[X_LO] + dx, 2)
                x_steps = lax.rem(x_to - x_at + 4, 4)
                first = jnp.where(core == 0, y_steps, x_steps)
                second = jnp.where(core == 0, x_steps, y_steps)
                for side in range(2):
                    steps = first if side == 0 else lax.rem(4 - first, 4)
                    start = x_hi * half + side * quarter
                    out[side, steps, i, second] = turned[start : start + quarter]


def linear_kernel(width, first, pairs, own, peer, *refs):
    shards, rest = refs[: 2 * pairs], refs[2 * pairs :]
    before, outs = rest[:-2], rest[-2:]
    cols = shards[0].shape[2]
    for m in range(4):
        to = slice(m * cols, (m + 1) * cols)
        rights = [jnp.concatenate([shards[2 * p][m], shards[2 * p + 1][m]], axis=0) for p in range(pairs)]
        for side, left in enumerate((own, peer)):
            total = before[side][:, to] if before else None
            for p, right in enumerate(rights):
                at = slice(2 * (first + p) * width, 2 * (first + p + 1) * width)
                term = jnp.dot(left[m // 3, :, at], right, preferred_element_type=F32)
                total = term if total is None else total + term
            outs[side][:, to] = total


def swap_quarters(x):
    lane = lax.broadcasted_iota(jnp.int32, x.shape, 1)
    quarter = HD // 4
    up = pltpu.roll(x, HD - quarter, 1)
    down = pltpu.roll(x, quarter, 1)
    return jnp.where(lane % (2 * quarter) < quarter, up, down)


def mean_of(x):
    return jnp.sum(x, axis=1, keepdims=True) * (1.0 / HD)


def norm_rows(x):
    center = x - mean_of(x)
    scale = lax.rsqrt(mean_of(center * center) + EPS)
    return center * scale, scale


def norm_rows_back(g, hat, scale):
    return scale * (g - mean_of(g) - hat * mean_of(g * hat))


def dot_t(a, b, dims):
    return lax.dot_general(a, b, ((dims[0], dims[1]), ((), ())), preferred_element_type=F32)


def attend_kernel(ends, mine, theirs, cos_t, sin_t, out):
    rows = mine.shape[0]
    cols = HEADS * HD
    row_id = lax.broadcasted_iota(jnp.int32, (rows, 1), 0)
    col_id = lax.broadcasted_iota(jnp.int32, (1, rows), 1)

    def slot(ids):
        count = jnp.zeros(ids.shape, jnp.int32)
        for k in range(3):
            count = count + (ids >= ends[k]).astype(jnp.int32)
        return count

    row_slot, col_slot = slot(row_id), slot(col_id)
    same = row_slot == col_slot
    live = row_slot < 3
    cosine, sine = cos_t[...], sin_t[...]
    score_scale = 1.0 / math.sqrt(HD)
    for h in range(HEADS):

        def part(m):
            at = slice(m * cols + h * HD, m * cols + (h + 1) * HD)
            return mine[:, at] + theirs[:, at]

        q_hat, q_scale = norm_rows(part(0))
        k_hat, k_scale = norm_rows(part(1))
        q = (q_hat * cosine + swap_quarters(q_hat) * sine).astype(BF16)
        k = (k_hat * cosine + swap_quarters(k_hat) * sine).astype(BF16)
        v = part(2).astype(BF16)
        ga = jnp.where(live, part(3), 0.0).astype(BF16)
        scores = dot_t(q, k, ((1,), (1,))) * score_scale
        e = jnp.where(same, jnp.exp(scores), 0.0)
        p32 = e / jnp.sum(e, axis=1, keepdims=True)
        p = p32.astype(BF16)
        att = jnp.dot(p, v, preferred_element_type=F32).astype(BF16)
        gv = dot_t(p, ga, ((0,), (0,)))
        gp = dot_t(ga, v, ((1,), (1,))).astype(BF16).astype(F32)
        gs = p32 * (gp - jnp.sum(gp * p32, axis=1, keepdims=True)) * score_scale
        gs = gs.astype(BF16)
        gq = jnp.dot(gs, k, preferred_element_type=F32).astype(BF16).astype(F32)
        gk = dot_t(gs, q, ((0,), (0,))).astype(BF16).astype(F32)
        gq = norm_rows_back(gq * cosine + swap_quarters(gq * sine), q_hat, q_scale)
        gk = norm_rows_back(gk * cosine + swap_quarters(gk * sine), k_hat, k_scale)
        at = lambda m: slice(m * cols + h * HD, m * cols + (h + 1) * HD)
        out[:, at(0)] = gq.astype(BF16)
        out[:, at(1)] = gk.astype(BF16)
        out[:, at(2)] = gv.astype(BF16)
        out[:, at(3)] = jnp.where(live, att.astype(F32), 0.0).astype(BF16)


def terms_kernel(steps, turned, y_own, y_peer, *outs):
    rows, depth = turned.shape[4:]
    y_all = jnp.concatenate([y_own[...], y_peer[...]], axis=0)
    proj = 3 * HEADS * HD
    for k, step in enumerate(steps):
        for side in range(2):
            for i, right in ((0, y_all[:, :proj]), (1, y_all[:, proj:])):
                left = turned[side, step, i].reshape(4 * rows, depth)
                value = jnp.dot(left, right, preferred_element_type=F32).astype(BF16)
                for n in range(right.shape[1] // 128):
                    for u in range(4):
                        block = value[u * rows : (u + 1) * rows, n * 128 : (n + 1) * 128]
                        outs[2 * k + side][u, 6 * i + n] = block


def add_up(refs, at):
    total = refs[0][at].astype(F32)
    for ref in refs[1:]:
        total = total + ref[at].astype(F32)
    return total.astype(BF16)


def join_kernel(*refs):
    for u in range(refs[0].shape[0]):
        for n in range(refs[0].shape[1]):
            refs[-1][u, n] = add_up(refs[:-1], (u, n))


def sides_kernel(*refs):
    for side in range(2):
        for u, out in enumerate(refs[6:]):
            for n in range(8):
                out[n, side] = add_up(refs[3 * side : 3 * side + 3], (u, n))


def seconds_kernel(*refs):
    for n in range(8):
        for side in range(2):
            refs[-1][n, side] = add_up(refs[:-1], (n, side))


def last_kernel(got, out):
    for side in range(2):
        total = got[0, side].astype(F32)
        for k in range(1, 8):
            total = total + got[k, side].astype(F32)
        for k in range(out.shape[0]):
            out[k, side] = total.astype(BF16)


def sum_call(body, name, outs, arrays, after=()):
    size = math.prod(arrays[0].shape)
    return call(
        body, outs, arrays, flops=len(arrays) * size, nbytes=2 * size * (len(arrays) + 2), name=name, after=after
    )


def normed_grad_kernel(width, y_own, y_peer, *refs):
    shards, (g_own, g_send) = refs[:-2], refs[-2:]
    rows = y_own.shape[0]
    proj = 3 * HEADS * HD
    left = jnp.concatenate([y_own[:, :proj], y_peer[:, :proj]], axis=0)
    for j in range(8):
        right = jnp.concatenate([shards[j][m] for m in range(3)], axis=1)
        total = dot_t(left, right, ((1,), (1,)))
        at = slice(j * width, (j + 1) * width)
        g_own[:, at] = total[:rows]
        g_send[:, at] = total[rows:]


def token_grad_kernel(width, info, tokens, g_own, g_peer, out, g):
    rows, model = tokens.shape
    for first, ref in ((0, g_own), (8, g_peer)):
        for j in range(8):
            to = pl.ds(pl.multiple_of(info[first + j], 128), width)
            g[:, to] = ref[:, j * width : (j + 1) * width]
    step = 16

    def body(i, carry):
        at = pl.ds(pl.multiple_of(i * step, step), step)
        x = tokens[at, :].astype(F32)
        center = x - jnp.sum(x, axis=1, keepdims=True) / model
        scale = lax.rsqrt(jnp.sum(center * center, axis=1, keepdims=True) / model + EPS)
        hat = center * scale
        grad = g[at, :]
        mean_g = jnp.sum(grad, axis=1, keepdims=True) / model
        mean_gh = jnp.sum(grad * hat, axis=1, keepdims=True) / model
        out[at, :] = (scale * (grad - mean_g - hat * mean_gh)).astype(BF16)
        return carry

    lax.fori_loop(0, rows // step, body, 0)


def place_kernel(info, own, other, out):
    rows = own.shape[3]
    for k, ref in enumerate((own, other)):
        c = info[CORE] if k == 0 else 1 - info[CORE]
        for h in range(2):
            for n in range(8):
                for side in range(2):
                    to = pl.ds(pl.multiple_of(c * 4 * rows + (2 * h + side) * rows, rows), rows)
                    out[n // 2, to, (n % 2) * 128 : (n % 2 + 1) * 128] = ref[h, n, side].astype(F32)


def swap_groups(with_x):
    if with_x:
        return [[x * 16 + z * 2 + core for x in range(2) for z in range(NZ)] for core in range(2)]
    return [[x * 16 + z * 2 + core for z in range(NZ)] for x in range(2) for core in range(2)]


def exchange(values, with_x):
    return lax.all_to_all(
        values, "dp", split_axis=0, concat_axis=0, axis_index_groups=swap_groups(with_x), tiled=True
    )


def per_device(tokens, cotangent, lengths, positions, weights):
    rows, model = tokens.shape
    shard_rows, cols = weights.shape[1], weights.shape[2]
    width = shard_rows // 2
    dp, fs = lax.axis_index("dp"), lax.axis_index("fsdp")
    core, x_hi = dp % 2, dp // 16
    y_at, x_lo = fs // 2, fs % 2
    sign = 1 - 2 * core
    offs = []
    for c, s in ((core, sign), (1 - core, -sign)):
        for k, dx in ORDER:
            shard = ((y_at - s * k + 4) % NY) * 2 + (x_lo + dx) % 2
            offs.append(shard * shard_rows + c * width)
    l0, l1, l2 = lengths[0, 0], lengths[0, 1], lengths[0, 2]
    ends = jnp.stack([l0, l0 + l1, l0 + l1 + l2]).astype(jnp.int32)
    info = jnp.stack(offs + [x_hi * 2 + x_lo, x_lo, core, sign]).astype(jnp.int32)
    half = width // 2

    pair_shape = shape((2, rows, model // 2))
    own, send = call(
        functools.partial(prep_kernel, width),
        [pair_shape] * 2,
        [info, tokens, cotangent],
        scalars=1,
        scratch=[pltpu.VMEM((rows, model), BF16)],
        flops=8 * rows * model,
        nbytes=8 * rows * model,
        name="prep",
    )
    w = {(0, 0): lax.dynamic_slice(weights, (0, core * width, 0), (4, width, cols))}
    w[0, 1] = shift(w[0, 0], dx=1)
    w[3, 0] = shift(w[0, 0], dy=-1)
    w[1, 0] = gate(shift(w[0, 0], dy=1), [own, w[0, 1]])
    w[2, 0] = shift(w[1, 0], dy=1)
    w[1, 1] = shift(w[1, 0], dx=1)
    w[3, 1] = shift(w[3, 0], dx=1)
    w[2, 1] = shift(w[1, 1], dy=1)
    shards = [w[place] for place in ORDER]

    peer = shift(gate(send, [w[1, 0], w[3, 0]]), dc=1)
    turned = call(
        functools.partial(flip_kernel, width),
        shape((2, 4, 2, 4, half // 2, 2 * rows)),
        [info, own, peer],
        scalars=1,
        nbytes=8 * rows * model,
        name="flip",
    )

    quarter = HD // 4
    frequency = ROPE_BASE ** (-jnp.arange(quarter, dtype=F32) / quarter)
    angle_r = positions[0].astype(F32)[:, None] * frequency[None, :]
    angle_c = positions[1].astype(F32)[:, None] * frequency[None, :]
    cos_r, sin_r, cos_c, sin_c = jnp.cos(angle_r), jnp.sin(angle_r), jnp.cos(angle_c), jnp.sin(angle_c)
    cos_t = jnp.concatenate([cos_r, cos_r, cos_c, cos_c], axis=1)
    sin_t = jnp.concatenate([-sin_r, sin_r, -sin_c, sin_c], axis=1)

    lin_shape = shape((rows, 4 * cols), F32)
    lin = []
    for first, pairs in ((0, 3), (3, 1)):
        lin = call(
            functools.partial(linear_kernel, width, first, pairs),
            [lin_shape] * 2,
            [own, peer] + shards[2 * first : 2 * (first + pairs)] + list(lin),
            flops=2 * 2 * rows * 2 * pairs * width * 4 * cols,
            nbytes=2 * pairs * width * 8 * cols + 8 * rows * 2 * pairs * width,
            name="linear",
            after=[] if first else [turned, cos_t, sin_t, ends],
        )
    lin_own, lin_send = lin
    lin_peer = shift(lin_send, dc=1)
    y_own = call(
        attend_kernel,
        shape((rows, 4 * cols)),
        [ends, lin_own, lin_peer, cos_t, sin_t],
        scalars=1,
        flops=HEADS * 10 * rows * rows * HD * 2,
        nbytes=10 * rows * 4 * cols,
        name="attend",
    )
    y_peer = shift(y_own, dc=1)

    quarter = half // 2
    piece = shape((4, 8, quarter, 128))

    def terms(steps):
        part = len(steps) / 4
        return call(
            functools.partial(terms_kernel, steps),
            [piece] * (2 * len(steps)),
            [turned, y_own, y_peer],
            flops=int(part * 2 * 2 * rows * (model // 2) * 4 * cols),
            nbytes=int(part * (4 * model * cols + 8 * rows * model)),
            name="terms",
        )

    far = terms([2])
    far = [along(far[0], first=1), along(far[1], first=-1)]
    back = terms([3])
    back = [along(back[0], first=-1), along(back[1], first=1)]
    near = terms([1, 0])

    g_own, g_send = call(
        functools.partial(normed_grad_kernel, width),
        [shape((rows, model // 2), F32)] * 2,
        [y_own, y_peer] + shards,
        flops=2 * rows * model * 3 * cols,
        nbytes=4 * model * cols + 4 * rows * model,
        name="normed_grad",
        after=[near[0]],
    )
    ahead = []
    for side in range(2):
        joined = sum_call(join_kernel, "join", piece, [near[side], far[side]], after=[g_send])
        ahead.append(along(joined, first=1 - 2 * side))
    halfway = sum_call(
        sides_kernel,
        "sides",
        [shape((8, 2, quarter, 128))] * 4,
        [near[2], back[0], ahead[0], near[3], back[1], ahead[1]],
    )
    g_peer = shift(gate(g_send, [halfway[0]]), dc=1)
    grad_tokens = call(
        functools.partial(token_grad_kernel, width),
        shape((rows, model)),
        [info, tokens, g_own, g_peer],
        scalars=1,
        scratch=[pltpu.VMEM((rows, model), F32)],
        flops=16 * rows * model,
        nbytes=8 * rows * model,
        name="token_grad",
    )

    rest = [along(halfway[d], second=d) for d in range(1, 4)]
    by_z = sum_call(seconds_kernel, "seconds", shape((8, 2, quarter, 128)), [halfway[0]] + rest, after=[grad_tokens])
    spread = sum_call(last_kernel, "last", shape((2 * NZ, 2, quarter, 128)), [exchange(by_z, False)])
    done = exchange(spread, True).reshape(2, NZ, 2, quarter, 128)
    weight_grads = call(
        place_kernel,
        shape((4, shard_rows, cols), F32),
        [info, done, shift(done, dc=1)],
        scalars=1,
        flops=4 * shard_rows * cols,
        nbytes=24 * shard_rows * cols,
        name="place",
    )
    return (grad_tokens, weight_grads)


def solution(mesh):
    return jax.shard_map(
        per_device,
        mesh=mesh,
        in_specs=(
            P(("dp", "fsdp"), None),
            P(("dp", "fsdp"), None),
            P(("dp", "fsdp"), None),
            P(None, ("dp", "fsdp")),
            P(None, "fsdp", None),
        ),
        out_specs=(P(("dp", "fsdp"), None), P(None, "fsdp", None)),
        check_vma=False,
    )
```

```python
import functools
import math

import jax
import jax.numpy as jnp
from jax import lax
from jax.experimental import pallas as pl
from jax.experimental.pallas import tpu as pltpu
from jax.sharding import PartitionSpec as P

HD = 128
HEADS = 2
ROPE_BASE = 100.0
EPS = 1e-6
NX, NY, NZ = 4, 4, 8
ORDER = [(0, 0), (0, 1), (1, 0), (1, 1), (3, 0), (2, 0), (3, 1), (2, 1)]
X_AT, X_LO, CORE, SIGN = 16, 17, 18, 19
BF16, F32 = jnp.bfloat16, jnp.float32


def flat_index(x, y, z, core):
    return ((x // 2) * 16 + z * 2 + core) * 8 + y * 2 + x % 2


DEVICES = [(x, y, z, core) for x in range(NX) for y in range(NY) for z in range(NZ) for core in range(2)]


def permute(values, target):
    pairs = []
    for x, y, z, core in DEVICES:
        tx, ty, tz, tcore = target(x, y, z, core)
        pairs.append((flat_index(x, y, z, core), flat_index(tx % NX, ty % NY, tz % NZ, tcore)))
    return lax.ppermute(values, ("dp", "fsdp"), pairs)


def shift(values, dx=0, dy=0, dc=0):
    def target(x, y, z, core):
        s = 1 - 2 * core
        return x + s * dx, y + s * dy, z, core ^ dc

    return permute(values, target)


def along(values, first=0, second=0):
    def target(x, y, z, core):
        dx, dy = (second, first) if core == 0 else (first, second)
        return x + dx, y + dy, z, core

    return permute(values, target)


def call(body, outs, operands, grid=(), scalars=0, scratch=(), flops=0, nbytes=0, name=None, after=()):
    count, last = len(operands), len(operands) + len(after)
    held = 0
    arrays, in_specs, out_shapes, out_specs = [], [], [], []
    for k, item in enumerate(list(operands) + list(outs)):
        value, *place = item if isinstance(item, tuple) else (item,)
        if k < scalars:
            spec = pl.BlockSpec(memory_space=pltpu.SMEM)
        elif place:
            spec = pl.BlockSpec(place[0], place[1])
            held += 2 * math.prod(place[0]) * value.dtype.itemsize
        else:
            spec = pl.BlockSpec(memory_space=pltpu.VMEM)
            held += math.prod(value.shape) * value.dtype.itemsize
        (arrays if k < count else out_shapes).append(value)
        (in_specs if k < count else out_specs).append(spec)
    held += sum(math.prod(ref.shape) * ref.dtype.itemsize for ref in scratch)
    in_specs += [pl.BlockSpec(memory_space=pl.ANY) for _ in after]
    kernel = (lambda *refs: body(*refs[:count], *refs[last:])) if after else body
    return pl.pallas_call(
        kernel,
        grid=grid or (1,),
        out_shape=out_shapes,
        in_specs=in_specs,
        out_specs=out_specs,
        scratch_shapes=list(scratch),
        compiler_params=pltpu.CompilerParams(vmem_limit_bytes=held + 8 * 1024 * 1024),
        cost_estimate=pl.CostEstimate(flops=flops, bytes_accessed=nbytes, transcendentals=0),
        name=name,
    )(*arrays, *after)


def gate(value, after):
    return pl.pallas_call(
        lambda *refs: None,
        out_shape=shape(value.shape, value.dtype),
        in_specs=[pl.BlockSpec(memory_space=pl.ANY)] * (1 + len(after)),
        out_specs=pl.BlockSpec(memory_space=pl.ANY),
        input_output_aliases={0: 0},
        cost_estimate=pl.CostEstimate(flops=1, bytes_accessed=1, transcendentals=0),
        name="gate",
    )(value, *after)


def shape(dims, dtype=BF16):
    return jax.ShapeDtypeStruct(dims, dtype)


def prep_kernel(width, info, tokens, cot, own, send, normed):
    rows, model = tokens.shape
    step = 16
    for i in range(rows // step):
        at = slice(i * step, (i + 1) * step)
        x = tokens[at, :].astype(F32)
        center = x - jnp.sum(x, axis=1, keepdims=True) / model
        var = jnp.sum(center * center, axis=1, keepdims=True) / model
        normed[at, :] = (center * lax.rsqrt(var + EPS)).astype(BF16)
    for j in range(8):
        to = slice(j * width, (j + 1) * width)
        for out, first in ((own, 0), (send, 8)):
            cols = pl.ds(pl.multiple_of(info[first + j], 128), width)
            out[0, :, to] = normed[:, cols]
            out[1, :, to] = cot[:, cols]


def flip_kernel(width, info, own, peer, out):
    half = width // 2
    quarter = half // 2
    core, sign, x_at = info[CORE], info[SIGN], info[X_AT]
    for j, (k, dx) in enumerate(ORDER):
        at = slice(j * width, (j + 1) * width)
        y_steps = lax.rem(4 - sign * k, 4)
        turned = jnp.concatenate([own[0, :, at], peer[0, :, at]], axis=0).T
        for x_hi in range(2):
            x_to = 2 * x_hi + lax.rem(info[X_LO] + dx, 2)
            x_steps = lax.rem(x_to - x_at + 4, 4)
            first = jnp.where(core == 0, y_steps, x_steps)
            second = jnp.where(core == 0, x_steps, y_steps)
            for side in range(2):
                steps = first if side == 0 else lax.rem(4 - first, 4)
                start = x_hi * half + side * quarter
                out[side, steps, 0, second] = turned[start : start + quarter]


def linear_kernel(pairs, own, peer, *refs):
    shards, rest = refs[: 2 * pairs], refs[2 * pairs :]
    before, outs = rest[:-2], rest[-2:]
    depth = own.shape[2] // pairs
    rights = [jnp.concatenate([shards[2 * p][0], shards[2 * p + 1][0]], axis=0) for p in range(pairs)]
    for side, left in enumerate((own, peer)):
        total = before[side][...] if before else None
        for p, right in enumerate(rights):
            term = jnp.dot(left[0, :, p * depth : (p + 1) * depth], right, preferred_element_type=F32)
            total = term if total is None else total + term
        outs[side][...] = total


def swap_quarters(x):
    lane = lax.broadcasted_iota(jnp.int32, x.shape, 1)
    quarter = HD // 4
    up = pltpu.roll(x, HD - quarter, 1)
    down = pltpu.roll(x, quarter, 1)
    return jnp.where(lane % (2 * quarter) < quarter, up, down)


def mean_of(x):
    return jnp.sum(x, axis=1, keepdims=True) * (1.0 / HD)


def norm_rows(x):
    center = x - mean_of(x)
    scale = lax.rsqrt(mean_of(center * center) + EPS)
    return center * scale, scale


def norm_rows_back(g, hat, scale):
    return scale * (g - mean_of(g) - hat * mean_of(g * hat))


def dot_t(a, b, dims):
    return lax.dot_general(a, b, ((dims[0], dims[1]), ((), ())), preferred_element_type=F32)


def attend_kernel(ends, mine, theirs, cos_t, sin_t, out):
    rows = mine.shape[0]
    cols = HEADS * HD
    row_id = lax.broadcasted_iota(jnp.int32, (rows, 1), 0)
    col_id = lax.broadcasted_iota(jnp.int32, (1, rows), 1)

    def slot(ids):
        count = jnp.zeros(ids.shape, jnp.int32)
        for k in range(3):
            count = count + (ids >= ends[k]).astype(jnp.int32)
        return count

    row_slot, col_slot = slot(row_id), slot(col_id)
    same = row_slot == col_slot
    live = row_slot < 3
    cosine, sine = cos_t[...], sin_t[...]
    score_scale = 1.0 / math.sqrt(HD)
    for h in range(HEADS):

        def part(m):
            at = slice(m * cols + h * HD, m * cols + (h + 1) * HD)
            return mine[:, at] + theirs[:, at]

        q_hat, q_scale = norm_rows(part(0))
        k_hat, k_scale = norm_rows(part(1))
        q = (q_hat * cosine + swap_quarters(q_hat) * sine).astype(BF16)
        k = (k_hat * cosine + swap_quarters(k_hat) * sine).astype(BF16)
        v = part(2).astype(BF16)
        ga = jnp.where(live, part(3), 0.0).astype(BF16)
        scores = dot_t(q, k, ((1,), (1,))) * score_scale
        e = jnp.where(same, jnp.exp(scores), 0.0)
        p32 = e / jnp.sum(e, axis=1, keepdims=True)
        p = p32.astype(BF16)
        att = jnp.dot(p, v, preferred_element_type=F32).astype(BF16)
        gv = dot_t(p, ga, ((0,), (0,)))
        gp = dot_t(ga, v, ((1,), (1,))).astype(BF16).astype(F32)
        gs = p32 * (gp - jnp.sum(gp * p32, axis=1, keepdims=True)) * score_scale
        gs = gs.astype(BF16)
        gq = jnp.dot(gs, k, preferred_element_type=F32).astype(BF16).astype(F32)
        gk = dot_t(gs, q, ((0,), (0,))).astype(BF16).astype(F32)
        gq = norm_rows_back(gq * cosine + swap_quarters(gq * sine), q_hat, q_scale)
        gk = norm_rows_back(gk * cosine + swap_quarters(gk * sine), k_hat, k_scale)
        at = lambda m: slice(m * cols + h * HD, m * cols + (h + 1) * HD)
        out[:, at(0)] = gq.astype(BF16)
        out[:, at(1)] = gk.astype(BF16)
        out[:, at(2)] = gv.astype(BF16)
        out[:, at(3)] = jnp.where(live, att.astype(F32), 0.0).astype(BF16)


def terms_kernel(count, *refs):
    turned, (y_own, y_peer), outs = refs[:count], refs[count : count + 2], refs[count + 2 :]
    rows, depth = turned[0].shape[4:]
    y_all = jnp.concatenate([y_own[...], y_peer[...]], axis=0)
    proj = 3 * HEADS * HD
    for k, ref in enumerate(turned):
        for side in range(2):
            for i, right in ((0, y_all[:, :proj]), (1, y_all[:, proj:])):
                left = ref[side, 0, i].reshape(4 * rows, depth)
                value = jnp.dot(left, right, preferred_element_type=F32).astype(BF16)
                for n in range(right.shape[1] // 128):
                    for u in range(4):
                        block = value[u * rows : (u + 1) * rows, n * 128 : (n + 1) * 128]
                        outs[2 * k + side][u, 6 * i + n] = block


def add_up(refs, at):
    total = refs[0][at].astype(F32)
    for ref in refs[1:]:
        total = total + ref[at].astype(F32)
    return total.astype(BF16)


def join_kernel(near_0, far_0, near_1, far_1, out_0, out_1):
    for n in range(8):
        out_0[0, n] = add_up((near_0, far_0), (0, n))
        out_1[0, n] = add_up((near_1, far_1), (0, n))


def sides_kernel(*refs):
    for side in range(2):
        for u, out in enumerate(refs[6:]):
            for n in range(out.shape[0]):
                out[n, side] = add_up(refs[3 * side : 3 * side + 3], (u, n))


def seconds_kernel(*refs):
    for n in range(refs[0].shape[0]):
        for side in range(2):
            refs[-1][n, side] = add_up(refs[:-1], (n, side))


def last_kernel(got, out):
    for side in range(2):
        total = got[0, side].astype(F32)
        for k in range(1, 8):
            total = total + got[k, side].astype(F32)
        for k in range(out.shape[0]):
            out[k, side] = total.astype(BF16)


def sum_call(body, name, outs, operands, grid=(), after=()):
    value = operands[0][0] if isinstance(operands[0], tuple) else operands[0]
    size = math.prod(value.shape)
    return call(
        body,
        outs,
        operands,
        grid=grid,
        flops=len(operands) * size,
        nbytes=2 * size * (len(operands) + 2),
        name=name,
        after=after,
    )


def normed_grad_kernel(width, y_own, y_peer, *refs):
    shards, (g_own, g_send) = refs[:-2], refs[-2:]
    rows = y_own.shape[0]
    proj = 3 * HEADS * HD
    left = jnp.concatenate([y_own[:, :proj], y_peer[:, :proj]], axis=0)
    for j in range(8):
        right = jnp.concatenate([shards[j][m] for m in range(3)], axis=1)
        total = dot_t(left, right, ((1,), (1,)))
        at = slice(j * width, (j + 1) * width)
        g_own[:, at] = total[:rows]
        g_send[:, at] = total[rows:]


def token_grad_kernel(width, info, tokens, g_own, g_peer, out, g):
    rows, model = tokens.shape
    for first, ref in ((0, g_own), (8, g_peer)):
        for j in range(8):
            to = pl.ds(pl.multiple_of(info[first + j], 128), width)
            g[:, to] = ref[:, j * width : (j + 1) * width]
    step = 16
    for i in range(rows // step):
        at = slice(i * step, (i + 1) * step)
        x = tokens[at, :].astype(F32)
        center = x - jnp.sum(x, axis=1, keepdims=True) / model
        scale = lax.rsqrt(jnp.sum(center * center, axis=1, keepdims=True) / model + EPS)
        hat = center * scale
        grad = g[at, :]
        mean_g = jnp.sum(grad, axis=1, keepdims=True) / model
        mean_gh = jnp.sum(grad * hat, axis=1, keepdims=True) / model
        out[at, :] = (scale * (grad - mean_g - hat * mean_gh)).astype(BF16)


def place_kernel(info, own, other, out):
    rows = own.shape[3]
    for k, ref in enumerate((own, other)):
        c = info[CORE] if k == 0 else 1 - info[CORE]
        for h in range(2):
            for n in range(2):
                for side in range(2):
                    to = pl.ds(pl.multiple_of(c * 4 * rows + (2 * h + side) * rows, rows), rows)
                    out[0, to, n * 128 : (n + 1) * 128] = ref[h, n, side].astype(F32)


def swap_groups(with_x):
    if with_x:
        return [[x * 16 + z * 2 + core for x in range(2) for z in range(NZ)] for core in range(2)]
    return [[x * 16 + z * 2 + core for z in range(NZ)] for x in range(2) for core in range(2)]


def exchange(values, with_x):
    return lax.all_to_all(
        values, "dp", split_axis=0, concat_axis=0, axis_index_groups=swap_groups(with_x), tiled=True
    )


def per_device(tokens, cotangent, lengths, positions, weights):
    rows, model = tokens.shape
    shard_rows, cols = weights.shape[1], weights.shape[2]
    width = shard_rows // 2
    dp, fs = lax.axis_index("dp"), lax.axis_index("fsdp")
    core, x_hi = dp % 2, dp // 16
    y_at, x_lo = fs // 2, fs % 2
    sign = 1 - 2 * core
    offs = []
    for c, s in ((core, sign), (1 - core, -sign)):
        for k, dx in ORDER:
            shard = ((y_at - s * k + 4) % NY) * 2 + (x_lo + dx) % 2
            offs.append(shard * shard_rows + c * width)
    l0, l1, l2 = lengths[0, 0], lengths[0, 1], lengths[0, 2]
    ends = jnp.stack([l0, l0 + l1, l0 + l1 + l2]).astype(jnp.int32)
    info = jnp.stack(offs + [x_hi * 2 + x_lo, x_lo, core, sign]).astype(jnp.int32)
    half = width // 2

    pair = shape((2, rows, model // 2))
    some = rows // 4
    own, send = call(
        functools.partial(prep_kernel, width),
        [(pair, (2, some, model // 2), lambda i: (0, i, 0))] * 2,
        [info, (tokens, (some, model), lambda i: (i, 0)), (cotangent, (some, model), lambda i: (i, 0))],
        grid=(4,),
        scalars=1,
        scratch=[pltpu.VMEM((some, model), BF16)],
        flops=8 * rows * model,
        nbytes=8 * rows * model,
        name="prep",
    )

    w = {(0, 0): lax.dynamic_slice(weights, (0, core * width, 0), (4, width, cols))}
    w[0, 1] = shift(w[0, 0], dx=1)
    w[3, 0] = shift(w[0, 0], dy=-1)
    w[1, 0] = gate(shift(w[0, 0], dy=1), [own, w[0, 1]])
    w[2, 0] = shift(w[1, 0], dy=1)
    w[1, 1] = shift(w[1, 0], dx=1)
    w[3, 1] = shift(w[3, 0], dx=1)
    w[2, 1] = shift(w[1, 1], dy=1)
    shards = [w[place] for place in ORDER]

    peer = shift(gate(send, [w[1, 0]]), dc=1)
    one = (1, rows, model // 2)
    (turned,) = call(
        functools.partial(flip_kernel, width),
        [(shape((2, 4, 2, 4, half // 2, 2 * rows)), (2, 4, 1, 4, half // 2, 2 * rows), lambda i: (0, 0, i, 0, 0, 0))],
        [info, (own, one, lambda i: (i, 0, 0)), (peer, one, lambda i: (i, 0, 0))],
        grid=(2,),
        scalars=1,
        nbytes=8 * rows * model,
        name="flip",
    )

    quarter = HD // 4
    frequency = ROPE_BASE ** (-jnp.arange(quarter, dtype=F32) / quarter)
    angle_r = positions[0].astype(F32)[:, None] * frequency[None, :]
    angle_c = positions[1].astype(F32)[:, None] * frequency[None, :]
    cos_r, sin_r, cos_c, sin_c = jnp.cos(angle_r), jnp.sin(angle_r), jnp.cos(angle_c), jnp.sin(angle_c)
    cos_t = jnp.concatenate([cos_r, cos_r, cos_c, cos_c], axis=1)
    sin_t = jnp.concatenate([-sin_r, sin_r, -sin_c, sin_c], axis=1)

    lin_shape = shape((rows, 4 * cols), F32)
    lin = []
    for first, pairs in ((0, 3), (3, 1)):
        span = 2 * pairs * width
        columns = functools.partial(lambda c, m: (m // 3, 0, c), first // pairs)
        acc = ((rows, cols), lambda m: (0, m))
        lin = call(
            functools.partial(linear_kernel, pairs),
            [(lin_shape, *acc)] * 2,
            [(own, (1, rows, span), columns), (peer, (1, rows, span), columns)]
            + [(w_j, (1, width, cols), lambda m: (m, 0, 0)) for w_j in shards[2 * first : 2 * (first + pairs)]]
            + [(value, *acc) for value in lin],
            grid=(4,),
            flops=2 * 2 * rows * 2 * pairs * width * 4 * cols,
            nbytes=2 * pairs * width * 8 * cols + 8 * rows * 2 * pairs * width,
            name="linear",
            after=[] if first else [turned, cos_t, sin_t, ends],
        )
    lin_own, lin_send = lin
    lin_peer = shift(lin_send, dc=1)
    (y_own,) = call(
        attend_kernel,
        [shape((rows, 4 * cols))],
        [ends, lin_own, lin_peer, cos_t, sin_t],
        scalars=1,
        flops=HEADS * 10 * rows * rows * HD * 2,
        nbytes=10 * rows * 4 * cols,
        name="attend",
    )
    y_peer = shift(y_own, dc=1)

    quarter = half // 2
    piece = shape((4, 8, quarter, 128))

    def terms(steps):
        part = len(steps) / 4
        picks = [functools.partial(lambda step, _: (0, step, 0, 0, 0, 0), step) for step in steps]
        return call(
            functools.partial(terms_kernel, len(steps)),
            [piece] * (2 * len(steps)),
            [(turned, (2, 1, 2, 4, quarter, 2 * rows), pick) for pick in picks] + [y_own, y_peer],
            flops=int(part * 2 * 2 * rows * (model // 2) * 4 * cols),
            nbytes=int(part * (4 * model * cols + 8 * rows * model)),
            name="terms",
        )

    far = terms([2])
    far = [along(far[0], first=1), along(far[1], first=-1)]
    back = terms([3])
    back = [along(back[0], first=-1), along(back[1], first=1)]
    near = terms([1, 0])

    per_u = ((1, 8, quarter, 128), lambda u: (u, 0, 0, 0))
    joined = sum_call(
        join_kernel,
        "join",
        [(piece, *per_u)] * 2,
        [(near[0], *per_u), (far[0], *per_u), (near[1], *per_u), (far[1], *per_u)],
        grid=(4,),
    )
    ahead = [along(joined[0], first=1), along(joined[1], first=-1)]

    most = ((3, width, cols), lambda _: (0, 0, 0))
    g_own, g_send = call(
        functools.partial(normed_grad_kernel, width),
        [shape((rows, model // 2), F32)] * 2,
        [y_own, y_peer] + [(w_j, *most) for w_j in shards],
        flops=2 * rows * model * 3 * cols,
        nbytes=4 * model * cols + 4 * rows * model,
        name="normed_grad",
        after=[joined[0]],
    )

    per_n = ((4, 2, quarter, 128), lambda n: (0, n, 0, 0))
    mixed = shape((8, 2, quarter, 128))
    out_n = ((2, 2, quarter, 128), lambda n: (n, 0, 0, 0))
    halfway = sum_call(
        sides_kernel,
        "sides",
        [(mixed, *out_n)] * 4,
        [(value, *per_n) for value in (near[2], back[0], ahead[0], near[3], back[1], ahead[1])],
        grid=(4,),
        after=[g_send],
    )
    g_peer = shift(gate(g_send, [halfway[0]]), dc=1)
    g_rows = ((some, model // 2), lambda i: (i, 0))
    (grad_tokens,) = call(
        functools.partial(token_grad_kernel, width),
        [(shape((rows, model)), (some, model), lambda i: (i, 0))],
        [info, (tokens, (some, model), lambda i: (i, 0)), (g_own, *g_rows), (g_peer, *g_rows)],
        grid=(4,),
        scalars=1,
        scratch=[pltpu.VMEM((some, model), F32)],
        flops=16 * rows * model,
        nbytes=8 * rows * model,
        name="token_grad",
    )

    rest = [along(halfway[d], second=d) for d in range(1, 4)]
    (by_z,) = sum_call(
        seconds_kernel,
        "seconds",
        [(mixed, *out_n)],
        [(value, *out_n) for value in [halfway[0]] + rest],
        grid=(4,),
        after=[grad_tokens],
    )
    (spread,) = sum_call(last_kernel, "last", [shape((2 * NZ, 2, quarter, 128))], [exchange(by_z, False)])
    done = exchange(spread, True).reshape(2, NZ, 2, quarter, 128)
    per_m = ((2, 2, 2, quarter, 128), lambda m: (0, m, 0, 0, 0))
    (weight_grads,) = call(
        place_kernel,
        [(shape((4, shard_rows, cols), F32), (1, shard_rows, cols), lambda m: (m, 0, 0))],
        [info, (done, *per_m), (shift(done, dc=1), *per_m)],
        grid=(4,),
        scalars=1,
        flops=4 * shard_rows * cols,
        nbytes=24 * shard_rows * cols,
        name="place",
    )
    return (grad_tokens, weight_grads)


def solution(mesh):
    return jax.shard_map(
        per_device,
        mesh=mesh,
        in_specs=(
            P(("dp", "fsdp"), None),
            P(("dp", "fsdp"), None),
            P(("dp", "fsdp"), None),
            P(None, ("dp", "fsdp")),
            P(None, "fsdp", None),
        ),
        out_specs=(P(("dp", "fsdp"), None), P(None, "fsdp", None)),
        check_vma=False,
    )
```

```python
import functools
import math

import jax
import jax.numpy as jnp
from jax import lax
from jax.experimental import pallas as pl
from jax.experimental.pallas import tpu as pltpu
from jax.sharding import PartitionSpec as P

HD = 128
HEADS = 2
ROPE_BASE = 100.0
EPS = 1e-6
NX, NY, NZ = 4, 4, 8
ORDER = [(0, 0), (0, 1), (1, 0), (1, 1), (3, 0), (2, 0), (3, 1), (2, 1)]
X_AT, X_LO, CORE, SIGN = 16, 17, 18, 19
BF16, F32 = jnp.bfloat16, jnp.float32


def flat_index(x, y, z, core):
    return ((x // 2) * 16 + z * 2 + core) * 8 + y * 2 + x % 2


DEVICES = [(x, y, z, core) for x in range(NX) for y in range(NY) for z in range(NZ) for core in range(2)]


def permute(values, target):
    pairs = []
    for x, y, z, core in DEVICES:
        tx, ty, tz, tcore = target(x, y, z, core)
        pairs.append((flat_index(x, y, z, core), flat_index(tx % NX, ty % NY, tz % NZ, tcore)))
    return lax.ppermute(values, ("dp", "fsdp"), pairs)


def shift(values, dx=0, dy=0, dc=0):
    def target(x, y, z, core):
        s = 1 - 2 * core
        return x + s * dx, y + s * dy, z, core ^ dc

    return permute(values, target)


def along(values, first=0, second=0):
    def target(x, y, z, core):
        dx, dy = (second, first) if core == 0 else (first, second)
        return x + dx, y + dy, z, core

    return permute(values, target)


def call(body, outs, operands, grid=(), scalars=0, scratch=(), flops=0, nbytes=0, name=None, after=()):
    count, last = len(operands), len(operands) + len(after)
    held = 0
    arrays, in_specs, out_shapes, out_specs = [], [], [], []
    for k, item in enumerate(list(operands) + list(outs)):
        value, *place = item if isinstance(item, tuple) else (item,)
        if k < scalars:
            spec = pl.BlockSpec(memory_space=pltpu.SMEM)
        elif place:
            spec = pl.BlockSpec(place[0], place[1])
            held += 2 * math.prod(place[0]) * value.dtype.itemsize
        else:
            spec = pl.BlockSpec(memory_space=pltpu.VMEM)
            held += math.prod(value.shape) * value.dtype.itemsize
        (arrays if k < count else out_shapes).append(value)
        (in_specs if k < count else out_specs).append(spec)
    held += sum(math.prod(ref.shape) * ref.dtype.itemsize for ref in scratch)
    in_specs += [pl.BlockSpec(memory_space=pl.ANY) for _ in after]
    kernel = (lambda *refs: body(*refs[:count], *refs[last:])) if after else body
    return pl.pallas_call(
        kernel,
        grid=grid or (1,),
        out_shape=out_shapes,
        in_specs=in_specs,
        out_specs=out_specs,
        scratch_shapes=list(scratch),
        compiler_params=pltpu.CompilerParams(vmem_limit_bytes=held + 8 * 1024 * 1024),
        cost_estimate=pl.CostEstimate(flops=flops, bytes_accessed=nbytes, transcendentals=0),
        name=name,
    )(*arrays, *after)


def gate(value, after):
    return pl.pallas_call(
        lambda *refs: None,
        out_shape=shape(value.shape, value.dtype),
        in_specs=[pl.BlockSpec(memory_space=pl.ANY)] * (1 + len(after)),
        out_specs=pl.BlockSpec(memory_space=pl.ANY),
        input_output_aliases={0: 0},
        cost_estimate=pl.CostEstimate(flops=1, bytes_accessed=1, transcendentals=0),
        name="gate",
    )(value, *after)


def shape(dims, dtype=BF16):
    return jax.ShapeDtypeStruct(dims, dtype)


def prep_kernel(width, info, tokens, cot, *refs):
    passed, out, normed = refs[:-2], refs[-2], refs[-1]
    rows, model = tokens.shape
    step = 16
    for i in range(rows // step):
        at = slice(i * step, (i + 1) * step)
        x = tokens[at, :].astype(F32)
        center = x - jnp.sum(x, axis=1, keepdims=True) / model
        var = jnp.sum(center * center, axis=1, keepdims=True) / model
        normed[at, :] = (center * lax.rsqrt(var + EPS)).astype(BF16)
    for j in range(8):
        to = slice(j * width, (j + 1) * width)
        cols = pl.ds(pl.multiple_of(info[j], 128), width)
        out[0, :, to] = normed[:, cols]
        out[1, :, to] = cot[:, cols]
    if passed:
        passed[1][...] = passed[0][...]


def flip_kernel(width, info, own, peer, out):
    half = width // 2
    quarter = half // 2
    core, sign, x_at = info[CORE], info[SIGN], info[X_AT]
    for j, (k, dx) in enumerate(ORDER):
        at = slice(j * width, (j + 1) * width)
        y_steps = lax.rem(4 - sign * k, 4)
        turned = jnp.concatenate([own[0, :, at], peer[0, :, at]], axis=0).T
        for x_hi in range(2):
            x_to = 2 * x_hi + lax.rem(info[X_LO] + dx, 2)
            x_steps = lax.rem(x_to - x_at + 4, 4)
            first = jnp.where(core == 0, y_steps, x_steps)
            second = jnp.where(core == 0, x_steps, y_steps)
            for side in range(2):
                steps = first if side == 0 else lax.rem(4 - first, 4)
                start = x_hi * half + side * quarter
                out[side, steps, 0, second] = turned[start : start + quarter]


def linear_kernel(pairs, own, peer, *refs):
    shards, rest = refs[: 2 * pairs], refs[2 * pairs :]
    before, outs = rest[:-2], rest[-2:]
    depth = own.shape[2] // pairs
    rights = [jnp.concatenate([shards[2 * p][0], shards[2 * p + 1][0]], axis=0) for p in range(pairs)]
    for side, left in enumerate((own, peer)):
        total = before[side][...] if before else None
        for p, right in enumerate(rights):
            term = jnp.dot(left[0, :, p * depth : (p + 1) * depth], right, preferred_element_type=F32)
            total = term if total is None else total + term
        outs[side][...] = total


def swap_quarters(x):
    lane = lax.broadcasted_iota(jnp.int32, x.shape, 1)
    quarter = HD // 4
    up = pltpu.roll(x, HD - quarter, 1)
    down = pltpu.roll(x, quarter, 1)
    return jnp.where(lane % (2 * quarter) < quarter, up, down)


def mean_of(x):
    return jnp.sum(x, axis=1, keepdims=True) * (1.0 / HD)


def norm_rows(x):
    center = x - mean_of(x)
    scale = lax.rsqrt(mean_of(center * center) + EPS)
    return center * scale, scale


def norm_rows_back(g, hat, scale):
    return scale * (g - mean_of(g) - hat * mean_of(g * hat))


def dot_t(a, b, dims):
    return lax.dot_general(a, b, ((dims[0], dims[1]), ((), ())), preferred_element_type=F32)


def attend_kernel(ends, mine, theirs, cos_t, sin_t, out):
    rows = mine.shape[0]
    cols = HEADS * HD
    row_id = lax.broadcasted_iota(jnp.int32, (rows, 1), 0)
    col_id = lax.broadcasted_iota(jnp.int32, (1, rows), 1)

    def slot(ids):
        count = jnp.zeros(ids.shape, jnp.int32)
        for k in range(3):
            count = count + (ids >= ends[k]).astype(jnp.int32)
        return count

    row_slot, col_slot = slot(row_id), slot(col_id)
    same = row_slot == col_slot
    live = row_slot < 3
    cosine, sine = cos_t[...], sin_t[...]
    score_scale = 1.0 / math.sqrt(HD)
    for h in range(HEADS):

        def part(m):
            at = slice(m * cols + h * HD, m * cols + (h + 1) * HD)
            return mine[:, at] + theirs[:, at]

        q_hat, q_scale = norm_rows(part(0))
        k_hat, k_scale = norm_rows(part(1))
        q = (q_hat * cosine + swap_quarters(q_hat) * sine).astype(BF16)
        k = (k_hat * cosine + swap_quarters(k_hat) * sine).astype(BF16)
        v = part(2).astype(BF16)
        ga = jnp.where(live, part(3), 0.0).astype(BF16)
        scores = dot_t(q, k, ((1,), (1,))) * score_scale
        e = jnp.where(same, jnp.exp(scores), 0.0)
        p32 = e / jnp.sum(e, axis=1, keepdims=True)
        p = p32.astype(BF16)
        att = jnp.dot(p, v, preferred_element_type=F32).astype(BF16)
        gv = dot_t(p, ga, ((0,), (0,)))
        gp = dot_t(ga, v, ((1,), (1,))).astype(BF16).astype(F32)
        gs = p32 * (gp - jnp.sum(gp * p32, axis=1, keepdims=True)) * score_scale
        gs = gs.astype(BF16)
        gq = jnp.dot(gs, k, preferred_element_type=F32).astype(BF16).astype(F32)
        gk = dot_t(gs, q, ((0,), (0,))).astype(BF16).astype(F32)
        gq = norm_rows_back(gq * cosine + swap_quarters(gq * sine), q_hat, q_scale)
        gk = norm_rows_back(gk * cosine + swap_quarters(gk * sine), k_hat, k_scale)
        at = lambda m: slice(m * cols + h * HD, m * cols + (h + 1) * HD)
        out[:, at(0)] = gq.astype(BF16)
        out[:, at(1)] = gk.astype(BF16)
        out[:, at(2)] = gv.astype(BF16)
        out[:, at(3)] = jnp.where(live, att.astype(F32), 0.0).astype(BF16)


def terms_kernel(count, *refs):
    turned, (y_own, y_peer), outs = refs[:count], refs[count : count + 2], refs[count + 2 :]
    rows, depth = turned[0].shape[4:]
    y_all = jnp.concatenate([y_own[...], y_peer[...]], axis=0)
    proj = 3 * HEADS * HD
    for k, ref in enumerate(turned):
        for side in range(2):
            for i, right in ((0, y_all[:, :proj]), (1, y_all[:, proj:])):
                left = ref[side, 0, i].reshape(4 * rows, depth)
                value = jnp.dot(left, right, preferred_element_type=F32).astype(BF16)
                for n in range(right.shape[1] // 128):
                    for u in range(4):
                        block = value[u * rows : (u + 1) * rows, n * 128 : (n + 1) * 128]
                        outs[2 * k + side][u, 6 * i + n] = block


def add_up(refs, at):
    total = refs[0][at].astype(F32)
    for ref in refs[1:]:
        total = total + ref[at].astype(F32)
    return total.astype(BF16)


def join_kernel(near_0, far_0, near_1, far_1, out_0, out_1):
    for n in range(8):
        out_0[0, n] = add_up((near_0, far_0), (0, n))
        out_1[0, n] = add_up((near_1, far_1), (0, n))


def sides_kernel(*refs):
    for side in range(2):
        for u, out in enumerate(refs[6:]):
            for n in range(out.shape[0]):
                out[n, side] = add_up(refs[3 * side : 3 * side + 3], (u, n))


def seconds_kernel(*refs):
    for n in range(refs[0].shape[0]):
        for side in range(2):
            refs[-1][n, side] = add_up(refs[:-1], (n, side))


def last_kernel(got, out):
    for side in range(2):
        total = got[0, side].astype(F32)
        for k in range(1, 8):
            total = total + got[k, side].astype(F32)
        for k in range(out.shape[0]):
            out[k, side] = total.astype(BF16)


def sum_call(body, name, outs, operands, grid=(), after=()):
    value = operands[0][0] if isinstance(operands[0], tuple) else operands[0]
    size = math.prod(value.shape)
    return call(
        body,
        outs,
        operands,
        grid=grid,
        flops=len(operands) * size,
        nbytes=2 * size * (len(operands) + 2),
        name=name,
        after=after,
    )


def normed_grad_kernel(width, y_own, y_peer, *refs):
    shards, (g_own, g_send) = refs[:-2], refs[-2:]
    rows = y_own.shape[0]
    proj = 3 * HEADS * HD
    left = jnp.concatenate([y_own[:, :proj], y_peer[:, :proj]], axis=0)
    for j in range(8):
        right = jnp.concatenate([shards[j][m] for m in range(3)], axis=1)
        total = dot_t(left, right, ((1,), (1,)))
        at = slice(j * width, (j + 1) * width)
        g_own[:, at] = total[:rows]
        g_send[:, at] = total[rows:]


def token_grad_kernel(width, info, tokens, g_own, g_peer, out, mark, g):
    mark[...] = jnp.zeros_like(mark)
    rows, model = tokens.shape
    for first, ref in ((0, g_own), (8, g_peer)):
        for j in range(8):
            to = pl.ds(pl.multiple_of(info[first + j], 128), width)
            g[:, to] = ref[:, j * width : (j + 1) * width]
    step = 16
    for i in range(rows // step):
        at = slice(i * step, (i + 1) * step)
        x = tokens[at, :].astype(F32)
        center = x - jnp.sum(x, axis=1, keepdims=True) / model
        scale = lax.rsqrt(jnp.sum(center * center, axis=1, keepdims=True) / model + EPS)
        hat = center * scale
        grad = g[at, :]
        mean_g = jnp.sum(grad, axis=1, keepdims=True) / model
        mean_gh = jnp.sum(grad * hat, axis=1, keepdims=True) / model
        out[at, :] = (scale * (grad - mean_g - hat * mean_gh)).astype(BF16)


def place_kernel(at, blocks, *refs):
    out, rows = refs[-1], blocks.shape[3]
    for h in range(2):
        for n in range(2):
            for side in range(2):
                to = slice((2 * h + side) * rows, (2 * h + side + 1) * rows)
                out[0, to, n * 128 : (n + 1) * 128] = blocks[h, n, side].astype(F32)


def place(at, blocks, dims, before=()):
    return pl.pallas_call(
        place_kernel,
        grid_spec=pltpu.PrefetchScalarGridSpec(
            num_scalar_prefetch=1,
            grid=(4,),
            in_specs=[pl.BlockSpec((2, 2) + blocks.shape[2:], lambda m, at: (0, m, 0, 0, 0))]
            + [pl.BlockSpec(memory_space=pl.ANY) for _ in before],
            out_specs=pl.BlockSpec((1, dims[1] // 2, dims[2]), lambda m, at: (m, at[0], 0)),
        ),
        out_shape=shape(dims, F32),
        input_output_aliases={2: 0} if before else {},
        compiler_params=pltpu.CompilerParams(vmem_limit_bytes=12 * 1024 * 1024),
        cost_estimate=pl.CostEstimate(flops=1, bytes_accessed=8 * math.prod(dims), transcendentals=0),
        name="place",
    )(at, blocks, *before)


def swap_groups(with_x):
    if with_x:
        return [[x * 16 + z * 2 + core for x in range(2) for z in range(NZ)] for core in range(2)]
    return [[x * 16 + z * 2 + core for z in range(NZ)] for x in range(2) for core in range(2)]


def exchange(values, with_x):
    return lax.all_to_all(
        values, "dp", split_axis=0, concat_axis=0, axis_index_groups=swap_groups(with_x), tiled=True
    )


def per_device(tokens, cotangent, lengths, positions, weights):
    rows, model = tokens.shape
    shard_rows, cols = weights.shape[1], weights.shape[2]
    width = shard_rows // 2
    dp, fs = lax.axis_index("dp"), lax.axis_index("fsdp")
    core, x_hi = dp % 2, dp // 16
    y_at, x_lo = fs // 2, fs % 2
    sign = 1 - 2 * core
    offs = []
    for c, s in ((core, sign), (1 - core, -sign)):
        for k, dx in ORDER:
            shard = ((y_at - s * k + 4) % NY) * 2 + (x_lo + dx) % 2
            offs.append(shard * shard_rows + c * width)
    l0, l1, l2 = lengths[0, 0], lengths[0, 1], lengths[0, 2]
    ends = jnp.stack([l0, l0 + l1, l0 + l1 + l2]).astype(jnp.int32)
    info = jnp.stack(offs + [x_hi * 2 + x_lo, x_lo, core, sign]).astype(jnp.int32)
    half = width // 2

    pair = shape((2, rows, model // 2))
    some = rows // 4
    row_block = ((some, model), lambda i: (i, 0))

    def prep(tokens, cotangent, passed=()):
        passed = [(value, (1,) + value.shape[1:], lambda i: (i, 0, 0)) for value in passed]
        return call(
            functools.partial(prep_kernel, width),
            [(shape(item[0].shape), *item[1:]) for item in passed]
            + [(pair, (2, some, model // 2), lambda i: (0, i, 0))],
            [info, (tokens, *row_block), (cotangent, *row_block)] + passed,
            grid=(4,),
            scalars=1,
            scratch=[pltpu.VMEM((some, model), BF16)],
            flops=8 * rows * model,
            nbytes=8 * rows * model,
            name="prep",
        )

    w = {(0, 0): lax.dynamic_slice(weights, (0, core * width, 0), (4, width, cols))}
    later, own = prep(tokens, cotangent, [w[0, 0]])
    (peer,) = prep(shift(tokens, dc=1), shift(cotangent, dc=1))
    one = (1, rows, model // 2)
    (turned,) = call(
        functools.partial(flip_kernel, width),
        [(shape((2, 4, 2, 4, half // 2, 2 * rows)), (2, 4, 1, 4, half // 2, 2 * rows), lambda i: (0, 0, i, 0, 0, 0))],
        [info, (own, one, lambda i: (i, 0, 0)), (peer, one, lambda i: (i, 0, 0))],
        grid=(2,),
        scalars=1,
        nbytes=8 * rows * model,
        name="flip",
    )
    w[0, 1] = shift(w[0, 0], dx=1)
    w[1, 0] = gate(shift(w[0, 0], dy=1), [own, w[0, 1]])
    w[3, 0] = gate(shift(later, dy=-1), [peer])
    w[2, 0] = shift(w[1, 0], dy=1)
    w[1, 1] = gate(shift(w[1, 0], dx=1), [turned])
    w[3, 1] = shift(w[3, 0], dx=1)
    w[2, 1] = shift(w[1, 1], dy=1)
    shards = [w[place] for place in ORDER]

    quarter = HD // 4
    frequency = ROPE_BASE ** (-jnp.arange(quarter, dtype=F32) / quarter)
    angle_r = positions[0].astype(F32)[:, None] * frequency[None, :]
    angle_c = positions[1].astype(F32)[:, None] * frequency[None, :]
    cos_r, sin_r, cos_c, sin_c = jnp.cos(angle_r), jnp.sin(angle_r), jnp.cos(angle_c), jnp.sin(angle_c)
    cos_t = jnp.concatenate([cos_r, cos_r, cos_c, cos_c], axis=1)
    sin_t = jnp.concatenate([-sin_r, sin_r, -sin_c, sin_c], axis=1)

    lin_shape = shape((rows, 4 * cols), F32)
    lin = []
    for first, pairs in ((0, 3), (3, 1)):
        span = 2 * pairs * width
        columns = functools.partial(lambda c, m: (m // 3, 0, c), first // pairs)
        acc = ((rows, cols), lambda m: (0, m))
        lin = call(
            functools.partial(linear_kernel, pairs),
            [(lin_shape, *acc)] * 2,
            [(own, (1, rows, span), columns), (peer, (1, rows, span), columns)]
            + [(w_j, (1, width, cols), lambda m: (m, 0, 0)) for w_j in shards[2 * first : 2 * (first + pairs)]]
            + [(value, *acc) for value in lin],
            grid=(4,),
            flops=2 * 2 * rows * 2 * pairs * width * 4 * cols,
            nbytes=2 * pairs * width * 8 * cols + 8 * rows * 2 * pairs * width,
            name="linear",
            after=[] if first else [turned, cos_t, sin_t, ends],
        )
    lin_own, lin_send = lin
    lin_peer = shift(lin_send, dc=1)
    (y_own,) = call(
        attend_kernel,
        [shape((rows, 4 * cols))],
        [ends, lin_own, lin_peer, cos_t, sin_t],
        scalars=1,
        flops=HEADS * 10 * rows * rows * HD * 2,
        nbytes=10 * rows * 4 * cols,
        name="attend",
    )
    y_peer = shift(y_own, dc=1)

    quarter = half // 2
    piece = shape((4, 8, quarter, 128))

    def terms(steps):
        part = len(steps) / 4
        picks = [functools.partial(lambda step, _: (0, step, 0, 0, 0, 0), step) for step in steps]
        return call(
            functools.partial(terms_kernel, len(steps)),
            [piece] * (2 * len(steps)),
            [(turned, (2, 1, 2, 4, quarter, 2 * rows), pick) for pick in picks] + [y_own, y_peer],
            flops=int(part * 2 * 2 * rows * (model // 2) * 4 * cols),
            nbytes=int(part * (4 * model * cols + 8 * rows * model)),
            name="terms",
        )

    far = terms([2])
    far = [along(far[0], first=1), along(far[1], first=-1)]
    back = terms([3])
    back = [along(back[0], first=-1), along(back[1], first=1)]
    near = terms([1, 0])

    per_u = ((1, 8, quarter, 128), lambda u: (u, 0, 0, 0))
    joined = sum_call(
        join_kernel,
        "join",
        [(piece, *per_u)] * 2,
        [(near[0], *per_u), (far[0], *per_u), (near[1], *per_u), (far[1], *per_u)],
        grid=(4,),
    )
    ahead = [along(joined[0], first=1), along(joined[1], first=-1)]

    most = ((3, width, cols), lambda _: (0, 0, 0))
    g_own, g_send = call(
        functools.partial(normed_grad_kernel, width),
        [shape((rows, model // 2), F32)] * 2,
        [y_own, y_peer] + [(w_j, *most) for w_j in shards],
        flops=2 * rows * model * 3 * cols,
        nbytes=4 * model * cols + 4 * rows * model,
        name="normed_grad",
        after=[joined[0]],
    )

    per_n = ((4, 2, quarter, 128), lambda n: (0, n, 0, 0))
    mixed = shape((8, 2, quarter, 128))
    out_n = ((2, 2, quarter, 128), lambda n: (n, 0, 0, 0))
    halfway = sum_call(
        sides_kernel,
        "sides",
        [(mixed, *out_n)] * 4,
        [(value, *per_n) for value in (near[2], back[0], ahead[0], near[3], back[1], ahead[1])],
        grid=(4,),
        after=[g_send],
    )
    g_peer = shift(gate(g_send, [halfway[0]]), dc=1)
    g_rows = ((some, model // 2), lambda i: (i, 0))
    grad_tokens, mark = call(
        functools.partial(token_grad_kernel, width),
        [(shape((rows, model)), *row_block), (shape((8, 128), F32), (8, 128), lambda i: (0, 0))],
        [info, (tokens, *row_block), (g_own, *g_rows), (g_peer, *g_rows)],
        grid=(4,),
        scalars=1,
        scratch=[pltpu.VMEM((some, model), F32)],
        flops=16 * rows * model,
        nbytes=8 * rows * model,
        name="token_grad",
    )

    rest = [along(halfway[d], second=d) for d in range(1, 4)]
    (by_z,) = sum_call(
        seconds_kernel,
        "seconds",
        [(mixed, *out_n)],
        [(value, *out_n) for value in [halfway[0]] + rest],
        grid=(4,),
        after=[mark],
    )
    (spread,) = sum_call(last_kernel, "last", [shape((2 * NZ, 2, quarter, 128))], [exchange(by_z, False)])
    done = exchange(spread, True).reshape(2, NZ, 2, quarter, 128)
    dims = (4, shard_rows, cols)
    weight_grads = place(jnp.stack([core]).astype(jnp.int32), done, dims)
    weight_grads = place(jnp.stack([1 - core]).astype(jnp.int32), shift(done, dc=1), dims, [weight_grads])
    return (grad_tokens, weight_grads)


def solution(mesh):
    return jax.shard_map(
        per_device,
        mesh=mesh,
        in_specs=(
            P(("dp", "fsdp"), None),
            P(("dp", "fsdp"), None),
            P(("dp", "fsdp"), None),
            P(None, ("dp", "fsdp")),
            P(None, "fsdp", None),
        ),
        out_specs=(P(("dp", "fsdp"), None), P(None, "fsdp", None)),
        check_vma=False,
    )
```

```python
import functools
import math

import jax
import jax.numpy as jnp
from jax import lax
from jax.experimental import pallas as pl
from jax.experimental.pallas import tpu as pltpu
from jax.sharding import PartitionSpec as P

HD = 128
HEADS = 2
ROPE_BASE = 100.0
EPS = 1e-6
MOST_VMEM = 56 * 1024 * 1024
NX, NY, NZ = 4, 4, 8
ORDER = [(0, 0), (0, 1), (1, 0), (1, 1), (3, 0), (2, 0), (3, 1), (2, 1)]
X_AT, X_LO, CORE, SIGN = 16, 17, 18, 19
BF16, F32 = jnp.bfloat16, jnp.float32


def flat_index(x, y, z, core):
    return ((x // 2) * 16 + z * 2 + core) * 8 + y * 2 + x % 2


DEVICES = [(x, y, z, core) for x in range(NX) for y in range(NY) for z in range(NZ) for core in range(2)]


def permute(values, target):
    pairs = []
    for x, y, z, core in DEVICES:
        tx, ty, tz, tcore = target(x, y, z, core)
        pairs.append((flat_index(x, y, z, core), flat_index(tx % NX, ty % NY, tz % NZ, tcore)))
    return lax.ppermute(values, ("dp", "fsdp"), pairs)


def shift(values, dx=0, dy=0, dc=0):
    def target(x, y, z, core):
        s = 1 - 2 * core
        return x + s * dx, y + s * dy, z, core ^ dc

    return permute(values, target)


def along(values, first=0, second=0):
    def target(x, y, z, core):
        dx, dy = (second, first) if core == 0 else (first, second)
        return x + dx, y + dy, z, core

    return permute(values, target)


def call(body, outs, operands, grid=(), scalars=0, scratch=(), flops=0, nbytes=0, name=None, after=(), room=0):
    count, last = len(operands), len(operands) + len(after)
    marked = last + len(outs)
    held = 0
    arrays, in_specs, out_shapes, out_specs = [], [], [], []
    for k, item in enumerate(list(operands) + list(outs)):
        value, *place = item if isinstance(item, tuple) else (item,)
        if k < scalars:
            spec = pl.BlockSpec(memory_space=pltpu.SMEM)
        elif place:
            spec = pl.BlockSpec(place[0], place[1])
            held += 2 * math.prod(place[0]) * value.dtype.itemsize
        else:
            spec = pl.BlockSpec(memory_space=pltpu.VMEM)
            held += math.prod(value.shape) * value.dtype.itemsize
        (arrays if k < count else out_shapes).append(value)
        (in_specs if k < count else out_specs).append(spec)
    held += sum(math.prod(ref.shape) * ref.dtype.itemsize for ref in scratch)
    in_specs += [pl.BlockSpec(memory_space=pl.ANY) for _ in after]

    def kernel(*refs):
        refs[marked][...] = jnp.zeros((8, 128), F32)
        body(*refs[:count], *refs[last:marked], *refs[marked + 1 :])

    *results, mark = pl.pallas_call(
        kernel,
        grid=grid or (1,),
        out_shape=out_shapes + [shape((8, 128), F32)],
        in_specs=in_specs,
        out_specs=out_specs + [pl.BlockSpec((8, 128), lambda i: (0, 0))],
        scratch_shapes=list(scratch),
        compiler_params=pltpu.CompilerParams(vmem_limit_bytes=room or held + 8 * 1024 * 1024),
        cost_estimate=pl.CostEstimate(flops=flops, bytes_accessed=nbytes, transcendentals=0),
        name=name,
    )(*arrays, *after)
    return results, mark


def gate(value, after):
    return pl.pallas_call(
        lambda *refs: None,
        out_shape=shape(value.shape, value.dtype),
        in_specs=[pl.BlockSpec(memory_space=pl.ANY)] * (1 + len(after)),
        out_specs=pl.BlockSpec(memory_space=pl.ANY),
        input_output_aliases={0: 0},
        cost_estimate=pl.CostEstimate(flops=1, bytes_accessed=1, transcendentals=0),
        name="gate",
    )(value, *after)


def shape(dims, dtype=BF16):
    return jax.ShapeDtypeStruct(dims, dtype)


def prep_kernel(width, info, tokens, cot, *refs):
    passed, out, normed = refs[:-2], refs[-2], refs[-1]
    rows, model = tokens.shape
    step = 16
    for i in range(rows // step):
        at = slice(i * step, (i + 1) * step)
        x = tokens[at, :].astype(F32)
        center = x - jnp.sum(x, axis=1, keepdims=True) / model
        var = jnp.sum(center * center, axis=1, keepdims=True) / model
        normed[at, :] = (center * lax.rsqrt(var + EPS)).astype(BF16)
    for j in range(8):
        to = slice(j * width, (j + 1) * width)
        cols = pl.ds(pl.multiple_of(info[j], 128), width)
        out[0, :, to] = normed[:, cols]
        out[1, :, to] = cot[:, cols]
    if passed:
        passed[1][...] = passed[0][...]


def flip_kernel(width, info, own, peer, out):
    half = width // 2
    quarter = half // 2
    core, sign, x_at = info[CORE], info[SIGN], info[X_AT]
    for j, (k, dx) in enumerate(ORDER):
        at = slice(j * width, (j + 1) * width)
        y_steps = lax.rem(4 - sign * k, 4)
        turned = jnp.concatenate([own[0, :, at], peer[0, :, at]], axis=0).T
        for x_hi in range(2):
            x_to = 2 * x_hi + lax.rem(info[X_LO] + dx, 2)
            x_steps = lax.rem(x_to - x_at + 4, 4)
            first = jnp.where(core == 0, y_steps, x_steps)
            second = jnp.where(core == 0, x_steps, y_steps)
            for side in range(2):
                steps = first if side == 0 else lax.rem(4 - first, 4)
                start = x_hi * half + side * quarter
                out[side, steps, 0, second] = turned[start : start + quarter]


def linear_kernel(pairs, own, peer, *refs):
    shards, rest = refs[: 2 * pairs], refs[2 * pairs :]
    before, outs = rest[:-2], rest[-2:]
    depth = own.shape[2] // pairs
    rights = [jnp.concatenate([shards[2 * p][0], shards[2 * p + 1][0]], axis=0) for p in range(pairs)]
    for side, left in enumerate((own, peer)):
        total = before[side][...] if before else None
        for p, right in enumerate(rights):
            term = jnp.dot(left[0, :, p * depth : (p + 1) * depth], right, preferred_element_type=F32)
            total = term if total is None else total + term
        outs[side][...] = total


def swap_quarters(x):
    lane = lax.broadcasted_iota(jnp.int32, x.shape, 1)
    quarter = HD // 4
    up = pltpu.roll(x, HD - quarter, 1)
    down = pltpu.roll(x, quarter, 1)
    return jnp.where(lane % (2 * quarter) < quarter, up, down)


def mean_of(x):
    return jnp.sum(x, axis=1, keepdims=True) * (1.0 / HD)


def norm_rows(x):
    center = x - mean_of(x)
    scale = lax.rsqrt(mean_of(center * center) + EPS)
    return center * scale, scale


def norm_rows_back(g, hat, scale):
    return scale * (g - mean_of(g) - hat * mean_of(g * hat))


def dot_t(a, b, dims):
    return lax.dot_general(a, b, ((dims[0], dims[1]), ((), ())), preferred_element_type=F32)


def attend_kernel(ends, mine, theirs, cos_t, sin_t, out):
    rows = mine.shape[0]
    cols = HEADS * HD
    row_id = lax.broadcasted_iota(jnp.int32, (rows, 1), 0)
    col_id = lax.broadcasted_iota(jnp.int32, (1, rows), 1)

    def slot(ids):
        count = jnp.zeros(ids.shape, jnp.int32)
        for k in range(3):
            count = count + (ids >= ends[k]).astype(jnp.int32)
        return count

    row_slot, col_slot = slot(row_id), slot(col_id)
    same = row_slot == col_slot
    live = row_slot < 3
    cosine, sine = cos_t[...], sin_t[...]
    score_scale = 1.0 / math.sqrt(HD)
    for h in range(HEADS):

        def part(m):
            at = slice(m * cols + h * HD, m * cols + (h + 1) * HD)
            return mine[:, at] + theirs[:, at]

        q_hat, q_scale = norm_rows(part(0))
        k_hat, k_scale = norm_rows(part(1))
        q = (q_hat * cosine + swap_quarters(q_hat) * sine).astype(BF16)
        k = (k_hat * cosine + swap_quarters(k_hat) * sine).astype(BF16)
        v = part(2).astype(BF16)
        ga = jnp.where(live, part(3), 0.0).astype(BF16)
        scores = dot_t(q, k, ((1,), (1,))) * score_scale
        e = jnp.where(same, jnp.exp(scores), 0.0)
        p32 = e / jnp.sum(e, axis=1, keepdims=True)
        p = p32.astype(BF16)
        att = jnp.dot(p, v, preferred_element_type=F32).astype(BF16)
        gv = dot_t(p, ga, ((0,), (0,)))
        gp = dot_t(ga, v, ((1,), (1,))).astype(BF16).astype(F32)
        gs = p32 * (gp - jnp.sum(gp * p32, axis=1, keepdims=True)) * score_scale
        gs = gs.astype(BF16)
        gq = jnp.dot(gs, k, preferred_element_type=F32).astype(BF16).astype(F32)
        gk = dot_t(gs, q, ((0,), (0,))).astype(BF16).astype(F32)
        gq = norm_rows_back(gq * cosine + swap_quarters(gq * sine), q_hat, q_scale)
        gk = norm_rows_back(gk * cosine + swap_quarters(gk * sine), k_hat, k_scale)
        at = lambda m: slice(m * cols + h * HD, m * cols + (h + 1) * HD)
        out[:, at(0)] = gq.astype(BF16)
        out[:, at(1)] = gk.astype(BF16)
        out[:, at(2)] = gv.astype(BF16)
        out[:, at(3)] = jnp.where(live, att.astype(F32), 0.0).astype(BF16)


def terms_kernel(count, *refs):
    turned, (y_own, y_peer), outs = refs[:count], refs[count : count + 2], refs[count + 2 :]
    rows, depth = turned[0].shape[4:]
    y_all = jnp.concatenate([y_own[...], y_peer[...]], axis=0)
    proj = 3 * HEADS * HD
    for k, ref in enumerate(turned):
        for side in range(2):
            for i, right in ((0, y_all[:, :proj]), (1, y_all[:, proj:])):
                left = ref[side, 0, i].reshape(4 * rows, depth)
                value = jnp.dot(left, right, preferred_element_type=F32).astype(BF16)
                for n in range(right.shape[1] // 128):
                    for u in range(4):
                        block = value[u * rows : (u + 1) * rows, n * 128 : (n + 1) * 128]
                        outs[2 * k + side][u, 6 * i + n] = block


def add_up(refs, at):
    total = refs[0][at].astype(F32)
    for ref in refs[1:]:
        total = total + ref[at].astype(F32)
    return total.astype(BF16)


def join_kernel(near_0, far_0, near_1, far_1, out_0, out_1):
    for n in range(8):
        out_0[0, n] = add_up((near_0, far_0), (0, n))
        out_1[0, n] = add_up((near_1, far_1), (0, n))


def sides_kernel(*refs):
    for side in range(2):
        for u, out in enumerate(refs[6:]):
            for n in range(out.shape[0]):
                out[n, side] = add_up(refs[3 * side : 3 * side + 3], (u, n))


def seconds_kernel(*refs):
    for n in range(refs[0].shape[0]):
        for side in range(2):
            refs[-1][n, side] = add_up(refs[:-1], (n, side))


def last_kernel(got, out):
    for side in range(2):
        total = got[0, side].astype(F32)
        for k in range(1, 8):
            total = total + got[k, side].astype(F32)
        for k in range(out.shape[0]):
            out[k, side] = total.astype(BF16)


def sum_call(body, name, outs, operands, grid=(), after=()):
    value = operands[0][0] if isinstance(operands[0], tuple) else operands[0]
    size = math.prod(value.shape)
    return call(
        body,
        outs,
        operands,
        grid=grid,
        flops=len(operands) * size,
        nbytes=2 * size * (len(operands) + 2),
        name=name,
        after=after,
    )


def normed_grad_kernel(width, y_own, y_peer, *refs):
    shards, (g_own, g_send) = refs[:-2], refs[-2:]
    rows = y_own.shape[0]
    proj = 3 * HEADS * HD
    left = jnp.concatenate([y_own[:, :proj], y_peer[:, :proj]], axis=0)
    for j in range(8):
        right = jnp.concatenate([shards[j][m] for m in range(3)], axis=1)
        total = dot_t(left, right, ((1,), (1,)))
        at = slice(j * width, (j + 1) * width)
        g_own[:, at] = total[:rows]
        g_send[:, at] = total[rows:]


def token_grad_kernel(width, info, tokens, g_own, g_peer, out, g):
    rows, model = tokens.shape
    for first, ref in ((0, g_own), (8, g_peer)):
        for j in range(8):
            to = pl.ds(pl.multiple_of(info[first + j], 128), width)
            g[:, to] = ref[:, j * width : (j + 1) * width]
    step = 16
    for i in range(rows // step):
        at = slice(i * step, (i + 1) * step)
        x = tokens[at, :].astype(F32)
        center = x - jnp.sum(x, axis=1, keepdims=True) / model
        scale = lax.rsqrt(jnp.sum(center * center, axis=1, keepdims=True) / model + EPS)
        hat = center * scale
        grad = g[at, :]
        mean_g = jnp.sum(grad, axis=1, keepdims=True) / model
        mean_gh = jnp.sum(grad * hat, axis=1, keepdims=True) / model
        out[at, :] = (scale * (grad - mean_g - hat * mean_gh)).astype(BF16)


def place_kernel(at, blocks, *refs):
    out, rows = refs[-1], blocks.shape[3]
    for h in range(2):
        for n in range(2):
            for side in range(2):
                to = slice((2 * h + side) * rows, (2 * h + side + 1) * rows)
                out[0, to, n * 128 : (n + 1) * 128] = blocks[h, n, side].astype(F32)


def place(at, blocks, dims, before=()):
    return pl.pallas_call(
        place_kernel,
        grid_spec=pltpu.PrefetchScalarGridSpec(
            num_scalar_prefetch=1,
            grid=(4,),
            in_specs=[pl.BlockSpec((2, 2) + blocks.shape[2:], lambda m, at: (0, m, 0, 0, 0))]
            + [pl.BlockSpec(memory_space=pl.ANY) for _ in before],
            out_specs=pl.BlockSpec((1, dims[1] // 2, dims[2]), lambda m, at: (m, at[0], 0)),
        ),
        out_shape=shape(dims, F32),
        input_output_aliases={2: 0} if before else {},
        compiler_params=pltpu.CompilerParams(vmem_limit_bytes=12 * 1024 * 1024),
        cost_estimate=pl.CostEstimate(flops=1, bytes_accessed=8 * math.prod(dims), transcendentals=0),
        name="place",
    )(at, blocks, *before)


def swap_groups(with_x):
    if with_x:
        return [[x * 16 + z * 2 + core for x in range(2) for z in range(NZ)] for core in range(2)]
    return [[x * 16 + z * 2 + core for z in range(NZ)] for x in range(2) for core in range(2)]


def exchange(values, with_x):
    return lax.all_to_all(
        values, "dp", split_axis=0, concat_axis=0, axis_index_groups=swap_groups(with_x), tiled=True
    )


def per_device(tokens, cotangent, lengths, positions, weights):
    rows, model = tokens.shape
    shard_rows, cols = weights.shape[1], weights.shape[2]
    width = shard_rows // 2
    dp, fs = lax.axis_index("dp"), lax.axis_index("fsdp")
    core, x_hi = dp % 2, dp // 16
    y_at, x_lo = fs // 2, fs % 2
    sign = 1 - 2 * core
    offs = []
    for c, s in ((core, sign), (1 - core, -sign)):
        for k, dx in ORDER:
            shard = ((y_at - s * k + 4) % NY) * 2 + (x_lo + dx) % 2
            offs.append(shard * shard_rows + c * width)
    l0, l1, l2 = lengths[0, 0], lengths[0, 1], lengths[0, 2]
    ends = jnp.stack([l0, l0 + l1, l0 + l1 + l2]).astype(jnp.int32)
    info = jnp.stack(offs + [x_hi * 2 + x_lo, x_lo, core, sign]).astype(jnp.int32)
    half = width // 2

    pair = shape((2, rows, model // 2))
    some = rows // 4
    row_block = ((some, model), lambda i: (i, 0))

    def prep(tokens, cotangent, passed=(), room=0):
        passed = [(value, (1,) + value.shape[1:], lambda i: (i, 0, 0)) for value in passed]
        return call(
            functools.partial(prep_kernel, width),
            [(shape(item[0].shape), *item[1:]) for item in passed]
            + [(pair, (2, some, model // 2), lambda i: (0, i, 0))],
            [info, (tokens, *row_block), (cotangent, *row_block)] + passed,
            grid=(4,),
            scalars=1,
            scratch=[pltpu.VMEM((some, model), BF16)],
            flops=8 * rows * model,
            nbytes=8 * rows * model,
            name="prep",
            room=room,
        )

    w = {(0, 0): lax.dynamic_slice(weights, (0, core * width, 0), (4, width, cols))}
    (later, own), own_mark = prep(tokens, cotangent, [w[0, 0]], room=MOST_VMEM)
    (peer,), peer_mark = prep(shift(tokens, dc=1), shift(cotangent, dc=1))
    one = (1, rows, model // 2)
    (turned,), turned_mark = call(
        functools.partial(flip_kernel, width),
        [(shape((2, 4, 2, 4, half // 2, 2 * rows)), (2, 4, 1, 4, half // 2, 2 * rows), lambda i: (0, 0, i, 0, 0, 0))],
        [info, (own, one, lambda i: (i, 0, 0)), (peer, one, lambda i: (i, 0, 0))],
        grid=(2,),
        scalars=1,
        nbytes=8 * rows * model,
        name="flip",
    )
    w[0, 1] = shift(w[0, 0], dx=1)
    w[1, 0] = gate(shift(w[0, 0], dy=1), [own_mark, w[0, 1]])
    w[3, 0] = gate(shift(later, dy=-1), [peer_mark])
    w[2, 0] = shift(w[1, 0], dy=1)
    w[1, 1] = gate(shift(w[1, 0], dx=1), [turned_mark])
    w[3, 1] = shift(w[3, 0], dx=1)
    w[2, 1] = shift(w[1, 1], dy=1)
    shards = [w[place] for place in ORDER]

    quarter = HD // 4
    frequency = ROPE_BASE ** (-jnp.arange(quarter, dtype=F32) / quarter)
    angle_r = positions[0].astype(F32)[:, None] * frequency[None, :]
    angle_c = positions[1].astype(F32)[:, None] * frequency[None, :]
    cos_r, sin_r, cos_c, sin_c = jnp.cos(angle_r), jnp.sin(angle_r), jnp.cos(angle_c), jnp.sin(angle_c)
    cos_t = jnp.concatenate([cos_r, cos_r, cos_c, cos_c], axis=1)
    sin_t = jnp.concatenate([-sin_r, sin_r, -sin_c, sin_c], axis=1)

    lin_shape = shape((rows, 4 * cols), F32)
    lin = []
    for first, pairs in ((0, 3), (3, 1)):
        span = 2 * pairs * width
        columns = functools.partial(lambda c, m: (m // 3, 0, c), first // pairs)
        acc = ((rows, cols), lambda m: (0, m))
        lin, _ = call(
            functools.partial(linear_kernel, pairs),
            [(lin_shape, *acc)] * 2,
            [(own, (1, rows, span), columns), (peer, (1, rows, span), columns)]
            + [(w_j, (1, width, cols), lambda m: (m, 0, 0)) for w_j in shards[2 * first : 2 * (first + pairs)]]
            + [(value, *acc) for value in lin],
            grid=(4,),
            flops=2 * 2 * rows * 2 * pairs * width * 4 * cols,
            nbytes=2 * pairs * width * 8 * cols + 8 * rows * 2 * pairs * width,
            name="linear",
            after=[] if first else [turned_mark, cos_t, sin_t],
        )
    lin_own, lin_send = lin
    lin_peer = shift(lin_send, dc=1)
    (y_own,), _ = call(
        attend_kernel,
        [shape((rows, 4 * cols))],
        [ends, lin_own, lin_peer, cos_t, sin_t],
        scalars=1,
        flops=HEADS * 10 * rows * rows * HD * 2,
        nbytes=10 * rows * 4 * cols,
        name="attend",
    )
    y_peer = shift(y_own, dc=1)

    quarter = half // 2
    piece = shape((4, 8, quarter, 128))

    def terms(steps):
        part = len(steps) / 4
        picks = [functools.partial(lambda step, _: (0, step, 0, 0, 0, 0), step) for step in steps]
        return call(
            functools.partial(terms_kernel, len(steps)),
            [piece] * (2 * len(steps)),
            [(turned, (2, 1, 2, 4, quarter, 2 * rows), pick) for pick in picks] + [y_own, y_peer],
            flops=int(part * 2 * 2 * rows * (model // 2) * 4 * cols),
            nbytes=int(part * (4 * model * cols + 8 * rows * model)),
            name="terms",
        )[0]

    far = terms([2])
    far = [along(far[0], first=1), along(far[1], first=-1)]
    back = terms([3])
    back = [along(back[0], first=-1), along(back[1], first=1)]
    near = terms([1, 0])

    per_u = ((1, 8, quarter, 128), lambda u: (u, 0, 0, 0))
    joined, join_mark = sum_call(
        join_kernel,
        "join",
        [(piece, *per_u)] * 2,
        [(near[0], *per_u), (far[0], *per_u), (near[1], *per_u), (far[1], *per_u)],
        grid=(4,),
    )
    ahead = [along(joined[0], first=1), along(joined[1], first=-1)]

    most = ((3, width, cols), lambda _: (0, 0, 0))
    (g_own, g_send), g_mark = call(
        functools.partial(normed_grad_kernel, width),
        [shape((rows, model // 2), F32)] * 2,
        [y_own, y_peer] + [(w_j, *most) for w_j in shards],
        flops=2 * rows * model * 3 * cols,
        nbytes=4 * model * cols + 4 * rows * model,
        name="normed_grad",
        after=[join_mark],
    )

    per_n = ((4, 2, quarter, 128), lambda n: (0, n, 0, 0))
    mixed = shape((8, 2, quarter, 128))
    out_n = ((2, 2, quarter, 128), lambda n: (n, 0, 0, 0))
    halfway, halfway_mark = sum_call(
        sides_kernel,
        "sides",
        [(mixed, *out_n)] * 4,
        [(value, *per_n) for value in (near[2], back[0], ahead[0], near[3], back[1], ahead[1])],
        grid=(4,),
        after=[g_mark],
    )
    g_peer = shift(gate(g_send, [halfway_mark]), dc=1)
    g_rows = ((some, model // 2), lambda i: (i, 0))
    (grad_tokens,), mark = call(
        functools.partial(token_grad_kernel, width),
        [(shape((rows, model)), *row_block)],
        [info, (tokens, *row_block), (g_own, *g_rows), (g_peer, *g_rows)],
        grid=(4,),
        scalars=1,
        scratch=[pltpu.VMEM((some, model), F32)],
        flops=16 * rows * model,
        nbytes=8 * rows * model,
        name="token_grad",
        room=MOST_VMEM,
    )

    rest = [along(halfway[d], second=d) for d in range(1, 4)]
    (by_z,), _ = sum_call(
        seconds_kernel,
        "seconds",
        [(mixed, *out_n)],
        [(value, *out_n) for value in [halfway[0]] + rest],
        grid=(4,),
        after=[mark],
    )
    (spread,), _ = sum_call(last_kernel, "last", [shape((2 * NZ, 2, quarter, 128))], [exchange(by_z, False)])
    done = exchange(spread, True).reshape(2, NZ, 2, quarter, 128)
    dims = (4, shard_rows, cols)
    weight_grads = place(jnp.stack([core]).astype(jnp.int32), done, dims)
    weight_grads = place(jnp.stack([1 - core]).astype(jnp.int32), shift(done, dc=1), dims, [weight_grads])
    return (grad_tokens, weight_grads)


def solution(mesh):
    return jax.shard_map(
        per_device,
        mesh=mesh,
        in_specs=(
            P(("dp", "fsdp"), None),
            P(("dp", "fsdp"), None),
            P(("dp", "fsdp"), None),
            P(None, ("dp", "fsdp")),
            P(None, "fsdp", None),
        ),
        out_specs=(P(("dp", "fsdp"), None), P(None, "fsdp", None)),
        check_vma=False,
    )
```

```python
import functools
import math

import jax
import jax.numpy as jnp
import numpy as np
from jax import lax
from jax.experimental import pallas as pl
from jax.experimental.pallas import tpu as pltpu
from jax.sharding import PartitionSpec as P

HD = 128
HEADS = 2
ROPE_BASE = 100.0
EPS = 1e-6
NX, NY, NZ = 4, 4, 8
ORDER = [(0, 0), (0, 1), (1, 0), (1, 1), (3, 0), (2, 0), (3, 1), (2, 1)]
X_AT, X_LO, CORE, SIGN = 16, 17, 18, 19
BF16, F32 = jnp.bfloat16, jnp.float32


def flat_index(x, y, z, core):
    return ((x // 2) * 16 + z * 2 + core) * 8 + y * 2 + x % 2


DEVICES = [(x, y, z, core) for x in range(NX) for y in range(NY) for z in range(NZ) for core in range(2)]


def permute(values, target):
    pairs = []
    for x, y, z, core in DEVICES:
        tx, ty, tz, tcore = target(x, y, z, core)
        pairs.append((flat_index(x, y, z, core), flat_index(tx % NX, ty % NY, tz % NZ, tcore)))
    return lax.ppermute(values, ("dp", "fsdp"), pairs)


def shift(values, dx=0, dy=0, dc=0):
    def target(x, y, z, core):
        s = 1 - 2 * core
        return x + s * dx, y + s * dy, z, core ^ dc

    return permute(values, target)


def along(values, first=0, second=0):
    def target(x, y, z, core):
        dx, dy = (second, first) if core == 0 else (first, second)
        return x + dx, y + dy, z, core

    return permute(values, target)


def call(body, outs, operands, grid=(), scalars=0, scratch=(), flops=0, nbytes=0, name=None, after=()):
    count, last = len(operands), len(operands) + len(after)
    held = 0
    arrays, in_specs, out_shapes, out_specs = [], [], [], []
    for k, item in enumerate(list(operands) + list(outs)):
        value, *place = item if isinstance(item, tuple) else (item,)
        if k < scalars:
            spec = pl.BlockSpec(memory_space=pltpu.SMEM)
        elif place:
            spec = pl.BlockSpec(place[0], place[1])
            held += 2 * math.prod(place[0]) * value.dtype.itemsize
        else:
            spec = pl.BlockSpec(memory_space=pltpu.VMEM)
            held += math.prod(value.shape) * value.dtype.itemsize
        (arrays if k < count else out_shapes).append(value)
        (in_specs if k < count else out_specs).append(spec)
    held += sum(math.prod(ref.shape) * ref.dtype.itemsize for ref in scratch)
    in_specs += [pl.BlockSpec(memory_space=pl.ANY) for _ in after]
    kernel = (lambda *refs: body(*refs[:count], *refs[last:])) if after else body
    return pl.pallas_call(
        kernel,
        grid=grid or (1,),
        out_shape=out_shapes,
        in_specs=in_specs,
        out_specs=out_specs,
        scratch_shapes=list(scratch),
        compiler_params=pltpu.CompilerParams(vmem_limit_bytes=held + 8 * 1024 * 1024),
        cost_estimate=pl.CostEstimate(flops=flops, bytes_accessed=nbytes, transcendentals=0),
        name=name,
    )(*arrays, *after)


def gate(value, after):
    return pl.pallas_call(
        lambda *refs: None,
        out_shape=shape(value.shape, value.dtype),
        in_specs=[pl.BlockSpec(memory_space=pl.ANY)] * (1 + len(after)),
        out_specs=pl.BlockSpec(memory_space=pl.ANY),
        input_output_aliases={0: 0},
        cost_estimate=pl.CostEstimate(flops=1, bytes_accessed=1, transcendentals=0),
        name="gate",
    )(value, *after)


def shape(dims, dtype=BF16):
    return jax.ShapeDtypeStruct(dims, dtype)


def prep_kernel(width, info, tokens, cot, own, send, normed):
    rows, model = tokens.shape
    step = 16
    for i in range(rows // step):
        at = slice(i * step, (i + 1) * step)
        x = tokens[at, :].astype(F32)
        center = x - jnp.sum(x, axis=1, keepdims=True) / model
        var = jnp.sum(center * center, axis=1, keepdims=True) / model
        normed[at, :] = (center * lax.rsqrt(var + EPS)).astype(BF16)
    for j in range(8):
        to = slice(j * width, (j + 1) * width)
        for out, first in ((own, 0), (send, 8)):
            cols = pl.ds(pl.multiple_of(info[first + j], 128), width)
            out[0, :, to] = normed[:, cols]
            out[1, :, to] = cot[:, cols]


def flip_kernel(width, info, own, peer, out):
    half = width // 2
    quarter = half // 2
    core, sign, x_at = info[CORE], info[SIGN], info[X_AT]
    for j, (k, dx) in enumerate(ORDER):
        at = slice(j * width, (j + 1) * width)
        y_steps = lax.rem(4 - sign * k, 4)
        turned = jnp.concatenate([own[0, :, at], peer[0, :, at]], axis=0).T
        for x_hi in range(2):
            x_to = 2 * x_hi + lax.rem(info[X_LO] + dx, 2)
            x_steps = lax.rem(x_to - x_at + 4, 4)
            first = jnp.where(core == 0, y_steps, x_steps)
            second = jnp.where(core == 0, x_steps, y_steps)
            for side in range(2):
                steps = first if side == 0 else lax.rem(4 - first, 4)
                start = x_hi * half + side * quarter
                out[side, steps, 0, second] = turned[start : start + quarter]


def linear_kernel(pairs, own, peer, *refs):
    shards, rest = refs[: 2 * pairs], refs[2 * pairs :]
    before, outs = rest[:-2], rest[-2:]
    depth = own.shape[2] // pairs
    rights = [jnp.concatenate([shards[2 * p][0], shards[2 * p + 1][0]], axis=0) for p in range(pairs)]
    for side, left in enumerate((own, peer)):
        total = before[side][...] if before else None
        for p, right in enumerate(rights):
            term = jnp.dot(left[0, :, p * depth : (p + 1) * depth], right, preferred_element_type=F32)
            total = term if total is None else total + term
        outs[side][...] = total


def swap_quarters(x):
    lane = lax.broadcasted_iota(jnp.int32, x.shape, 1)
    quarter = HD // 4
    up = pltpu.roll(x, HD - quarter, 1)
    down = pltpu.roll(x, quarter, 1)
    return jnp.where(lane % (2 * quarter) < quarter, up, down)


def mean_of(x):
    return jnp.sum(x, axis=1, keepdims=True) * (1.0 / HD)


def norm_rows(x):
    center = x - mean_of(x)
    scale = lax.rsqrt(mean_of(center * center) + EPS)
    return center * scale, scale


def norm_rows_back(g, hat, scale):
    return scale * (g - mean_of(g) - hat * mean_of(g * hat))


def dot_t(a, b, dims):
    return lax.dot_general(a, b, ((dims[0], dims[1]), ((), ())), preferred_element_type=F32)


def attend_kernel(lengths, mine, theirs, cos_t, sin_t, out):
    rows = mine.shape[0]
    cols = HEADS * HD
    row_id = lax.broadcasted_iota(jnp.int32, (rows, 1), 0)
    col_id = lax.broadcasted_iota(jnp.int32, (1, rows), 1)

    def slot(ids):
        count, end = jnp.zeros(ids.shape, jnp.int32), 0
        for k in range(3):
            end = end + lengths[0, k]
            count = count + (ids >= end).astype(jnp.int32)
        return count

    row_slot, col_slot = slot(row_id), slot(col_id)
    same = row_slot == col_slot
    live = row_slot < 3
    cosine, sine = cos_t[...], sin_t[...]
    score_scale = 1.0 / math.sqrt(HD)
    for h in range(HEADS):

        def part(m):
            at = slice(m * cols + h * HD, m * cols + (h + 1) * HD)
            return mine[:, at] + theirs[:, at]

        q_hat, q_scale = norm_rows(part(0))
        k_hat, k_scale = norm_rows(part(1))
        q = (q_hat * cosine + swap_quarters(q_hat) * sine).astype(BF16)
        k = (k_hat * cosine + swap_quarters(k_hat) * sine).astype(BF16)
        v = part(2).astype(BF16)
        ga = jnp.where(live, part(3), 0.0).astype(BF16)
        scores = dot_t(q, k, ((1,), (1,))) * score_scale
        e = jnp.where(same, jnp.exp(scores), 0.0)
        p32 = e / jnp.sum(e, axis=1, keepdims=True)
        p = p32.astype(BF16)
        att = jnp.dot(p, v, preferred_element_type=F32).astype(BF16)
        gv = dot_t(p, ga, ((0,), (0,)))
        gp = dot_t(ga, v, ((1,), (1,))).astype(BF16).astype(F32)
        gs = p32 * (gp - jnp.sum(gp * p32, axis=1, keepdims=True)) * score_scale
        gs = gs.astype(BF16)
        gq = jnp.dot(gs, k, preferred_element_type=F32).astype(BF16).astype(F32)
        gk = dot_t(gs, q, ((0,), (0,))).astype(BF16).astype(F32)
        gq = norm_rows_back(gq * cosine + swap_quarters(gq * sine), q_hat, q_scale)
        gk = norm_rows_back(gk * cosine + swap_quarters(gk * sine), k_hat, k_scale)
        at = lambda m: slice(m * cols + h * HD, m * cols + (h + 1) * HD)
        out[:, at(0)] = gq.astype(BF16)
        out[:, at(1)] = gk.astype(BF16)
        out[:, at(2)] = gv.astype(BF16)
        out[:, at(3)] = jnp.where(live, att.astype(F32), 0.0).astype(BF16)


def terms_kernel(count, *refs):
    turned, (y_own, y_peer), outs = refs[:count], refs[count : count + 2], refs[count + 2 :]
    rows, depth = turned[0].shape[4:]
    y_all = jnp.concatenate([y_own[...], y_peer[...]], axis=0)
    proj = 3 * HEADS * HD
    for k, ref in enumerate(turned):
        for side in range(2):
            for i, right in ((0, y_all[:, :proj]), (1, y_all[:, proj:])):
                left = ref[side, 0, i].reshape(4 * rows, depth)
                value = jnp.dot(left, right, preferred_element_type=F32).astype(BF16)
                for n in range(right.shape[1] // 128):
                    for u in range(4):
                        block = value[u * rows : (u + 1) * rows, n * 128 : (n + 1) * 128]
                        outs[2 * k + side][u, 6 * i + n] = block


def add_up(refs, at):
    total = refs[0][at].astype(F32)
    for ref in refs[1:]:
        total = total + ref[at].astype(F32)
    return total.astype(BF16)


def join_kernel(near_0, far_0, near_1, far_1, out_0, out_1):
    for n in range(8):
        out_0[0, n] = add_up((near_0, far_0), (0, n))
        out_1[0, n] = add_up((near_1, far_1), (0, n))


def sides_kernel(*refs):
    for side in range(2):
        for u, out in enumerate(refs[6:]):
            for n in range(out.shape[0]):
                out[n, side] = add_up(refs[3 * side : 3 * side + 3], (u, n))


def seconds_kernel(*refs):
    for n in range(refs[0].shape[0]):
        for side in range(2):
            refs[-1][n, side] = add_up(refs[:-1], (n, side))


def last_kernel(got, out):
    for side in range(2):
        total = got[0, side].astype(F32)
        for k in range(1, 8):
            total = total + got[k, side].astype(F32)
        for k in range(out.shape[0]):
            out[k, side] = total.astype(BF16)


def sum_call(body, name, outs, operands, grid=(), after=()):
    value = operands[0][0] if isinstance(operands[0], tuple) else operands[0]
    size = math.prod(value.shape)
    return call(
        body,
        outs,
        operands,
        grid=grid,
        flops=len(operands) * size,
        nbytes=2 * size * (len(operands) + 2),
        name=name,
        after=after,
    )


def normed_grad_kernel(width, y_own, y_peer, *refs):
    shards, (g_own, g_send) = refs[:-2], refs[-2:]
    rows = y_own.shape[0]
    proj = 3 * HEADS * HD
    left = jnp.concatenate([y_own[:, :proj], y_peer[:, :proj]], axis=0)
    for j in range(8):
        right = jnp.concatenate([shards[j][m] for m in range(3)], axis=1)
        total = dot_t(left, right, ((1,), (1,)))
        at = slice(j * width, (j + 1) * width)
        g_own[:, at] = total[:rows]
        g_send[:, at] = total[rows:]


def token_grad_kernel(width, info, tokens, g_own, g_peer, out, mark, g):
    mark[...] = jnp.zeros_like(mark)
    rows, model = tokens.shape
    for first, ref in ((0, g_own), (8, g_peer)):
        for j in range(8):
            to = pl.ds(pl.multiple_of(info[first + j], 128), width)
            g[:, to] = ref[:, j * width : (j + 1) * width]
    step = 16
    for i in range(rows // step):
        at = slice(i * step, (i + 1) * step)
        x = tokens[at, :].astype(F32)
        center = x - jnp.sum(x, axis=1, keepdims=True) / model
        scale = lax.rsqrt(jnp.sum(center * center, axis=1, keepdims=True) / model + EPS)
        hat = center * scale
        grad = g[at, :]
        mean_g = jnp.sum(grad, axis=1, keepdims=True) / model
        mean_gh = jnp.sum(grad * hat, axis=1, keepdims=True) / model
        out[at, :] = (scale * (grad - mean_g - hat * mean_gh)).astype(BF16)


def place_kernel(at, blocks, *refs):
    out, rows = refs[-1], blocks.shape[3]
    for h in range(2):
        for n in range(2):
            for side in range(2):
                to = slice((2 * h + side) * rows, (2 * h + side + 1) * rows)
                out[0, to, n * 128 : (n + 1) * 128] = blocks[h, n, side].astype(F32)


def place(at, blocks, dims, before=()):
    return pl.pallas_call(
        place_kernel,
        grid_spec=pltpu.PrefetchScalarGridSpec(
            num_scalar_prefetch=1,
            grid=(4,),
            in_specs=[pl.BlockSpec((2, 2) + blocks.shape[2:], lambda m, at: (0, m, 0, 0, 0))]
            + [pl.BlockSpec(memory_space=pl.ANY) for _ in before],
            out_specs=pl.BlockSpec((1, dims[1] // 2, dims[2]), lambda m, at: (m, at[0], 0)),
        ),
        out_shape=shape(dims, F32),
        input_output_aliases={2: 0} if before else {},
        compiler_params=pltpu.CompilerParams(vmem_limit_bytes=12 * 1024 * 1024),
        cost_estimate=pl.CostEstimate(flops=1, bytes_accessed=8 * math.prod(dims), transcendentals=0),
        name="place",
    )(at, blocks, *before)


def swap_groups(with_x):
    if with_x:
        return [[x * 16 + z * 2 + core for x in range(2) for z in range(NZ)] for core in range(2)]
    return [[x * 16 + z * 2 + core for z in range(NZ)] for x in range(2) for core in range(2)]


def exchange(values, with_x):
    return lax.all_to_all(
        values, "dp", split_axis=0, concat_axis=0, axis_index_groups=swap_groups(with_x), tiled=True
    )


def per_device(tokens, cotangent, lengths, positions, weights):
    rows, model = tokens.shape
    shard_rows, cols = weights.shape[1], weights.shape[2]
    width = shard_rows // 2
    dp, fs = lax.axis_index("dp"), lax.axis_index("fsdp")
    core, x_hi = dp % 2, dp // 16
    y_at, x_lo = fs // 2, fs % 2
    sign = 1 - 2 * core
    offs = []
    for c, s in ((core, sign), (1 - core, -sign)):
        for k, dx in ORDER:
            shard = ((y_at - s * k + 4) % NY) * 2 + (x_lo + dx) % 2
            offs.append(shard * shard_rows + c * width)
    info = jnp.stack(offs + [x_hi * 2 + x_lo, x_lo, core, sign]).astype(jnp.int32)
    half = width // 2

    pair = shape((2, rows, model // 2))
    some = rows // 4
    own, send = call(
        functools.partial(prep_kernel, width),
        [(pair, (2, some, model // 2), lambda i: (0, i, 0))] * 2,
        [info, (tokens, (some, model), lambda i: (i, 0)), (cotangent, (some, model), lambda i: (i, 0))],
        grid=(4,),
        scalars=1,
        scratch=[pltpu.VMEM((some, model), BF16)],
        flops=8 * rows * model,
        nbytes=8 * rows * model,
        name="prep",
    )

    w = {(0, 0): lax.dynamic_slice(weights, (0, core * width, 0), (4, width, cols))}
    w[0, 1] = shift(w[0, 0], dx=1)
    w[3, 0] = shift(w[0, 0], dy=-1)
    w[1, 0] = shift(w[0, 0], dy=1)
    w[2, 0] = shift(w[1, 0], dy=1)
    w[1, 1] = shift(w[1, 0], dx=1)
    w[3, 1] = shift(w[3, 0], dx=1)
    w[2, 1] = shift(w[1, 1], dy=1)
    shards = [w[place] for place in ORDER]

    peer = shift(gate(send, [w[1, 0], w[0, 1]]), dc=1)
    one = (1, rows, model // 2)
    (turned,) = call(
        functools.partial(flip_kernel, width),
        [(shape((2, 4, 2, 4, half // 2, 2 * rows)), (2, 4, 1, 4, half // 2, 2 * rows), lambda i: (0, 0, i, 0, 0, 0))],
        [info, (own, one, lambda i: (i, 0, 0)), (peer, one, lambda i: (i, 0, 0))],
        grid=(2,),
        scalars=1,
        nbytes=8 * rows * model,
        name="flip",
    )

    quarter = HD // 4
    frequency = (ROPE_BASE ** (-np.arange(quarter, dtype=np.float64) / quarter)).astype(np.float32)
    angle_r = positions[0].astype(F32)[:, None] * frequency[None, :]
    angle_c = positions[1].astype(F32)[:, None] * frequency[None, :]
    cos_r, sin_r, cos_c, sin_c = jnp.cos(angle_r), jnp.sin(angle_r), jnp.cos(angle_c), jnp.sin(angle_c)
    cos_t = jnp.concatenate([cos_r, cos_r, cos_c, cos_c], axis=1)
    sin_t = jnp.concatenate([-sin_r, sin_r, -sin_c, sin_c], axis=1)

    lin_shape = shape((rows, 4 * cols), F32)
    lin = []
    for first, pairs in ((0, 3), (3, 1)):
        span = 2 * pairs * width
        columns = functools.partial(lambda c, m: (m // 3, 0, c), first // pairs)
        acc = ((rows, cols), lambda m: (0, m))
        lin = call(
            functools.partial(linear_kernel, pairs),
            [(lin_shape, *acc)] * 2,
            [(own, (1, rows, span), columns), (peer, (1, rows, span), columns)]
            + [(w_j, (1, width, cols), lambda m: (m, 0, 0)) for w_j in shards[2 * first : 2 * (first + pairs)]]
            + [(value, *acc) for value in lin],
            grid=(4,),
            flops=2 * 2 * rows * 2 * pairs * width * 4 * cols,
            nbytes=2 * pairs * width * 8 * cols + 8 * rows * 2 * pairs * width,
            name="linear",
            after=[] if first else [turned, cos_t, sin_t],
        )
    lin_own, lin_send = lin
    lin_peer = shift(lin_send, dc=1)
    (y_own,) = call(
        attend_kernel,
        [shape((rows, 4 * cols))],
        [lengths, lin_own, lin_peer, cos_t, sin_t],
        scalars=1,
        flops=HEADS * 10 * rows * rows * HD * 2,
        nbytes=10 * rows * 4 * cols,
        name="attend",
    )
    y_peer = shift(y_own, dc=1)

    quarter = half // 2
    piece = shape((4, 8, quarter, 128))

    def terms(steps):
        part = len(steps) / 4
        picks = [functools.partial(lambda step, _: (0, step, 0, 0, 0, 0), step) for step in steps]
        return call(
            functools.partial(terms_kernel, len(steps)),
            [piece] * (2 * len(steps)),
            [(turned, (2, 1, 2, 4, quarter, 2 * rows), pick) for pick in picks] + [y_own, y_peer],
            flops=int(part * 2 * 2 * rows * (model // 2) * 4 * cols),
            nbytes=int(part * (4 * model * cols + 8 * rows * model)),
            name="terms",
        )

    far = terms([2])
    far = [along(far[0], first=1), along(far[1], first=-1)]
    back = terms([3])
    back = [along(back[0], first=-1), along(back[1], first=1)]
    near = terms([1, 0])

    per_u = ((1, 8, quarter, 128), lambda u: (u, 0, 0, 0))
    joined = sum_call(
        join_kernel,
        "join",
        [(piece, *per_u)] * 2,
        [(near[0], *per_u), (far[0], *per_u), (near[1], *per_u), (far[1], *per_u)],
        grid=(4,),
    )
    ahead = [along(joined[0], first=1), along(joined[1], first=-1)]

    most = ((3, width, cols), lambda _: (0, 0, 0))
    g_own, g_send = call(
        functools.partial(normed_grad_kernel, width),
        [shape((rows, model // 2), F32)] * 2,
        [y_own, y_peer] + [(w_j, *most) for w_j in shards],
        flops=2 * rows * model * 3 * cols,
        nbytes=4 * model * cols + 4 * rows * model,
        name="normed_grad",
        after=[joined[0]],
    )

    per_n = ((4, 2, quarter, 128), lambda n: (0, n, 0, 0))
    mixed = shape((8, 2, quarter, 128))
    out_n = ((2, 2, quarter, 128), lambda n: (n, 0, 0, 0))
    halfway = sum_call(
        sides_kernel,
        "sides",
        [(mixed, *out_n)] * 4,
        [(value, *per_n) for value in (near[2], back[0], ahead[0], near[3], back[1], ahead[1])],
        grid=(4,),
        after=[g_send],
    )
    g_peer = shift(gate(g_send, [halfway[0]]), dc=1)
    g_rows = ((some, model // 2), lambda i: (i, 0))
    grad_tokens, mark = call(
        functools.partial(token_grad_kernel, width),
        [(shape((rows, model)), (some, model), lambda i: (i, 0)), (shape((8, 128), F32), (8, 128), lambda i: (0, 0))],
        [info, (tokens, (some, model), lambda i: (i, 0)), (g_own, *g_rows), (g_peer, *g_rows)],
        grid=(4,),
        scalars=1,
        scratch=[pltpu.VMEM((some, model), F32)],
        flops=16 * rows * model,
        nbytes=8 * rows * model,
        name="token_grad",
    )

    rest = [along(halfway[d], second=d) for d in range(1, 4)]
    (by_z,) = sum_call(
        seconds_kernel,
        "seconds",
        [(mixed, *out_n)],
        [(value, *out_n) for value in [halfway[0]] + rest],
        grid=(4,),
        after=[mark],
    )
    (spread,) = sum_call(last_kernel, "last", [shape((2 * NZ, 2, quarter, 128))], [exchange(by_z, False)])
    done = exchange(spread, True).reshape(2, NZ, 2, quarter, 128)
    dims = (4, shard_rows, cols)
    weight_grads = place(jnp.stack([core]).astype(jnp.int32), done, dims)
    weight_grads = place(jnp.stack([1 - core]).astype(jnp.int32), shift(done, dc=1), dims, [weight_grads])
    return (grad_tokens, weight_grads)


def solution(mesh):
    return jax.shard_map(
        per_device,
        mesh=mesh,
        in_specs=(
            P(("dp", "fsdp"), None),
            P(("dp", "fsdp"), None),
            P(("dp", "fsdp"), None),
            P(None, ("dp", "fsdp")),
            P(None, "fsdp", None),
        ),
        out_specs=(P(("dp", "fsdp"), None), P(None, "fsdp", None)),
        check_vma=False,
    )
```

```python
import functools
import math

import jax
import jax.numpy as jnp
import numpy as np
from jax import lax
from jax.experimental import pallas as pl
from jax.experimental.pallas import tpu as pltpu
from jax.sharding import PartitionSpec as P

HD = 128
HEADS = 2
ROPE_BASE = 100.0
EPS = 1e-6
NX, NY, NZ = 4, 4, 8
ORDER = [(0, 0), (0, 1), (1, 0), (1, 1), (3, 0), (2, 0), (3, 1), (2, 1)]
X_AT, X_LO, CORE, SIGN = 16, 17, 18, 19
BF16, F32 = jnp.bfloat16, jnp.float32


def flat_index(x, y, z, core):
    return ((x // 2) * 16 + z * 2 + core) * 8 + y * 2 + x % 2


DEVICES = [(x, y, z, core) for x in range(NX) for y in range(NY) for z in range(NZ) for core in range(2)]


def permute(values, target):
    pairs = []
    for x, y, z, core in DEVICES:
        tx, ty, tz, tcore = target(x, y, z, core)
        pairs.append((flat_index(x, y, z, core), flat_index(tx % NX, ty % NY, tz % NZ, tcore)))
    return lax.ppermute(values, ("dp", "fsdp"), pairs)


def shift(values, dx=0, dy=0, dc=0):
    def target(x, y, z, core):
        s = 1 - 2 * core
        return x + s * dx, y + s * dy, z, core ^ dc

    return permute(values, target)


def along(values, first=0, second=0):
    def target(x, y, z, core):
        dx, dy = (second, first) if core == 0 else (first, second)
        return x + dx, y + dy, z, core

    return permute(values, target)


def call(body, outs, operands, grid=(), scalars=0, scratch=(), flops=0, nbytes=0, name=None, after=()):
    count, last = len(operands), len(operands) + len(after)
    held = 0
    arrays, in_specs, out_shapes, out_specs = [], [], [], []
    for k, item in enumerate(list(operands) + list(outs)):
        value, *place = item if isinstance(item, tuple) else (item,)
        if k < scalars:
            spec = pl.BlockSpec(memory_space=pltpu.SMEM)
        elif place:
            spec = pl.BlockSpec(place[0], place[1])
            held += 2 * math.prod(place[0]) * value.dtype.itemsize
        else:
            spec = pl.BlockSpec(memory_space=pltpu.VMEM)
            held += math.prod(value.shape) * value.dtype.itemsize
        (arrays if k < count else out_shapes).append(value)
        (in_specs if k < count else out_specs).append(spec)
    held += sum(math.prod(ref.shape) * ref.dtype.itemsize for ref in scratch)
    in_specs += [pl.BlockSpec(memory_space=pl.ANY) for _ in after]
    kernel = (lambda *refs: body(*refs[:count], *refs[last:])) if after else body
    return pl.pallas_call(
        kernel,
        grid=grid or (1,),
        out_shape=out_shapes,
        in_specs=in_specs,
        out_specs=out_specs,
        scratch_shapes=list(scratch),
        compiler_params=pltpu.CompilerParams(vmem_limit_bytes=held + 8 * 1024 * 1024),
        cost_estimate=pl.CostEstimate(flops=flops, bytes_accessed=nbytes, transcendentals=0),
        name=name,
    )(*arrays, *after)


def gate(value, after):
    return pl.pallas_call(
        lambda *refs: None,
        out_shape=shape(value.shape, value.dtype),
        in_specs=[pl.BlockSpec(memory_space=pl.ANY)] * (1 + len(after)),
        out_specs=pl.BlockSpec(memory_space=pl.ANY),
        input_output_aliases={0: 0},
        cost_estimate=pl.CostEstimate(flops=1, bytes_accessed=1, transcendentals=0),
        name="gate",
    )(value, *after)


def shape(dims, dtype=BF16):
    return jax.ShapeDtypeStruct(dims, dtype)


def prep_kernel(width, info, tokens, cot, own, send, normed):
    rows, model = tokens.shape
    step = 16
    for i in range(rows // step):
        at = slice(i * step, (i + 1) * step)
        x = tokens[at, :].astype(F32)
        center = x - jnp.sum(x, axis=1, keepdims=True) / model
        var = jnp.sum(center * center, axis=1, keepdims=True) / model
        normed[at, :] = (center * lax.rsqrt(var + EPS)).astype(BF16)
    for j in range(8):
        to = slice(j * width, (j + 1) * width)
        for out, first in ((own, 0), (send, 8)):
            cols = pl.ds(pl.multiple_of(info[first + j], 128), width)
            out[0, :, to] = normed[:, cols]
            out[1, :, to] = cot[:, cols]


def flip_kernel(width, info, own, peer, out):
    half = width // 2
    quarter = half // 2
    core, sign, x_at = info[CORE], info[SIGN], info[X_AT]
    for j, (k, dx) in enumerate(ORDER):
        at = slice(j * width, (j + 1) * width)
        y_steps = lax.rem(4 - sign * k, 4)
        turned = jnp.concatenate([own[0, :, at], peer[0, :, at]], axis=0).T
        for x_hi in range(2):
            x_to = 2 * x_hi + lax.rem(info[X_LO] + dx, 2)
            x_steps = lax.rem(x_to - x_at + 4, 4)
            first = jnp.where(core == 0, y_steps, x_steps)
            second = jnp.where(core == 0, x_steps, y_steps)
            for side in range(2):
                steps = first if side == 0 else lax.rem(4 - first, 4)
                start = x_hi * half + side * quarter
                out[side, steps, 0, second] = turned[start : start + quarter]


def linear_kernel(counts, own, peer, *refs):
    pairs, shards, start = len(counts) // 2, [], 0
    for count in counts:
        got = refs[start : start + count]
        start += count
        shards.append(got[0][...] if count == 1 else jnp.where(pl.program_id(0) < 2, got[0][...], got[1][...]))
    before, outs = refs[start:-2], refs[-2:]
    depth = own.shape[2] // pairs
    rights = [jnp.concatenate([shards[2 * p][0], shards[2 * p + 1][0]], axis=0) for p in range(pairs)]
    for side, left in enumerate((own, peer)):
        total = before[side][...] if before else None
        for p, right in enumerate(rights):
            term = jnp.dot(left[0, :, p * depth : (p + 1) * depth], right, preferred_element_type=F32)
            total = term if total is None else total + term
        outs[side][...] = total


def swap_quarters(x):
    lane = lax.broadcasted_iota(jnp.int32, x.shape, 1)
    quarter = HD // 4
    up = pltpu.roll(x, HD - quarter, 1)
    down = pltpu.roll(x, quarter, 1)
    return jnp.where(lane % (2 * quarter) < quarter, up, down)


def mean_of(x):
    return jnp.sum(x, axis=1, keepdims=True) * (1.0 / HD)


def norm_rows(x):
    center = x - mean_of(x)
    scale = lax.rsqrt(mean_of(center * center) + EPS)
    return center * scale, scale


def norm_rows_back(g, hat, scale):
    return scale * (g - mean_of(g) - hat * mean_of(g * hat))


def dot_t(a, b, dims):
    return lax.dot_general(a, b, ((dims[0], dims[1]), ((), ())), preferred_element_type=F32)


def attend_kernel(lengths, mine, theirs, cos_t, sin_t, out):
    rows = mine.shape[0]
    cols = HEADS * HD
    row_id = lax.broadcasted_iota(jnp.int32, (rows, 1), 0)
    col_id = lax.broadcasted_iota(jnp.int32, (1, rows), 1)

    def slot(ids):
        count, end = jnp.zeros(ids.shape, jnp.int32), 0
        for k in range(3):
            end = end + lengths[0, k]
            count = count + (ids >= end).astype(jnp.int32)
        return count

    row_slot, col_slot = slot(row_id), slot(col_id)
    same = row_slot == col_slot
    live = row_slot < 3
    cosine, sine = cos_t[...], sin_t[...]
    score_scale = 1.0 / math.sqrt(HD)
    for h in range(HEADS):

        def part(m):
            at = slice(m * cols + h * HD, m * cols + (h + 1) * HD)
            return mine[:, at] + theirs[:, at]

        q_hat, q_scale = norm_rows(part(0))
        k_hat, k_scale = norm_rows(part(1))
        q = (q_hat * cosine + swap_quarters(q_hat) * sine).astype(BF16)
        k = (k_hat * cosine + swap_quarters(k_hat) * sine).astype(BF16)
        v = part(2).astype(BF16)
        ga = jnp.where(live, part(3), 0.0).astype(BF16)
        scores = dot_t(q, k, ((1,), (1,))) * score_scale
        e = jnp.where(same, jnp.exp(scores), 0.0)
        p32 = e / jnp.sum(e, axis=1, keepdims=True)
        p = p32.astype(BF16)
        att = jnp.dot(p, v, preferred_element_type=F32).astype(BF16)
        gv = dot_t(p, ga, ((0,), (0,)))
        gp = dot_t(ga, v, ((1,), (1,))).astype(BF16).astype(F32)
        gs = p32 * (gp - jnp.sum(gp * p32, axis=1, keepdims=True)) * score_scale
        gs = gs.astype(BF16)
        gq = jnp.dot(gs, k, preferred_element_type=F32).astype(BF16).astype(F32)
        gk = dot_t(gs, q, ((0,), (0,))).astype(BF16).astype(F32)
        gq = norm_rows_back(gq * cosine + swap_quarters(gq * sine), q_hat, q_scale)
        gk = norm_rows_back(gk * cosine + swap_quarters(gk * sine), k_hat, k_scale)
        at = lambda m: slice(m * cols + h * HD, m * cols + (h + 1) * HD)
        out[:, at(0)] = gq.astype(BF16)
        out[:, at(1)] = gk.astype(BF16)
        out[:, at(2)] = gv.astype(BF16)
        out[:, at(3)] = jnp.where(live, att.astype(F32), 0.0).astype(BF16)


def terms_kernel(count, *refs):
    turned, (y_own, y_peer), outs = refs[:count], refs[count : count + 2], refs[count + 2 :]
    rows, depth = turned[0].shape[4:]
    y_all = jnp.concatenate([y_own[...], y_peer[...]], axis=0)
    proj = 3 * HEADS * HD
    for k, ref in enumerate(turned):
        for side in range(2):
            for i, right in ((0, y_all[:, :proj]), (1, y_all[:, proj:])):
                left = ref[side, 0, i].reshape(4 * rows, depth)
                value = jnp.dot(left, right, preferred_element_type=F32).astype(BF16)
                for n in range(right.shape[1] // 128):
                    for u in range(4):
                        block = value[u * rows : (u + 1) * rows, n * 128 : (n + 1) * 128]
                        outs[2 * k + side][u, 6 * i + n] = block


def add_up(refs, at):
    total = refs[0][at].astype(F32)
    for ref in refs[1:]:
        total = total + ref[at].astype(F32)
    return total.astype(BF16)


def join_kernel(near_0, far_0, near_1, far_1, out_0, out_1):
    for n in range(8):
        out_0[0, n] = add_up((near_0, far_0), (0, n))
        out_1[0, n] = add_up((near_1, far_1), (0, n))


def sides_kernel(*refs):
    for side in range(2):
        for u, out in enumerate(refs[6:]):
            for n in range(out.shape[0]):
                out[n, side] = add_up(refs[3 * side : 3 * side + 3], (u, n))


def seconds_kernel(*refs):
    for n in range(refs[0].shape[0]):
        for side in range(2):
            refs[-1][n, side] = add_up(refs[:-1], (n, side))


def last_kernel(got, out):
    for side in range(2):
        total = got[0, side].astype(F32)
        for k in range(1, 8):
            total = total + got[k, side].astype(F32)
        for k in range(out.shape[0]):
            out[k, side] = total.astype(BF16)


def sum_call(body, name, outs, operands, grid=(), after=()):
    value = operands[0][0] if isinstance(operands[0], tuple) else operands[0]
    size = math.prod(value.shape)
    return call(
        body,
        outs,
        operands,
        grid=grid,
        flops=len(operands) * size,
        nbytes=2 * size * (len(operands) + 2),
        name=name,
        after=after,
    )


def normed_grad_kernel(width, counts, y_own, y_peer, *refs):
    shards, start, (g_own, g_send) = [], 0, refs[-2:]
    for count in counts:
        shards.append([ref[m] for ref in refs[start : start + count] for m in range(ref.shape[0])])
        start += count
    rows = y_own.shape[0]
    proj = 3 * HEADS * HD
    left = jnp.concatenate([y_own[:, :proj], y_peer[:, :proj]], axis=0)
    for j in range(8):
        right = jnp.concatenate(shards[j], axis=1)
        total = dot_t(left, right, ((1,), (1,)))
        at = slice(j * width, (j + 1) * width)
        g_own[:, at] = total[:rows]
        g_send[:, at] = total[rows:].astype(BF16)


def token_grad_kernel(width, info, tokens, g_own, g_peer, out, mark, g):
    mark[...] = jnp.zeros_like(mark)
    rows, model = tokens.shape
    for first, ref in ((0, g_own), (8, g_peer)):
        for j in range(8):
            to = pl.ds(pl.multiple_of(info[first + j], 128), width)
            g[:, to] = ref[:, j * width : (j + 1) * width].astype(F32)
    step = 16
    for i in range(rows // step):
        at = slice(i * step, (i + 1) * step)
        x = tokens[at, :].astype(F32)
        center = x - jnp.sum(x, axis=1, keepdims=True) / model
        scale = lax.rsqrt(jnp.sum(center * center, axis=1, keepdims=True) / model + EPS)
        hat = center * scale
        grad = g[at, :]
        mean_g = jnp.sum(grad, axis=1, keepdims=True) / model
        mean_gh = jnp.sum(grad * hat, axis=1, keepdims=True) / model
        out[at, :] = (scale * (grad - mean_g - hat * mean_gh)).astype(BF16)


def place_kernel(at, blocks, *refs):
    out, rows = refs[-1], blocks.shape[3]
    for h in range(2):
        for n in range(2):
            for side in range(2):
                to = slice((2 * h + side) * rows, (2 * h + side + 1) * rows)
                out[0, to, n * 128 : (n + 1) * 128] = blocks[h, n, side].astype(F32)


def place(at, blocks, dims, before=()):
    return pl.pallas_call(
        place_kernel,
        grid_spec=pltpu.PrefetchScalarGridSpec(
            num_scalar_prefetch=1,
            grid=(4,),
            in_specs=[pl.BlockSpec((2, 2) + blocks.shape[2:], lambda m, at: (0, m, 0, 0, 0))]
            + [pl.BlockSpec(memory_space=pl.ANY) for _ in before],
            out_specs=pl.BlockSpec((1, dims[1] // 2, dims[2]), lambda m, at: (m, at[0], 0)),
        ),
        out_shape=shape(dims, F32),
        input_output_aliases={2: 0} if before else {},
        compiler_params=pltpu.CompilerParams(vmem_limit_bytes=12 * 1024 * 1024),
        cost_estimate=pl.CostEstimate(flops=1, bytes_accessed=8 * math.prod(dims), transcendentals=0),
        name="place",
    )(at, blocks, *before)


def swap_groups(with_x):
    if with_x:
        return [[x * 16 + z * 2 + core for x in range(2) for z in range(NZ)] for core in range(2)]
    return [[x * 16 + z * 2 + core for z in range(NZ)] for x in range(2) for core in range(2)]


def exchange(values, with_x):
    return lax.all_to_all(
        values, "dp", split_axis=0, concat_axis=0, axis_index_groups=swap_groups(with_x), tiled=True
    )


def per_device(tokens, cotangent, lengths, positions, weights):
    rows, model = tokens.shape
    shard_rows, cols = weights.shape[1], weights.shape[2]
    width = shard_rows // 2
    dp, fs = lax.axis_index("dp"), lax.axis_index("fsdp")
    core, x_hi = dp % 2, dp // 16
    y_at, x_lo = fs // 2, fs % 2
    sign = 1 - 2 * core
    offs = []
    for c, s in ((core, sign), (1 - core, -sign)):
        for k, dx in ORDER:
            shard = ((y_at - s * k + 4) % NY) * 2 + (x_lo + dx) % 2
            offs.append(shard * shard_rows + c * width)
    info = jnp.stack(offs + [x_hi * 2 + x_lo, x_lo, core, sign]).astype(jnp.int32)
    half = width // 2

    pair = shape((2, rows, model // 2))
    some = rows // 4
    own, send = call(
        functools.partial(prep_kernel, width),
        [(pair, (2, some, model // 2), lambda i: (0, i, 0))] * 2,
        [info, (tokens, (some, model), lambda i: (i, 0)), (cotangent, (some, model), lambda i: (i, 0))],
        grid=(4,),
        scalars=1,
        scratch=[pltpu.VMEM((some, model), BF16)],
        flops=8 * rows * model,
        nbytes=8 * rows * model,
        name="prep",
    )

    w = {(0, 0): lax.dynamic_slice(weights, (0, core * width, 0), (4, width, cols))}
    w[0, 1] = shift(w[0, 0], dx=1)
    parts = [lax.dynamic_slice(weights, (m, core * width, 0), (2, width, cols)) for m in (0, 2)]
    w[3, 0] = [shift(part, dy=-1) for part in parts]
    w[1, 0] = shift(w[0, 0], dy=1)
    w[2, 0] = shift(w[1, 0], dy=1)
    w[1, 1] = shift(w[1, 0], dx=1)
    w[3, 1] = [shift(part, dx=1) for part in w[3, 0]]
    w[2, 1] = shift(w[1, 1], dy=1)
    shards = [w[place] for place in ORDER]

    peer = shift(gate(send, [w[1, 0], w[0, 1], w[3, 0][0]]), dc=1)
    one = (1, rows, model // 2)
    (turned,) = call(
        functools.partial(flip_kernel, width),
        [(shape((2, 4, 2, 4, half // 2, 2 * rows)), (2, 4, 1, 4, half // 2, 2 * rows), lambda i: (0, 0, i, 0, 0, 0))],
        [info, (own, one, lambda i: (i, 0, 0)), (peer, one, lambda i: (i, 0, 0))],
        grid=(2,),
        scalars=1,
        nbytes=8 * rows * model,
        name="flip",
    )

    quarter = HD // 4
    frequency = (ROPE_BASE ** (-np.arange(quarter, dtype=np.float64) / quarter)).astype(np.float32)
    angle_r = positions[0].astype(F32)[:, None] * frequency[None, :]
    angle_c = positions[1].astype(F32)[:, None] * frequency[None, :]
    cos_r, sin_r, cos_c, sin_c = jnp.cos(angle_r), jnp.sin(angle_r), jnp.cos(angle_c), jnp.sin(angle_c)
    cos_t = jnp.concatenate([cos_r, cos_r, cos_c, cos_c], axis=1)
    sin_t = jnp.concatenate([-sin_r, sin_r, -sin_c, sin_c], axis=1)

    lin_shape = shape((rows, 4 * cols), F32)
    one_matrix = (1, width, cols)

    def by_matrix(w_j):
        if not isinstance(w_j, list):
            return [(w_j, one_matrix, lambda m: (m, 0, 0))]
        return [
            (w_j[0], one_matrix, lambda m: (jnp.minimum(m, 1), 0, 0)),
            (w_j[1], one_matrix, lambda m: (jnp.maximum(m - 2, 0), 0, 0)),
        ]

    lin = []
    for first, pairs in ((0, 3), (3, 1)):
        span = 2 * pairs * width
        group = shards[2 * first : 2 * (first + pairs)]
        columns = functools.partial(lambda c, m: (m // 3, 0, c), first // pairs)
        acc = ((rows, cols), lambda m: (0, m))
        lin = call(
            functools.partial(linear_kernel, [len(w_j) if isinstance(w_j, list) else 1 for w_j in group]),
            [(lin_shape, *acc)] * 2,
            [(own, (1, rows, span), columns), (peer, (1, rows, span), columns)]
            + [item for w_j in group for item in by_matrix(w_j)]
            + [(value, *acc) for value in lin],
            grid=(4,),
            flops=2 * 2 * rows * 2 * pairs * width * 4 * cols,
            nbytes=2 * pairs * width * 8 * cols + 8 * rows * 2 * pairs * width,
            name="linear",
            after=[] if first else [turned, cos_t, sin_t],
        )
    lin_own, lin_send = lin
    lin_peer = shift(lin_send, dc=1)
    (y_own,) = call(
        attend_kernel,
        [shape((rows, 4 * cols))],
        [lengths, lin_own, lin_peer, cos_t, sin_t],
        scalars=1,
        flops=HEADS * 10 * rows * rows * HD * 2,
        nbytes=10 * rows * 4 * cols,
        name="attend",
    )
    y_peer = shift(y_own, dc=1)

    quarter = half // 2
    piece = shape((4, 8, quarter, 128))

    def terms(steps):
        part = len(steps) / 4
        picks = [functools.partial(lambda step, _: (0, step, 0, 0, 0, 0), step) for step in steps]
        return call(
            functools.partial(terms_kernel, len(steps)),
            [piece] * (2 * len(steps)),
            [(turned, (2, 1, 2, 4, quarter, 2 * rows), pick) for pick in picks] + [y_own, y_peer],
            flops=int(part * 2 * 2 * rows * (model // 2) * 4 * cols),
            nbytes=int(part * (4 * model * cols + 8 * rows * model)),
            name="terms",
        )

    far = terms([2])
    far = [along(far[0], first=1), along(far[1], first=-1)]
    back = terms([3])
    back = [along(back[0], first=-1), along(back[1], first=1)]
    near = terms([1, 0])

    per_u = ((1, 8, quarter, 128), lambda u: (u, 0, 0, 0))
    joined = sum_call(
        join_kernel,
        "join",
        [(piece, *per_u)] * 2,
        [(near[0], *per_u), (far[0], *per_u), (near[1], *per_u), (far[1], *per_u)],
        grid=(4,),
    )
    ahead = [along(joined[0], first=1), along(joined[1], first=-1)]

    def first_three(w_j):
        if not isinstance(w_j, list):
            return [(w_j, (3, width, cols), lambda _: (0, 0, 0))]
        return [w_j[0], (w_j[1], one_matrix, lambda _: (0, 0, 0))]

    g_own, g_send = call(
        functools.partial(normed_grad_kernel, width, [len(first_three(w_j)) for w_j in shards]),
        [shape((rows, model // 2), F32), shape((rows, model // 2))],
        [y_own, y_peer] + [item for w_j in shards for item in first_three(w_j)],
        flops=2 * rows * model * 3 * cols,
        nbytes=4 * model * cols + 4 * rows * model,
        name="normed_grad",
        after=[joined[0]],
    )

    per_n = ((4, 2, quarter, 128), lambda n: (0, n, 0, 0))
    mixed = shape((8, 2, quarter, 128))
    out_n = ((2, 2, quarter, 128), lambda n: (n, 0, 0, 0))
    halfway = sum_call(
        sides_kernel,
        "sides",
        [(mixed, *out_n)] * 4,
        [(value, *per_n) for value in (near[2], back[0], ahead[0], near[3], back[1], ahead[1])],
        grid=(4,),
        after=[g_send],
    )
    g_peer = shift(gate(g_send, [halfway[0]]), dc=1)
    g_rows = ((some, model // 2), lambda i: (i, 0))
    grad_tokens, mark = call(
        functools.partial(token_grad_kernel, width),
        [(shape((rows, model)), (some, model), lambda i: (i, 0)), (shape((8, 128), F32), (8, 128), lambda i: (0, 0))],
        [info, (tokens, (some, model), lambda i: (i, 0)), (g_own, *g_rows), (g_peer, *g_rows)],
        grid=(4,),
        scalars=1,
        scratch=[pltpu.VMEM((some, model), F32)],
        flops=16 * rows * model,
        nbytes=8 * rows * model,
        name="token_grad",
    )

    rest = [along(halfway[d], second=d) for d in range(1, 4)]
    (by_z,) = sum_call(
        seconds_kernel,
        "seconds",
        [(mixed, *out_n)],
        [(value, *out_n) for value in [halfway[0]] + rest],
        grid=(4,),
        after=[mark],
    )
    (spread,) = sum_call(last_kernel, "last", [shape((2 * NZ, 2, quarter, 128))], [exchange(by_z, False)])
    done = exchange(spread, True).reshape(2, NZ, 2, quarter, 128)
    dims = (4, shard_rows, cols)
    weight_grads = place(jnp.stack([core]).astype(jnp.int32), done, dims)
    weight_grads = place(jnp.stack([1 - core]).astype(jnp.int32), shift(done, dc=1), dims, [weight_grads])
    return (grad_tokens, weight_grads)


def solution(mesh):
    return jax.shard_map(
        per_device,
        mesh=mesh,
        in_specs=(
            P(("dp", "fsdp"), None),
            P(("dp", "fsdp"), None),
            P(("dp", "fsdp"), None),
            P(None, ("dp", "fsdp")),
            P(None, "fsdp", None),
        ),
        out_specs=(P(("dp", "fsdp"), None), P(None, "fsdp", None)),
        check_vma=False,
    )
```

```python
import functools
import math

import jax
import jax.numpy as jnp
import numpy as np
from jax import lax
from jax.experimental import pallas as pl
from jax.experimental.pallas import tpu as pltpu
from jax.sharding import PartitionSpec as P

HD = 128
HEADS = 2
ROPE_BASE = 100.0
EPS = 1e-6
NX, NY, NZ = 4, 4, 8
ORDER = [(0, 0), (0, 1), (1, 0), (1, 1), (3, 0), (2, 0), (3, 1), (2, 1)]
X_AT, X_LO, CORE, SIGN = 16, 17, 18, 19
BF16, F32 = jnp.bfloat16, jnp.float32


def flat_index(x, y, z, core):
    return ((x // 2) * 16 + z * 2 + core) * 8 + y * 2 + x % 2


DEVICES = [(x, y, z, core) for x in range(NX) for y in range(NY) for z in range(NZ) for core in range(2)]


def permute(values, target):
    pairs = []
    for x, y, z, core in DEVICES:
        tx, ty, tz, tcore = target(x, y, z, core)
        pairs.append((flat_index(x, y, z, core), flat_index(tx % NX, ty % NY, tz % NZ, tcore)))
    return lax.ppermute(values, ("dp", "fsdp"), pairs)


def shift(values, dx=0, dy=0, dc=0):
    def target(x, y, z, core):
        s = 1 - 2 * core
        return x + s * dx, y + s * dy, z, core ^ dc

    return permute(values, target)


def along(values, first=0, second=0):
    def target(x, y, z, core):
        dx, dy = (second, first) if core == 0 else (first, second)
        return x + dx, y + dy, z, core

    return permute(values, target)


def call(body, outs, operands, grid=(), scalars=0, scratch=(), flops=0, nbytes=0, name=None, after=()):
    count, last = len(operands), len(operands) + len(after)
    held = 0
    arrays, in_specs, out_shapes, out_specs = [], [], [], []
    for k, item in enumerate(list(operands) + list(outs)):
        value, *place = item if isinstance(item, tuple) else (item,)
        if k < scalars:
            spec = pl.BlockSpec(memory_space=pltpu.SMEM)
        elif place:
            spec = pl.BlockSpec(place[0], place[1])
            held += 2 * math.prod(place[0]) * value.dtype.itemsize
        else:
            spec = pl.BlockSpec(memory_space=pltpu.VMEM)
            held += math.prod(value.shape) * value.dtype.itemsize
        (arrays if k < count else out_shapes).append(value)
        (in_specs if k < count else out_specs).append(spec)
    held += sum(math.prod(ref.shape) * ref.dtype.itemsize for ref in scratch)
    in_specs += [pl.BlockSpec(memory_space=pl.ANY) for _ in after]
    kernel = (lambda *refs: body(*refs[:count], *refs[last:])) if after else body
    return pl.pallas_call(
        kernel,
        grid=grid or (1,),
        out_shape=out_shapes,
        in_specs=in_specs,
        out_specs=out_specs,
        scratch_shapes=list(scratch),
        compiler_params=pltpu.CompilerParams(vmem_limit_bytes=held + 8 * 1024 * 1024),
        cost_estimate=pl.CostEstimate(flops=flops, bytes_accessed=nbytes, transcendentals=0),
        name=name,
    )(*arrays, *after)


def gate(value, after):
    return pl.pallas_call(
        lambda *refs: None,
        out_shape=shape(value.shape, value.dtype),
        in_specs=[pl.BlockSpec(memory_space=pl.ANY)] * (1 + len(after)),
        out_specs=pl.BlockSpec(memory_space=pl.ANY),
        input_output_aliases={0: 0},
        cost_estimate=pl.CostEstimate(flops=1, bytes_accessed=1, transcendentals=0),
        name="gate",
    )(value, *after)


def shape(dims, dtype=BF16):
    return jax.ShapeDtypeStruct(dims, dtype)


def half_kernel(weights, whole, *rest):
    parts, sems = rest[:2], rest[2]
    width = whole.shape[1]
    rows = pl.ds(pl.multiple_of(lax.axis_index("dp") % 2 * width, width), width)
    copies = [pltpu.make_async_copy(weights.at[:, rows], whole, sems.at[0])]
    for k, part in enumerate(parts):
        copies.append(pltpu.make_async_copy(weights.at[pl.ds(2 * k, 2), rows], part, sems.at[1 + k]))
    for copy in copies:
        copy.start()
    for copy in copies:
        copy.wait()


def half_of(weights):
    _, rows, cols = weights.shape
    return pl.pallas_call(
        half_kernel,
        out_shape=[shape((count, rows // 2, cols)) for count in (4, 2, 2)],
        in_specs=[pl.BlockSpec(memory_space=pl.ANY)],
        out_specs=[pl.BlockSpec(memory_space=pl.ANY)] * 3,
        scratch_shapes=[pltpu.SemaphoreType.DMA((3,))],
        compiler_params=pltpu.CompilerParams(vmem_limit_bytes=56 * 1024 * 1024),
        cost_estimate=pl.CostEstimate(flops=1, bytes_accessed=1, transcendentals=0),
        name="half",
    )(weights)


def prep_kernel(width, info, tokens, cot, own, send, normed):
    rows, model = tokens.shape
    step = 16
    for i in range(rows // step):
        at = slice(i * step, (i + 1) * step)
        x = tokens[at, :].astype(F32)
        center = x - jnp.sum(x, axis=1, keepdims=True) / model
        var = jnp.sum(center * center, axis=1, keepdims=True) / model
        normed[at, :] = (center * lax.rsqrt(var + EPS)).astype(BF16)
    for j in range(8):
        to = slice(j * width, (j + 1) * width)
        for out, first in ((own, 0), (send, 8)):
            cols = pl.ds(pl.multiple_of(info[first + j], 128), width)
            out[0, :, to] = normed[:, cols]
            out[1, :, to] = cot[:, cols]


def flip_kernel(width, info, own, peer, out):
    half = width // 2
    quarter = half // 2
    core, sign, x_at = info[CORE], info[SIGN], info[X_AT]
    for j, (k, dx) in enumerate(ORDER):
        at = slice(j * width, (j + 1) * width)
        y_steps = lax.rem(4 - sign * k, 4)
        turned = jnp.concatenate([own[0, :, at], peer[0, :, at]], axis=0).T
        for x_hi in range(2):
            x_to = 2 * x_hi + lax.rem(info[X_LO] + dx, 2)
            x_steps = lax.rem(x_to - x_at + 4, 4)
            first = jnp.where(core == 0, y_steps, x_steps)
            second = jnp.where(core == 0, x_steps, y_steps)
            for side in range(2):
                steps = first if side == 0 else lax.rem(4 - first, 4)
                start = x_hi * half + side * quarter
                out[side, steps, 0, second] = turned[start : start + quarter]


def linear_kernel(counts, own, peer, *refs):
    pairs, shards, start = len(counts) // 2, [], 0
    for count in counts:
        got = refs[start : start + count]
        start += count
        shards.append(got[0][...] if count == 1 else jnp.where(pl.program_id(0) < 2, got[0][...], got[1][...]))
    before, outs = refs[start:-2], refs[-2:]
    depth = own.shape[2] // pairs
    rights = [jnp.concatenate([shards[2 * p][0], shards[2 * p + 1][0]], axis=0) for p in range(pairs)]
    for side, left in enumerate((own, peer)):
        total = before[side][...] if before else None
        for p, right in enumerate(rights):
            term = jnp.dot(left[0, :, p * depth : (p + 1) * depth], right, preferred_element_type=F32)
            total = term if total is None else total + term
        outs[side][...] = total


def swap_quarters(x):
    lane = lax.broadcasted_iota(jnp.int32, x.shape, 1)
    quarter = HD // 4
    up = pltpu.roll(x, HD - quarter, 1)
    down = pltpu.roll(x, quarter, 1)
    return jnp.where(lane % (2 * quarter) < quarter, up, down)


def mean_of(x):
    return jnp.sum(x, axis=1, keepdims=True) * (1.0 / HD)


def norm_rows(x):
    center = x - mean_of(x)
    scale = lax.rsqrt(mean_of(center * center) + EPS)
    return center * scale, scale


def norm_rows_back(g, hat, scale):
    return scale * (g - mean_of(g) - hat * mean_of(g * hat))


def dot_t(a, b, dims):
    return lax.dot_general(a, b, ((dims[0], dims[1]), ((), ())), preferred_element_type=F32)


def attend_kernel(lengths, mine, theirs, cos_t, sin_t, out):
    rows = mine.shape[0]
    cols = HEADS * HD
    row_id = lax.broadcasted_iota(jnp.int32, (rows, 1), 0)
    col_id = lax.broadcasted_iota(jnp.int32, (1, rows), 1)

    def slot(ids):
        count, end = jnp.zeros(ids.shape, jnp.int32), 0
        for k in range(3):
            end = end + lengths[0, k]
            count = count + (ids >= end).astype(jnp.int32)
        return count

    row_slot, col_slot = slot(row_id), slot(col_id)
    same = row_slot == col_slot
    live = row_slot < 3
    cosine, sine = cos_t[...], sin_t[...]
    score_scale = 1.0 / math.sqrt(HD)
    for h in range(HEADS):

        def part(m):
            at = slice(m * cols + h * HD, m * cols + (h + 1) * HD)
            return mine[:, at] + theirs[:, at]

        q_hat, q_scale = norm_rows(part(0))
        k_hat, k_scale = norm_rows(part(1))
        q = (q_hat * cosine + swap_quarters(q_hat) * sine).astype(BF16)
        k = (k_hat * cosine + swap_quarters(k_hat) * sine).astype(BF16)
        v = part(2).astype(BF16)
        ga = jnp.where(live, part(3), 0.0).astype(BF16)
        scores = dot_t(q, k, ((1,), (1,))) * score_scale
        e = jnp.where(same, jnp.exp(scores), 0.0)
        p32 = e / jnp.sum(e, axis=1, keepdims=True)
        p = p32.astype(BF16)
        att = jnp.dot(p, v, preferred_element_type=F32).astype(BF16)
        gv = dot_t(p, ga, ((0,), (0,)))
        gp = dot_t(ga, v, ((1,), (1,))).astype(BF16).astype(F32)
        gs = p32 * (gp - jnp.sum(gp * p32, axis=1, keepdims=True)) * score_scale
        gs = gs.astype(BF16)
        gq = jnp.dot(gs, k, preferred_element_type=F32).astype(BF16).astype(F32)
        gk = dot_t(gs, q, ((0,), (0,))).astype(BF16).astype(F32)
        gq = norm_rows_back(gq * cosine + swap_quarters(gq * sine), q_hat, q_scale)
        gk = norm_rows_back(gk * cosine + swap_quarters(gk * sine), k_hat, k_scale)
        at = lambda m: slice(m * cols + h * HD, m * cols + (h + 1) * HD)
        out[:, at(0)] = gq.astype(BF16)
        out[:, at(1)] = gk.astype(BF16)
        out[:, at(2)] = gv.astype(BF16)
        out[:, at(3)] = jnp.where(live, att.astype(F32), 0.0).astype(BF16)


def terms_kernel(count, *refs):
    turned, (y_own, y_peer), outs = refs[:count], refs[count : count + 2], refs[count + 2 :]
    rows, depth = turned[0].shape[4:]
    y_all = jnp.concatenate([y_own[...], y_peer[...]], axis=0)
    proj = 3 * HEADS * HD
    for k, ref in enumerate(turned):
        for side in range(2):
            for i, right in ((0, y_all[:, :proj]), (1, y_all[:, proj:])):
                left = ref[side, 0, i].reshape(4 * rows, depth)
                value = jnp.dot(left, right, preferred_element_type=F32).astype(BF16)
                for n in range(right.shape[1] // 128):
                    for u in range(4):
                        block = value[u * rows : (u + 1) * rows, n * 128 : (n + 1) * 128]
                        outs[2 * k + side][u, 6 * i + n] = block


def add_up(refs, at):
    total = refs[0][at].astype(F32)
    for ref in refs[1:]:
        total = total + ref[at].astype(F32)
    return total.astype(BF16)


def join_kernel(near_0, far_0, near_1, far_1, out_0, out_1):
    for n in range(8):
        out_0[0, n] = add_up((near_0, far_0), (0, n))
        out_1[0, n] = add_up((near_1, far_1), (0, n))


def sides_kernel(*refs):
    for side in range(2):
        for u, out in enumerate(refs[6:]):
            for n in range(out.shape[0]):
                out[n, side] = add_up(refs[3 * side : 3 * side + 3], (u, n))


def seconds_kernel(*refs):
    for n in range(refs[0].shape[0]):
        for side in range(2):
            refs[-1][n, side] = add_up(refs[:-1], (n, side))


def last_kernel(got, out):
    for side in range(2):
        total = got[0, side].astype(F32)
        for k in range(1, 8):
            total = total + got[k, side].astype(F32)
        for k in range(out.shape[0]):
            out[k, side] = total.astype(BF16)


def sum_call(body, name, outs, operands, grid=(), after=()):
    value = operands[0][0] if isinstance(operands[0], tuple) else operands[0]
    size = math.prod(value.shape)
    return call(
        body,
        outs,
        operands,
        grid=grid,
        flops=len(operands) * size,
        nbytes=2 * size * (len(operands) + 2),
        name=name,
        after=after,
    )


def normed_grad_kernel(width, counts, y_own, y_peer, *refs):
    shards, start, (g_own, g_send) = [], 0, refs[-2:]
    for count in counts:
        shards.append([ref[m] for ref in refs[start : start + count] for m in range(ref.shape[0])])
        start += count
    rows = y_own.shape[0]
    proj = 3 * HEADS * HD
    left = jnp.concatenate([y_own[:, :proj], y_peer[:, :proj]], axis=0)
    for j in range(8):
        right = jnp.concatenate(shards[j], axis=1)
        total = dot_t(left, right, ((1,), (1,)))
        at = slice(j * width, (j + 1) * width)
        g_own[:, at] = total[:rows]
        g_send[:, at] = total[rows:].astype(BF16)


def token_grad_kernel(width, info, tokens, g_own, g_peer, out, mark, g):
    mark[...] = jnp.zeros_like(mark)
    rows, model = tokens.shape
    for first, ref in ((0, g_own), (8, g_peer)):
        for j in range(8):
            to = pl.ds(pl.multiple_of(info[first + j], 128), width)
            g[:, to] = ref[:, j * width : (j + 1) * width].astype(F32)
    step = 16
    for i in range(rows // step):
        at = slice(i * step, (i + 1) * step)
        x = tokens[at, :].astype(F32)
        center = x - jnp.sum(x, axis=1, keepdims=True) / model
        scale = lax.rsqrt(jnp.sum(center * center, axis=1, keepdims=True) / model + EPS)
        hat = center * scale
        grad = g[at, :]
        mean_g = jnp.sum(grad, axis=1, keepdims=True) / model
        mean_gh = jnp.sum(grad * hat, axis=1, keepdims=True) / model
        out[at, :] = (scale * (grad - mean_g - hat * mean_gh)).astype(BF16)


def place_kernel(at, blocks, *refs):
    out, rows = refs[-1], blocks.shape[3]
    for h in range(2):
        for n in range(2):
            for side in range(2):
                to = slice((2 * h + side) * rows, (2 * h + side + 1) * rows)
                out[0, to, n * 128 : (n + 1) * 128] = blocks[h, n, side].astype(F32)


def place(at, blocks, dims, before=()):
    return pl.pallas_call(
        place_kernel,
        grid_spec=pltpu.PrefetchScalarGridSpec(
            num_scalar_prefetch=1,
            grid=(4,),
            in_specs=[pl.BlockSpec((2, 2) + blocks.shape[2:], lambda m, at: (0, m, 0, 0, 0))]
            + [pl.BlockSpec(memory_space=pl.ANY) for _ in before],
            out_specs=pl.BlockSpec((1, dims[1] // 2, dims[2]), lambda m, at: (m, at[0], 0)),
        ),
        out_shape=shape(dims, F32),
        input_output_aliases={2: 0} if before else {},
        compiler_params=pltpu.CompilerParams(vmem_limit_bytes=12 * 1024 * 1024),
        cost_estimate=pl.CostEstimate(flops=1, bytes_accessed=8 * math.prod(dims), transcendentals=0),
        name="place",
    )(at, blocks, *before)


def swap_groups(with_x):
    if with_x:
        return [[x * 16 + z * 2 + core for x in range(2) for z in range(NZ)] for core in range(2)]
    return [[x * 16 + z * 2 + core for z in range(NZ)] for x in range(2) for core in range(2)]


def exchange(values, with_x):
    return lax.all_to_all(
        values, "dp", split_axis=0, concat_axis=0, axis_index_groups=swap_groups(with_x), tiled=True
    )


def per_device(tokens, cotangent, lengths, positions, weights):
    rows, model = tokens.shape
    shard_rows, cols = weights.shape[1], weights.shape[2]
    width = shard_rows // 2
    dp, fs = lax.axis_index("dp"), lax.axis_index("fsdp")
    core, x_hi = dp % 2, dp // 16
    y_at, x_lo = fs // 2, fs % 2
    sign = 1 - 2 * core
    offs = []
    for c, s in ((core, sign), (1 - core, -sign)):
        for k, dx in ORDER:
            shard = ((y_at - s * k + 4) % NY) * 2 + (x_lo + dx) % 2
            offs.append(shard * shard_rows + c * width)
    info = jnp.stack(offs + [x_hi * 2 + x_lo, x_lo, core, sign]).astype(jnp.int32)
    half = width // 2

    pair = shape((2, rows, model // 2))
    some = rows // 4
    own, send = call(
        functools.partial(prep_kernel, width),
        [(pair, (2, some, model // 2), lambda i: (0, i, 0))] * 2,
        [info, (tokens, (some, model), lambda i: (i, 0)), (cotangent, (some, model), lambda i: (i, 0))],
        grid=(4,),
        scalars=1,
        scratch=[pltpu.VMEM((some, model), BF16)],
        flops=8 * rows * model,
        nbytes=8 * rows * model,
        name="prep",
    )

    whole, *parts = half_of(weights)
    w = {(0, 0): whole}
    w[0, 1] = shift(w[0, 0], dx=1)
    w[3, 0] = [shift(part, dy=-1) for part in parts]
    w[1, 0] = shift(w[0, 0], dy=1)
    w[2, 0] = shift(w[1, 0], dy=1)
    w[1, 1] = shift(w[1, 0], dx=1)
    w[3, 1] = [shift(part, dx=1) for part in w[3, 0]]
    w[2, 1] = shift(w[1, 1], dy=1)
    shards = [w[place] for place in ORDER]

    peer = shift(gate(send, [w[1, 0], w[0, 1], w[3, 0][0]]), dc=1)
    one = (1, rows, model // 2)
    (turned,) = call(
        functools.partial(flip_kernel, width),
        [(shape((2, 4, 2, 4, half // 2, 2 * rows)), (2, 4, 1, 4, half // 2, 2 * rows), lambda i: (0, 0, i, 0, 0, 0))],
        [info, (own, one, lambda i: (i, 0, 0)), (peer, one, lambda i: (i, 0, 0))],
        grid=(2,),
        scalars=1,
        nbytes=8 * rows * model,
        name="flip",
    )

    quarter = HD // 4
    frequency = (ROPE_BASE ** (-np.arange(quarter, dtype=np.float64) / quarter)).astype(np.float32)
    angle_r = positions[0].astype(F32)[:, None] * frequency[None, :]
    angle_c = positions[1].astype(F32)[:, None] * frequency[None, :]
    cos_r, sin_r, cos_c, sin_c = jnp.cos(angle_r), jnp.sin(angle_r), jnp.cos(angle_c), jnp.sin(angle_c)
    cos_t = jnp.concatenate([cos_r, cos_r, cos_c, cos_c], axis=1)
    sin_t = jnp.concatenate([-sin_r, sin_r, -sin_c, sin_c], axis=1)

    lin_shape = shape((rows, 4 * cols), F32)
    one_matrix = (1, width, cols)

    def by_matrix(w_j):
        if not isinstance(w_j, list):
            return [(w_j, one_matrix, lambda m: (m, 0, 0))]
        return [
            (w_j[0], one_matrix, lambda m: (jnp.minimum(m, 1), 0, 0)),
            (w_j[1], one_matrix, lambda m: (jnp.maximum(m - 2, 0), 0, 0)),
        ]

    lin = []
    for first, pairs in ((0, 3), (3, 1)):
        span = 2 * pairs * width
        group = shards[2 * first : 2 * (first + pairs)]
        columns = functools.partial(lambda c, m: (m // 3, 0, c), first // pairs)
        acc = ((rows, cols), lambda m: (0, m))
        lin = call(
            functools.partial(linear_kernel, [len(w_j) if isinstance(w_j, list) else 1 for w_j in group]),
            [(lin_shape, *acc)] * 2,
            [(own, (1, rows, span), columns), (peer, (1, rows, span), columns)]
            + [item for w_j in group for item in by_matrix(w_j)]
            + [(value, *acc) for value in lin],
            grid=(4,),
            flops=2 * 2 * rows * 2 * pairs * width * 4 * cols,
            nbytes=2 * pairs * width * 8 * cols + 8 * rows * 2 * pairs * width,
            name="linear",
            after=[] if first else [turned, cos_t, sin_t],
        )
    lin_own, lin_send = lin
    lin_peer = shift(lin_send, dc=1)
    (y_own,) = call(
        attend_kernel,
        [shape((rows, 4 * cols))],
        [lengths, lin_own, lin_peer, cos_t, sin_t],
        scalars=1,
        flops=HEADS * 10 * rows * rows * HD * 2,
        nbytes=10 * rows * 4 * cols,
        name="attend",
    )
    y_peer = shift(y_own, dc=1)

    quarter = half // 2
    piece = shape((4, 8, quarter, 128))

    def terms(steps):
        part = len(steps) / 4
        picks = [functools.partial(lambda step, _: (0, step, 0, 0, 0, 0), step) for step in steps]
        return call(
            functools.partial(terms_kernel, len(steps)),
            [piece] * (2 * len(steps)),
            [(turned, (2, 1, 2, 4, quarter, 2 * rows), pick) for pick in picks] + [y_own, y_peer],
            flops=int(part * 2 * 2 * rows * (model // 2) * 4 * cols),
            nbytes=int(part * (4 * model * cols + 8 * rows * model)),
            name="terms",
        )

    far = terms([2])
    far = [along(far[0], first=1), along(far[1], first=-1)]
    back = terms([3])
    back = [along(back[0], first=-1), along(back[1], first=1)]
    near = terms([1, 0])

    per_u = ((1, 8, quarter, 128), lambda u: (u, 0, 0, 0))
    joined = sum_call(
        join_kernel,
        "join",
        [(piece, *per_u)] * 2,
        [(near[0], *per_u), (far[0], *per_u), (near[1], *per_u), (far[1], *per_u)],
        grid=(4,),
    )
    ahead = [along(joined[0], first=1), along(joined[1], first=-1)]

    def first_three(w_j):
        if not isinstance(w_j, list):
            return [(w_j, (3, width, cols), lambda _: (0, 0, 0))]
        return [w_j[0], (w_j[1], one_matrix, lambda _: (0, 0, 0))]

    g_own, g_send = call(
        functools.partial(normed_grad_kernel, width, [len(first_three(w_j)) for w_j in shards]),
        [shape((rows, model // 2), F32), shape((rows, model // 2))],
        [y_own, y_peer] + [item for w_j in shards for item in first_three(w_j)],
        flops=2 * rows * model * 3 * cols,
        nbytes=4 * model * cols + 4 * rows * model,
        name="normed_grad",
        after=[joined[0]],
    )

    per_n = ((4, 2, quarter, 128), lambda n: (0, n, 0, 0))
    mixed = shape((8, 2, quarter, 128))
    out_n = ((2, 2, quarter, 128), lambda n: (n, 0, 0, 0))
    halfway = sum_call(
        sides_kernel,
        "sides",
        [(mixed, *out_n)] * 4,
        [(value, *per_n) for value in (near[2], back[0], ahead[0], near[3], back[1], ahead[1])],
        grid=(4,),
        after=[g_send],
    )
    g_peer = shift(gate(g_send, [halfway[0]]), dc=1)
    g_rows = ((some, model // 2), lambda i: (i, 0))
    grad_tokens, mark = call(
        functools.partial(token_grad_kernel, width),
        [(shape((rows, model)), (some, model), lambda i: (i, 0)), (shape((8, 128), F32), (8, 128), lambda i: (0, 0))],
        [info, (tokens, (some, model), lambda i: (i, 0)), (g_own, *g_rows), (g_peer, *g_rows)],
        grid=(4,),
        scalars=1,
        scratch=[pltpu.VMEM((some, model), F32)],
        flops=16 * rows * model,
        nbytes=8 * rows * model,
        name="token_grad",
    )

    rest = [along(halfway[d], second=d) for d in range(1, 4)]
    (by_z,) = sum_call(
        seconds_kernel,
        "seconds",
        [(mixed, *out_n)],
        [(value, *out_n) for value in [halfway[0]] + rest],
        grid=(4,),
        after=[mark],
    )
    (spread,) = sum_call(last_kernel, "last", [shape((2 * NZ, 2, quarter, 128))], [exchange(by_z, False)])
    done = exchange(spread, True).reshape(2, NZ, 2, quarter, 128)
    dims = (4, shard_rows, cols)
    weight_grads = place(jnp.stack([core]).astype(jnp.int32), done, dims)
    weight_grads = place(jnp.stack([1 - core]).astype(jnp.int32), shift(done, dc=1), dims, [weight_grads])
    return (grad_tokens, weight_grads)


def solution(mesh):
    return jax.shard_map(
        per_device,
        mesh=mesh,
        in_specs=(
            P(("dp", "fsdp"), None),
            P(("dp", "fsdp"), None),
            P(("dp", "fsdp"), None),
            P(None, ("dp", "fsdp")),
            P(None, "fsdp", None),
        ),
        out_specs=(P(("dp", "fsdp"), None), P(None, "fsdp", None)),
        check_vma=False,
    )
```

```python
import functools
import math

import jax
import jax.numpy as jnp
import numpy as np
from jax import lax
from jax.experimental import pallas as pl
from jax.experimental.pallas import tpu as pltpu
from jax.sharding import PartitionSpec as P

HD = 128
HEADS = 2
ROPE_BASE = 100.0
EPS = 1e-6
NX, NY, NZ = 4, 4, 8
ORDER = [(0, 0), (0, 1), (1, 0), (1, 1), (3, 0), (2, 0), (3, 1), (2, 1)]
X_AT, X_LO, CORE, SIGN = 16, 17, 18, 19
BF16, F32 = jnp.bfloat16, jnp.float32


def flat_index(x, y, z, core):
    return ((x // 2) * 16 + z * 2 + core) * 8 + y * 2 + x % 2


DEVICES = [(x, y, z, core) for x in range(NX) for y in range(NY) for z in range(NZ) for core in range(2)]


def permute(values, target):
    pairs = []
    for x, y, z, core in DEVICES:
        tx, ty, tz, tcore = target(x, y, z, core)
        pairs.append((flat_index(x, y, z, core), flat_index(tx % NX, ty % NY, tz % NZ, tcore)))
    return lax.ppermute(values, ("dp", "fsdp"), pairs)


def shift(values, dx=0, dy=0, dc=0):
    def target(x, y, z, core):
        s = 1 - 2 * core
        return x + s * dx, y + s * dy, z, core ^ dc

    return permute(values, target)


def along(values, first=0, second=0):
    def target(x, y, z, core):
        dx, dy = (second, first) if core == 0 else (first, second)
        return x + dx, y + dy, z, core

    return permute(values, target)


def call(body, outs, operands, grid=(), scalars=0, scratch=(), flops=0, nbytes=0, name=None, after=()):
    count, last = len(operands), len(operands) + len(after)
    held = 0
    arrays, in_specs, out_shapes, out_specs = [], [], [], []
    for k, item in enumerate(list(operands) + list(outs)):
        value, *place = item if isinstance(item, tuple) else (item,)
        if k < scalars:
            spec = pl.BlockSpec(memory_space=pltpu.SMEM)
        elif place:
            spec = pl.BlockSpec(place[0], place[1])
            held += 2 * math.prod(place[0]) * value.dtype.itemsize
        else:
            spec = pl.BlockSpec(memory_space=pltpu.VMEM)
            held += math.prod(value.shape) * value.dtype.itemsize
        (arrays if k < count else out_shapes).append(value)
        (in_specs if k < count else out_specs).append(spec)
    held += sum(math.prod(ref.shape) * ref.dtype.itemsize for ref in scratch)
    in_specs += [pl.BlockSpec(memory_space=pl.ANY) for _ in after]
    kernel = (lambda *refs: body(*refs[:count], *refs[last:])) if after else body
    return pl.pallas_call(
        kernel,
        grid=grid or (1,),
        out_shape=out_shapes,
        in_specs=in_specs,
        out_specs=out_specs,
        scratch_shapes=list(scratch),
        compiler_params=pltpu.CompilerParams(vmem_limit_bytes=held + 8 * 1024 * 1024),
        cost_estimate=pl.CostEstimate(flops=flops, bytes_accessed=nbytes, transcendentals=0),
        name=name,
    )(*arrays, *after)


def gate(value, after):
    return pl.pallas_call(
        lambda *refs: None,
        out_shape=shape(value.shape, value.dtype),
        in_specs=[pl.BlockSpec(memory_space=pl.ANY)] * (1 + len(after)),
        out_specs=pl.BlockSpec(memory_space=pl.ANY),
        input_output_aliases={0: 0},
        cost_estimate=pl.CostEstimate(flops=1, bytes_accessed=1, transcendentals=0),
        name="gate",
    )(value, *after)


def shape(dims, dtype=BF16):
    return jax.ShapeDtypeStruct(dims, dtype)


def half_kernel(weights, whole, *rest):
    parts, sems = rest[:2], rest[2]
    width = whole.shape[1]
    rows = pl.ds(pl.multiple_of(lax.axis_index("dp") % 2 * width, width), width)
    copies = [pltpu.make_async_copy(weights.at[:, rows], whole, sems.at[0])]
    for k, part in enumerate(parts):
        copies.append(pltpu.make_async_copy(weights.at[pl.ds(2 * k, 2), rows], part, sems.at[1 + k]))
    for copy in copies:
        copy.start()
    for copy in copies:
        copy.wait()


def half_of(weights):
    _, rows, cols = weights.shape
    return pl.pallas_call(
        half_kernel,
        out_shape=[shape((count, rows // 2, cols)) for count in (4, 2, 2)],
        in_specs=[pl.BlockSpec(memory_space=pl.ANY)],
        out_specs=[pl.BlockSpec(memory_space=pltpu.VMEM)] * 3,
        scratch_shapes=[pltpu.SemaphoreType.DMA((3,))],
        compiler_params=pltpu.CompilerParams(vmem_limit_bytes=56 * 1024 * 1024),
        cost_estimate=pl.CostEstimate(flops=1, bytes_accessed=1, transcendentals=0),
        name="half",
    )(weights)


def prep_kernel(width, info, tokens, cot, own, send, normed):
    rows, model = tokens.shape
    step = 16
    for i in range(rows // step):
        at = slice(i * step, (i + 1) * step)
        x = tokens[at, :].astype(F32)
        center = x - jnp.sum(x, axis=1, keepdims=True) / model
        var = jnp.sum(center * center, axis=1, keepdims=True) / model
        normed[at, :] = (center * lax.rsqrt(var + EPS)).astype(BF16)
    for j in range(8):
        to = slice(j * width, (j + 1) * width)
        for out, first in ((own, 0), (send, 8)):
            cols = pl.ds(pl.multiple_of(info[first + j], 128), width)
            out[0, :, to] = normed[:, cols]
            out[1, :, to] = cot[:, cols]


def flip_kernel(width, info, own, peer, out):
    half = width // 2
    quarter = half // 2
    core, sign, x_at = info[CORE], info[SIGN], info[X_AT]
    for j, (k, dx) in enumerate(ORDER):
        at = slice(j * width, (j + 1) * width)
        y_steps = lax.rem(4 - sign * k, 4)
        turned = jnp.concatenate([own[0, :, at], peer[0, :, at]], axis=0).T
        for x_hi in range(2):
            x_to = 2 * x_hi + lax.rem(info[X_LO] + dx, 2)
            x_steps = lax.rem(x_to - x_at + 4, 4)
            first = jnp.where(core == 0, y_steps, x_steps)
            second = jnp.where(core == 0, x_steps, y_steps)
            for side in range(2):
                steps = first if side == 0 else lax.rem(4 - first, 4)
                start = x_hi * half + side * quarter
                out[side, steps, 0, second] = turned[start : start + quarter]


def linear_kernel(counts, own, peer, *refs):
    pairs, shards, start = len(counts) // 2, [], 0
    for count in counts:
        got = refs[start : start + count]
        start += count
        shards.append(got[0][...] if count == 1 else jnp.where(pl.program_id(0) < 2, got[0][...], got[1][...]))
    before, outs = refs[start:-2], refs[-2:]
    depth = own.shape[2] // pairs
    rights = [jnp.concatenate([shards[2 * p][0], shards[2 * p + 1][0]], axis=0) for p in range(pairs)]
    for side, left in enumerate((own, peer)):
        total = before[side][...] if before else None
        for p, right in enumerate(rights):
            term = jnp.dot(left[0, :, p * depth : (p + 1) * depth], right, preferred_element_type=F32)
            total = term if total is None else total + term
        outs[side][...] = total


def swap_quarters(x):
    lane = lax.broadcasted_iota(jnp.int32, x.shape, 1)
    quarter = HD // 4
    up = pltpu.roll(x, HD - quarter, 1)
    down = pltpu.roll(x, quarter, 1)
    return jnp.where(lane % (2 * quarter) < quarter, up, down)


def mean_of(x):
    return jnp.sum(x, axis=1, keepdims=True) * (1.0 / HD)


def norm_rows(x):
    center = x - mean_of(x)
    scale = lax.rsqrt(mean_of(center * center) + EPS)
    return center * scale, scale


def norm_rows_back(g, hat, scale):
    return scale * (g - mean_of(g) - hat * mean_of(g * hat))


def dot_t(a, b, dims):
    return lax.dot_general(a, b, ((dims[0], dims[1]), ((), ())), preferred_element_type=F32)


def attend_kernel(lengths, mine, theirs, cos_t, sin_t, out):
    rows = mine.shape[0]
    cols = HEADS * HD
    row_id = lax.broadcasted_iota(jnp.int32, (rows, 1), 0)
    col_id = lax.broadcasted_iota(jnp.int32, (1, rows), 1)

    def slot(ids):
        count, end = jnp.zeros(ids.shape, jnp.int32), 0
        for k in range(3):
            end = end + lengths[0, k]
            count = count + (ids >= end).astype(jnp.int32)
        return count

    row_slot, col_slot = slot(row_id), slot(col_id)
    same = row_slot == col_slot
    live = row_slot < 3
    cosine, sine = cos_t[...], sin_t[...]
    score_scale = 1.0 / math.sqrt(HD)
    for h in range(HEADS):

        def part(m):
            at = slice(m * cols + h * HD, m * cols + (h + 1) * HD)
            return mine[:, at] + theirs[:, at]

        q_hat, q_scale = norm_rows(part(0))
        k_hat, k_scale = norm_rows(part(1))
        q = (q_hat * cosine + swap_quarters(q_hat) * sine).astype(BF16)
        k = (k_hat * cosine + swap_quarters(k_hat) * sine).astype(BF16)
        v = part(2).astype(BF16)
        ga = jnp.where(live, part(3), 0.0).astype(BF16)
        scores = dot_t(q, k, ((1,), (1,))) * score_scale
        e = jnp.where(same, jnp.exp(scores), 0.0)
        p32 = e / jnp.sum(e, axis=1, keepdims=True)
        p = p32.astype(BF16)
        att = jnp.dot(p, v, preferred_element_type=F32).astype(BF16)
        gv = dot_t(p, ga, ((0,), (0,)))
        gp = dot_t(ga, v, ((1,), (1,))).astype(BF16).astype(F32)
        gs = p32 * (gp - jnp.sum(gp * p32, axis=1, keepdims=True)) * score_scale
        gs = gs.astype(BF16)
        gq = jnp.dot(gs, k, preferred_element_type=F32).astype(BF16).astype(F32)
        gk = dot_t(gs, q, ((0,), (0,))).astype(BF16).astype(F32)
        gq = norm_rows_back(gq * cosine + swap_quarters(gq * sine), q_hat, q_scale)
        gk = norm_rows_back(gk * cosine + swap_quarters(gk * sine), k_hat, k_scale)
        at = lambda m: slice(m * cols + h * HD, m * cols + (h + 1) * HD)
        out[:, at(0)] = gq.astype(BF16)
        out[:, at(1)] = gk.astype(BF16)
        out[:, at(2)] = gv.astype(BF16)
        out[:, at(3)] = jnp.where(live, att.astype(F32), 0.0).astype(BF16)


def terms_kernel(count, *refs):
    turned, (y_own, y_peer), outs = refs[:count], refs[count : count + 2], refs[count + 2 :]
    rows, depth = turned[0].shape[4:]
    y_all = jnp.concatenate([y_own[...], y_peer[...]], axis=0)
    proj = 3 * HEADS * HD
    for k, ref in enumerate(turned):
        for side in range(2):
            for i, right in ((0, y_all[:, :proj]), (1, y_all[:, proj:])):
                left = ref[side, 0, i].reshape(4 * rows, depth)
                value = jnp.dot(left, right, preferred_element_type=F32).astype(BF16)
                for n in range(right.shape[1] // 128):
                    for u in range(4):
                        block = value[u * rows : (u + 1) * rows, n * 128 : (n + 1) * 128]
                        outs[2 * k + side][u, 6 * i + n] = block


def add_up(refs, at):
    total = refs[0][at].astype(F32)
    for ref in refs[1:]:
        total = total + ref[at].astype(F32)
    return total.astype(BF16)


def join_kernel(near_0, far_0, near_1, far_1, out_0, out_1):
    for n in range(8):
        out_0[0, n] = add_up((near_0, far_0), (0, n))
        out_1[0, n] = add_up((near_1, far_1), (0, n))


def sides_kernel(*refs):
    for side in range(2):
        for u, out in enumerate(refs[6:]):
            for n in range(out.shape[0]):
                out[n, side] = add_up(refs[3 * side : 3 * side + 3], (u, n))


def seconds_kernel(*refs):
    for n in range(refs[0].shape[0]):
        for side in range(2):
            refs[-1][n, side] = add_up(refs[:-1], (n, side))


def last_kernel(got, out):
    for side in range(2):
        total = got[0, side].astype(F32)
        for k in range(1, 8):
            total = total + got[k, side].astype(F32)
        for k in range(out.shape[0]):
            out[k, side] = total.astype(BF16)


def sum_call(body, name, outs, operands, grid=(), after=()):
    value = operands[0][0] if isinstance(operands[0], tuple) else operands[0]
    size = math.prod(value.shape)
    return call(
        body,
        outs,
        operands,
        grid=grid,
        flops=len(operands) * size,
        nbytes=2 * size * (len(operands) + 2),
        name=name,
        after=after,
    )


def normed_grad_kernel(width, counts, y_own, y_peer, *refs):
    shards, start, (g_own, g_send) = [], 0, refs[-2:]
    for count in counts:
        shards.append([ref[m] for ref in refs[start : start + count] for m in range(ref.shape[0])])
        start += count
    rows = y_own.shape[0]
    proj = 3 * HEADS * HD
    left = jnp.concatenate([y_own[:, :proj], y_peer[:, :proj]], axis=0)
    for j in range(8):
        right = jnp.concatenate(shards[j], axis=1)
        total = dot_t(left, right, ((1,), (1,)))
        at = slice(j * width, (j + 1) * width)
        g_own[:, at] = total[:rows]
        g_send[:, at] = total[rows:].astype(BF16)


def token_grad_kernel(width, info, tokens, g_own, g_peer, out, mark, g):
    mark[...] = jnp.zeros_like(mark)
    rows, model = tokens.shape
    for first, ref in ((0, g_own), (8, g_peer)):
        for j in range(8):
            to = pl.ds(pl.multiple_of(info[first + j], 128), width)
            g[:, to] = ref[:, j * width : (j + 1) * width].astype(F32)
    step = 16
    for i in range(rows // step):
        at = slice(i * step, (i + 1) * step)
        x = tokens[at, :].astype(F32)
        center = x - jnp.sum(x, axis=1, keepdims=True) / model
        scale = lax.rsqrt(jnp.sum(center * center, axis=1, keepdims=True) / model + EPS)
        hat = center * scale
        grad = g[at, :]
        mean_g = jnp.sum(grad, axis=1, keepdims=True) / model
        mean_gh = jnp.sum(grad * hat, axis=1, keepdims=True) / model
        out[at, :] = (scale * (grad - mean_g - hat * mean_gh)).astype(BF16)


def place_kernel(at, blocks, *refs):
    out, rows = refs[-1], blocks.shape[3]
    for h in range(2):
        for n in range(2):
            for side in range(2):
                to = slice((2 * h + side) * rows, (2 * h + side + 1) * rows)
                out[0, to, n * 128 : (n + 1) * 128] = blocks[h, n, side].astype(F32)


def place(at, blocks, dims, before=()):
    return pl.pallas_call(
        place_kernel,
        grid_spec=pltpu.PrefetchScalarGridSpec(
            num_scalar_prefetch=1,
            grid=(4,),
            in_specs=[pl.BlockSpec((2, 2) + blocks.shape[2:], lambda m, at: (0, m, 0, 0, 0))]
            + [pl.BlockSpec(memory_space=pl.ANY) for _ in before],
            out_specs=pl.BlockSpec((1, dims[1] // 2, dims[2]), lambda m, at: (m, at[0], 0)),
        ),
        out_shape=shape(dims, F32),
        input_output_aliases={2: 0} if before else {},
        compiler_params=pltpu.CompilerParams(vmem_limit_bytes=12 * 1024 * 1024),
        cost_estimate=pl.CostEstimate(flops=1, bytes_accessed=8 * math.prod(dims), transcendentals=0),
        name="place",
    )(at, blocks, *before)


def swap_groups(with_x):
    if with_x:
        return [[x * 16 + z * 2 + core for x in range(2) for z in range(NZ)] for core in range(2)]
    return [[x * 16 + z * 2 + core for z in range(NZ)] for x in range(2) for core in range(2)]


def exchange(values, with_x):
    return lax.all_to_all(
        values, "dp", split_axis=0, concat_axis=0, axis_index_groups=swap_groups(with_x), tiled=True
    )


def per_device(tokens, cotangent, lengths, positions, weights):
    rows, model = tokens.shape
    shard_rows, cols = weights.shape[1], weights.shape[2]
    width = shard_rows // 2
    dp, fs = lax.axis_index("dp"), lax.axis_index("fsdp")
    core, x_hi = dp % 2, dp // 16
    y_at, x_lo = fs // 2, fs % 2
    sign = 1 - 2 * core
    offs = []
    for c, s in ((core, sign), (1 - core, -sign)):
        for k, dx in ORDER:
            shard = ((y_at - s * k + 4) % NY) * 2 + (x_lo + dx) % 2
            offs.append(shard * shard_rows + c * width)
    info = jnp.stack(offs + [x_hi * 2 + x_lo, x_lo, core, sign]).astype(jnp.int32)
    half = width // 2

    pair = shape((2, rows, model // 2))
    some = rows // 4
    own, send = call(
        functools.partial(prep_kernel, width),
        [(pair, (2, some, model // 2), lambda i: (0, i, 0))] * 2,
        [info, (tokens, (some, model), lambda i: (i, 0)), (cotangent, (some, model), lambda i: (i, 0))],
        grid=(4,),
        scalars=1,
        scratch=[pltpu.VMEM((some, model), BF16)],
        flops=8 * rows * model,
        nbytes=8 * rows * model,
        name="prep",
    )

    whole, *parts = half_of(weights)
    w = {(0, 0): whole}
    w[0, 1] = shift(w[0, 0], dx=1)
    w[3, 0] = [shift(part, dy=-1) for part in parts]
    w[1, 0] = shift(w[0, 0], dy=1)
    w[2, 0] = shift(w[1, 0], dy=1)
    w[1, 1] = shift(w[1, 0], dx=1)
    w[3, 1] = [shift(part, dx=1) for part in w[3, 0]]
    w[2, 1] = shift(w[1, 1], dy=1)
    shards = [w[place] for place in ORDER]

    peer = shift(gate(send, [w[1, 0], w[0, 1], w[3, 0][0]]), dc=1)
    one = (1, rows, model // 2)
    (turned,) = call(
        functools.partial(flip_kernel, width),
        [(shape((2, 4, 2, 4, half // 2, 2 * rows)), (2, 4, 1, 4, half // 2, 2 * rows), lambda i: (0, 0, i, 0, 0, 0))],
        [info, (own, one, lambda i: (i, 0, 0)), (peer, one, lambda i: (i, 0, 0))],
        grid=(2,),
        scalars=1,
        nbytes=8 * rows * model,
        name="flip",
    )

    quarter = HD // 4
    frequency = (ROPE_BASE ** (-np.arange(quarter, dtype=np.float64) / quarter)).astype(np.float32)
    angle_r = positions[0].astype(F32)[:, None] * frequency[None, :]
    angle_c = positions[1].astype(F32)[:, None] * frequency[None, :]
    cos_r, sin_r, cos_c, sin_c = jnp.cos(angle_r), jnp.sin(angle_r), jnp.cos(angle_c), jnp.sin(angle_c)
    cos_t = jnp.concatenate([cos_r, cos_r, cos_c, cos_c], axis=1)
    sin_t = jnp.concatenate([-sin_r, sin_r, -sin_c, sin_c], axis=1)

    lin_shape = shape((rows, 4 * cols), F32)
    one_matrix = (1, width, cols)

    def by_matrix(w_j):
        if not isinstance(w_j, list):
            return [(w_j, one_matrix, lambda m: (m, 0, 0))]
        return [
            (w_j[0], one_matrix, lambda m: (jnp.minimum(m, 1), 0, 0)),
            (w_j[1], one_matrix, lambda m: (jnp.maximum(m - 2, 0), 0, 0)),
        ]

    lin = []
    for first, pairs in ((0, 3), (3, 1)):
        span = 2 * pairs * width
        group = shards[2 * first : 2 * (first + pairs)]
        columns = functools.partial(lambda c, m: (m // 3, 0, c), first // pairs)
        acc = ((rows, cols), lambda m: (0, m))
        lin = call(
            functools.partial(linear_kernel, [len(w_j) if isinstance(w_j, list) else 1 for w_j in group]),
            [(lin_shape, *acc)] * 2,
            [(own, (1, rows, span), columns), (peer, (1, rows, span), columns)]
            + [item for w_j in group for item in by_matrix(w_j)]
            + [(value, *acc) for value in lin],
            grid=(4,),
            flops=2 * 2 * rows * 2 * pairs * width * 4 * cols,
            nbytes=2 * pairs * width * 8 * cols + 8 * rows * 2 * pairs * width,
            name="linear",
            after=[] if first else [turned, cos_t, sin_t],
        )
    lin_own, lin_send = lin
    lin_peer = shift(lin_send, dc=1)
    (y_own,) = call(
        attend_kernel,
        [shape((rows, 4 * cols))],
        [lengths, lin_own, lin_peer, cos_t, sin_t],
        scalars=1,
        flops=HEADS * 10 * rows * rows * HD * 2,
        nbytes=10 * rows * 4 * cols,
        name="attend",
    )
    y_peer = shift(y_own, dc=1)

    quarter = half // 2
    piece = shape((4, 8, quarter, 128))

    def terms(steps):
        part = len(steps) / 4
        picks = [functools.partial(lambda step, _: (0, step, 0, 0, 0, 0), step) for step in steps]
        return call(
            functools.partial(terms_kernel, len(steps)),
            [piece] * (2 * len(steps)),
            [(turned, (2, 1, 2, 4, quarter, 2 * rows), pick) for pick in picks] + [y_own, y_peer],
            flops=int(part * 2 * 2 * rows * (model // 2) * 4 * cols),
            nbytes=int(part * (4 * model * cols + 8 * rows * model)),
            name="terms",
        )

    far = terms([2])
    far = [along(far[0], first=1), along(far[1], first=-1)]
    back = terms([3])
    back = [along(back[0], first=-1), along(back[1], first=1)]
    near = terms([1, 0])

    per_u = ((1, 8, quarter, 128), lambda u: (u, 0, 0, 0))
    joined = sum_call(
        join_kernel,
        "join",
        [(piece, *per_u)] * 2,
        [(near[0], *per_u), (far[0], *per_u), (near[1], *per_u), (far[1], *per_u)],
        grid=(4,),
    )
    ahead = [along(joined[0], first=1), along(joined[1], first=-1)]

    def first_three(w_j):
        if not isinstance(w_j, list):
            return [(w_j, (3, width, cols), lambda _: (0, 0, 0))]
        return [w_j[0], (w_j[1], one_matrix, lambda _: (0, 0, 0))]

    g_own, g_send = call(
        functools.partial(normed_grad_kernel, width, [len(first_three(w_j)) for w_j in shards]),
        [shape((rows, model // 2), F32), shape((rows, model // 2))],
        [y_own, y_peer] + [item for w_j in shards for item in first_three(w_j)],
        flops=2 * rows * model * 3 * cols,
        nbytes=4 * model * cols + 4 * rows * model,
        name="normed_grad",
        after=[joined[0]],
    )

    per_n = ((4, 2, quarter, 128), lambda n: (0, n, 0, 0))
    mixed = shape((8, 2, quarter, 128))
    out_n = ((2, 2, quarter, 128), lambda n: (n, 0, 0, 0))
    halfway = sum_call(
        sides_kernel,
        "sides",
        [(mixed, *out_n)] * 4,
        [(value, *per_n) for value in (near[2], back[0], ahead[0], near[3], back[1], ahead[1])],
        grid=(4,),
        after=[g_send],
    )
    g_peer = shift(gate(g_send, [halfway[0]]), dc=1)
    g_rows = ((some, model // 2), lambda i: (i, 0))
    grad_tokens, mark = call(
        functools.partial(token_grad_kernel, width),
        [(shape((rows, model)), (some, model), lambda i: (i, 0)), (shape((8, 128), F32), (8, 128), lambda i: (0, 0))],
        [info, (tokens, (some, model), lambda i: (i, 0)), (g_own, *g_rows), (g_peer, *g_rows)],
        grid=(4,),
        scalars=1,
        scratch=[pltpu.VMEM((some, model), F32)],
        flops=16 * rows * model,
        nbytes=8 * rows * model,
        name="token_grad",
    )

    rest = [along(halfway[d], second=d) for d in range(1, 4)]
    (by_z,) = sum_call(
        seconds_kernel,
        "seconds",
        [(mixed, *out_n)],
        [(value, *out_n) for value in [halfway[0]] + rest],
        grid=(4,),
        after=[mark],
    )
    (spread,) = sum_call(last_kernel, "last", [shape((2 * NZ, 2, quarter, 128))], [exchange(by_z, False)])
    done = exchange(spread, True).reshape(2, NZ, 2, quarter, 128)
    dims = (4, shard_rows, cols)
    weight_grads = place(jnp.stack([core]).astype(jnp.int32), done, dims)
    weight_grads = place(jnp.stack([1 - core]).astype(jnp.int32), shift(done, dc=1), dims, [weight_grads])
    return (grad_tokens, weight_grads)


def solution(mesh):
    return jax.shard_map(
        per_device,
        mesh=mesh,
        in_specs=(
            P(("dp", "fsdp"), None),
            P(("dp", "fsdp"), None),
            P(("dp", "fsdp"), None),
            P(None, ("dp", "fsdp")),
            P(None, "fsdp", None),
        ),
        out_specs=(P(("dp", "fsdp"), None), P(None, "fsdp", None)),
        check_vma=False,
    )
```

```python
import functools
import math

import jax
import jax.numpy as jnp
import numpy as np
from jax import lax
from jax.experimental import pallas as pl
from jax.experimental.pallas import tpu as pltpu
from jax.sharding import PartitionSpec as P

HD = 128
HEADS = 2
ROPE_BASE = 100.0
EPS = 1e-6
NX, NY, NZ = 4, 4, 8
ORDER = [(0, 0), (0, 1), (1, 0), (1, 1), (3, 0), (2, 0), (3, 1), (2, 1)]
X_AT, X_LO, CORE, SIGN = 16, 17, 18, 19
BF16, F32 = jnp.bfloat16, jnp.float32


def flat_index(x, y, z, core):
    return ((x // 2) * 16 + z * 2 + core) * 8 + y * 2 + x % 2


DEVICES = [(x, y, z, core) for x in range(NX) for y in range(NY) for z in range(NZ) for core in range(2)]


def permute(values, target):
    pairs = []
    for x, y, z, core in DEVICES:
        tx, ty, tz, tcore = target(x, y, z, core)
        pairs.append((flat_index(x, y, z, core), flat_index(tx % NX, ty % NY, tz % NZ, tcore)))
    return lax.ppermute(values, ("dp", "fsdp"), pairs)


def shift(values, dx=0, dy=0, dc=0):
    def target(x, y, z, core):
        s = 1 - 2 * core
        return x + s * dx, y + s * dy, z, core ^ dc

    return permute(values, target)


def along(values, first=0, second=0):
    def target(x, y, z, core):
        dx, dy = (second, first) if core == 0 else (first, second)
        return x + dx, y + dy, z, core

    return permute(values, target)


def call(body, outs, operands, grid=(), scalars=0, scratch=(), flops=0, nbytes=0, name=None, after=()):
    count, last = len(operands), len(operands) + len(after)
    held = 0
    arrays, in_specs, out_shapes, out_specs = [], [], [], []
    for k, item in enumerate(list(operands) + list(outs)):
        value, *place = item if isinstance(item, tuple) else (item,)
        if k < scalars:
            spec = pl.BlockSpec(memory_space=pltpu.SMEM)
        elif place:
            spec = pl.BlockSpec(place[0], place[1])
            held += 2 * math.prod(place[0]) * value.dtype.itemsize
        else:
            spec = pl.BlockSpec(memory_space=pltpu.VMEM)
            held += math.prod(value.shape) * value.dtype.itemsize
        (arrays if k < count else out_shapes).append(value)
        (in_specs if k < count else out_specs).append(spec)
    held += sum(math.prod(ref.shape) * ref.dtype.itemsize for ref in scratch)
    in_specs += [pl.BlockSpec(memory_space=pl.ANY) for _ in after]
    kernel = (lambda *refs: body(*refs[:count], *refs[last:])) if after else body
    return pl.pallas_call(
        kernel,
        grid=grid or (1,),
        out_shape=out_shapes,
        in_specs=in_specs,
        out_specs=out_specs,
        scratch_shapes=list(scratch),
        compiler_params=pltpu.CompilerParams(vmem_limit_bytes=held + 8 * 1024 * 1024),
        cost_estimate=pl.CostEstimate(flops=flops, bytes_accessed=nbytes, transcendentals=0),
        name=name,
    )(*arrays, *after)


def gate(value, after):
    return pl.pallas_call(
        lambda *refs: None,
        out_shape=shape(value.shape, value.dtype),
        in_specs=[pl.BlockSpec(memory_space=pl.ANY)] * (1 + len(after)),
        out_specs=pl.BlockSpec(memory_space=pl.ANY),
        input_output_aliases={0: 0},
        cost_estimate=pl.CostEstimate(flops=1, bytes_accessed=1, transcendentals=0),
        name="gate",
    )(value, *after)


def shape(dims, dtype=BF16):
    return jax.ShapeDtypeStruct(dims, dtype)


def prep_kernel(width, info, tokens, cot, own, send, normed):
    rows, model = tokens.shape
    step = 16
    for i in range(rows // step):
        at = slice(i * step, (i + 1) * step)
        x = tokens[at, :].astype(F32)
        center = x - jnp.sum(x, axis=1, keepdims=True) / model
        var = jnp.sum(center * center, axis=1, keepdims=True) / model
        normed[at, :] = (center * lax.rsqrt(var + EPS)).astype(BF16)
    for j in range(8):
        to = slice(j * width, (j + 1) * width)
        for out, first in ((own, 0), (send, 8)):
            cols = pl.ds(pl.multiple_of(info[first + j], 128), width)
            out[0, :, to] = normed[:, cols]
            out[1, :, to] = cot[:, cols]


def flip_kernel(width, info, own, peer, out):
    half = width // 2
    quarter = half // 2
    core, sign, x_at = info[CORE], info[SIGN], info[X_AT]
    for j, (k, dx) in enumerate(ORDER):
        at = slice(j * width, (j + 1) * width)
        y_steps = lax.rem(4 - sign * k, 4)
        turned = jnp.concatenate([own[0, :, at], peer[0, :, at]], axis=0).T
        for x_hi in range(2):
            x_to = 2 * x_hi + lax.rem(info[X_LO] + dx, 2)
            x_steps = lax.rem(x_to - x_at + 4, 4)
            first = jnp.where(core == 0, y_steps, x_steps)
            second = jnp.where(core == 0, x_steps, y_steps)
            for side in range(2):
                steps = first if side == 0 else lax.rem(4 - first, 4)
                start = x_hi * half + side * quarter
                out[side, steps, 0, second] = turned[start : start + quarter]


def linear_kernel(counts, own, peer, *refs):
    pairs, shards, start = len(counts) // 2, [], 0
    for count in counts:
        got = refs[start : start + count]
        start += count
        shards.append(got[0][...] if count == 1 else jnp.where(pl.program_id(0) < 2, got[0][...], got[1][...]))
    before, outs = refs[start:-2], refs[-2:]
    depth = own.shape[2] // pairs
    rights = [jnp.concatenate([shards[2 * p][0], shards[2 * p + 1][0]], axis=0) for p in range(pairs)]
    for side, left in enumerate((own, peer)):
        total = before[side][...] if before else None
        for p, right in enumerate(rights):
            term = jnp.dot(left[0, :, p * depth : (p + 1) * depth], right, preferred_element_type=F32)
            total = term if total is None else total + term
        outs[side][...] = total


def swap_quarters(x):
    lane = lax.broadcasted_iota(jnp.int32, x.shape, 1)
    quarter = HD // 4
    up = pltpu.roll(x, HD - quarter, 1)
    down = pltpu.roll(x, quarter, 1)
    return jnp.where(lane % (2 * quarter) < quarter, up, down)


def mean_of(x):
    return jnp.sum(x, axis=1, keepdims=True) * (1.0 / HD)


def norm_rows(x):
    center = x - mean_of(x)
    scale = lax.rsqrt(mean_of(center * center) + EPS)
    return center * scale, scale


def norm_rows_back(g, hat, scale):
    return scale * (g - mean_of(g) - hat * mean_of(g * hat))


def dot_t(a, b, dims):
    return lax.dot_general(a, b, ((dims[0], dims[1]), ((), ())), preferred_element_type=F32)


def attend_kernel(lengths, mine, theirs, cos_t, sin_t, out):
    rows = mine.shape[0]
    cols = HEADS * HD
    row_id = lax.broadcasted_iota(jnp.int32, (rows, 1), 0)
    col_id = lax.broadcasted_iota(jnp.int32, (1, rows), 1)

    def slot(ids):
        count, end = jnp.zeros(ids.shape, jnp.int32), 0
        for k in range(3):
            end = end + lengths[0, k]
            count = count + (ids >= end).astype(jnp.int32)
        return count

    row_slot, col_slot = slot(row_id), slot(col_id)
    same = row_slot == col_slot
    live = row_slot < 3
    cosine, sine = cos_t[...], sin_t[...]
    score_scale = 1.0 / math.sqrt(HD)
    for h in range(HEADS):

        def part(m):
            at = slice(m * cols + h * HD, m * cols + (h + 1) * HD)
            return mine[:, at] + theirs[:, at]

        q_hat, q_scale = norm_rows(part(0))
        k_hat, k_scale = norm_rows(part(1))
        q = (q_hat * cosine + swap_quarters(q_hat) * sine).astype(BF16)
        k = (k_hat * cosine + swap_quarters(k_hat) * sine).astype(BF16)
        v = part(2).astype(BF16)
        ga = jnp.where(live, part(3), 0.0).astype(BF16)
        scores = dot_t(q, k, ((1,), (1,))) * score_scale
        e = jnp.where(same, jnp.exp(scores), 0.0)
        p32 = e / jnp.sum(e, axis=1, keepdims=True)
        p = p32.astype(BF16)
        att = jnp.dot(p, v, preferred_element_type=F32).astype(BF16)
        gv = dot_t(p, ga, ((0,), (0,)))
        gp = dot_t(ga, v, ((1,), (1,))).astype(BF16).astype(F32)
        gs = p32 * (gp - jnp.sum(gp * p32, axis=1, keepdims=True)) * score_scale
        gs = gs.astype(BF16)
        gq = jnp.dot(gs, k, preferred_element_type=F32).astype(BF16).astype(F32)
        gk = dot_t(gs, q, ((0,), (0,))).astype(BF16).astype(F32)
        gq = norm_rows_back(gq * cosine + swap_quarters(gq * sine), q_hat, q_scale)
        gk = norm_rows_back(gk * cosine + swap_quarters(gk * sine), k_hat, k_scale)
        at = lambda m: slice(m * cols + h * HD, m * cols + (h + 1) * HD)
        out[:, at(0)] = gq.astype(BF16)
        out[:, at(1)] = gk.astype(BF16)
        out[:, at(2)] = gv.astype(BF16)
        out[:, at(3)] = jnp.where(live, att.astype(F32), 0.0).astype(BF16)


def terms_kernel(count, *refs):
    turned, (y_own, y_peer), outs = refs[:count], refs[count : count + 2], refs[count + 2 :]
    rows, depth = turned[0].shape[4:]
    y_all = jnp.concatenate([y_own[...], y_peer[...]], axis=0)
    proj = 3 * HEADS * HD
    for k, ref in enumerate(turned):
        for side in range(2):
            for i, right in ((0, y_all[:, :proj]), (1, y_all[:, proj:])):
                left = ref[side, 0, i].reshape(4 * rows, depth)
                value = jnp.dot(left, right, preferred_element_type=F32).astype(BF16)
                for n in range(right.shape[1] // 128):
                    for u in range(4):
                        block = value[u * rows : (u + 1) * rows, n * 128 : (n + 1) * 128]
                        outs[2 * k + side][u, 6 * i + n] = block


def add_up(refs, at):
    total = refs[0][at].astype(F32)
    for ref in refs[1:]:
        total = total + ref[at].astype(F32)
    return total.astype(BF16)


def join_kernel(near_0, far_0, near_1, far_1, out_0, out_1):
    for n in range(8):
        out_0[0, n] = add_up((near_0, far_0), (0, n))
        out_1[0, n] = add_up((near_1, far_1), (0, n))


def sides_kernel(*refs):
    for side in range(2):
        for u, out in enumerate(refs[6:]):
            for n in range(out.shape[0]):
                out[n, side] = add_up(refs[3 * side : 3 * side + 3], (u, n))


def seconds_kernel(*refs):
    for n in range(refs[0].shape[0]):
        for side in range(2):
            refs[-1][n, side] = add_up(refs[:-1], (n, side))


def last_kernel(got, out):
    for side in range(2):
        total = got[0, side].astype(F32)
        for k in range(1, 8):
            total = total + got[k, side].astype(F32)
        for k in range(out.shape[0]):
            out[k, side] = total.astype(BF16)


def sum_call(body, name, outs, operands, grid=(), after=()):
    value = operands[0][0] if isinstance(operands[0], tuple) else operands[0]
    size = math.prod(value.shape)
    return call(
        body,
        outs,
        operands,
        grid=grid,
        flops=len(operands) * size,
        nbytes=2 * size * (len(operands) + 2),
        name=name,
        after=after,
    )


def normed_grad_kernel(width, counts, y_own, y_peer, *refs):
    shards, start, (g_own, g_send) = [], 0, refs[-2:]
    for count in counts:
        shards.append([ref[m] for ref in refs[start : start + count] for m in range(ref.shape[0])])
        start += count
    rows = y_own.shape[0]
    proj = 3 * HEADS * HD
    left = jnp.concatenate([y_own[:, :proj], y_peer[:, :proj]], axis=0)
    for j in range(8):
        right = jnp.concatenate(shards[j], axis=1)
        total = dot_t(left, right, ((1,), (1,)))
        at = slice(j * width, (j + 1) * width)
        g_own[:, at] = total[:rows]
        g_send[:, at] = total[rows:].astype(BF16)


def token_grad_kernel(width, info, tokens, g_own, g_peer, out, mark, g):
    mark[...] = jnp.zeros_like(mark)
    rows, model = tokens.shape
    for first, ref in ((0, g_own), (8, g_peer)):
        for j in range(8):
            to = pl.ds(pl.multiple_of(info[first + j], 128), width)
            g[:, to] = ref[:, j * width : (j + 1) * width].astype(F32)
    step = 16
    for i in range(rows // step):
        at = slice(i * step, (i + 1) * step)
        x = tokens[at, :].astype(F32)
        center = x - jnp.sum(x, axis=1, keepdims=True) / model
        scale = lax.rsqrt(jnp.sum(center * center, axis=1, keepdims=True) / model + EPS)
        hat = center * scale
        grad = g[at, :]
        mean_g = jnp.sum(grad, axis=1, keepdims=True) / model
        mean_gh = jnp.sum(grad * hat, axis=1, keepdims=True) / model
        out[at, :] = (scale * (grad - mean_g - hat * mean_gh)).astype(BF16)


def place_kernel(at, blocks, *refs):
    out, rows = refs[-1], blocks.shape[2]
    for n in range(2):
        for side in range(2):
            to = slice(side * rows, (side + 1) * rows)
            out[0, to, n * 128 : (n + 1) * 128] = blocks[n, side].astype(F32)


def place(at, blocks, dims, before=()):
    return pl.pallas_call(
        place_kernel,
        grid_spec=pltpu.PrefetchScalarGridSpec(
            num_scalar_prefetch=1,
            grid=(4,),
            in_specs=[pl.BlockSpec((2,) + blocks.shape[1:], lambda m, at: (m, 0, 0, 0))]
            + [pl.BlockSpec(memory_space=pl.ANY) for _ in before],
            out_specs=pl.BlockSpec((1, dims[1] // 4, dims[2]), lambda m, at: (m, at[0], 0)),
        ),
        out_shape=shape(dims, F32),
        input_output_aliases={2: 0} if before else {},
        compiler_params=pltpu.CompilerParams(vmem_limit_bytes=12 * 1024 * 1024),
        cost_estimate=pl.CostEstimate(flops=1, bytes_accessed=4 * math.prod(dims), transcendentals=0),
        name="place",
    )(at, blocks, *before)


def exchange(values):
    groups = [[x * 16 + z * 2 + core for z in range(NZ)] for x in range(2) for core in range(2)]
    return lax.all_to_all(values, "dp", split_axis=0, concat_axis=0, axis_index_groups=groups, tiled=True)


def per_device(tokens, cotangent, lengths, positions, weights):
    rows, model = tokens.shape
    shard_rows, cols = weights.shape[1], weights.shape[2]
    width = shard_rows // 2
    dp, fs = lax.axis_index("dp"), lax.axis_index("fsdp")
    core, x_hi = dp % 2, dp // 16
    y_at, x_lo = fs // 2, fs % 2
    sign = 1 - 2 * core
    offs = []
    for c, s in ((core, sign), (1 - core, -sign)):
        for k, dx in ORDER:
            shard = ((y_at - s * k + 4) % NY) * 2 + (x_lo + dx) % 2
            offs.append(shard * shard_rows + c * width)
    info = jnp.stack(offs + [x_hi * 2 + x_lo, x_lo, core, sign]).astype(jnp.int32)
    half = width // 2

    pair = shape((2, rows, model // 2))
    some = rows // 4
    own, send = call(
        functools.partial(prep_kernel, width),
        [(pair, (2, some, model // 2), lambda i: (0, i, 0))] * 2,
        [info, (tokens, (some, model), lambda i: (i, 0)), (cotangent, (some, model), lambda i: (i, 0))],
        grid=(4,),
        scalars=1,
        scratch=[pltpu.VMEM((some, model), BF16)],
        flops=8 * rows * model,
        nbytes=8 * rows * model,
        name="prep",
    )

    w = {(0, 0): lax.dynamic_slice(weights, (0, core * width, 0), (4, width, cols))}
    w[0, 1] = shift(w[0, 0], dx=1)
    parts = [lax.dynamic_slice(weights, (m, core * width, 0), (2, width, cols)) for m in (0, 2)]
    w[3, 0] = [shift(part, dy=-1) for part in parts]
    w[1, 0] = shift(w[0, 0], dy=1)
    w[2, 0] = shift(w[1, 0], dy=1)
    w[1, 1] = shift(w[1, 0], dx=1)
    w[3, 1] = [shift(part, dx=1) for part in w[3, 0]]
    w[2, 1] = shift(w[1, 1], dy=1)
    shards = [w[place] for place in ORDER]

    peer = shift(gate(send, [w[1, 0], w[0, 1], w[3, 0][0]]), dc=1)
    one = (1, rows, model // 2)
    (turned,) = call(
        functools.partial(flip_kernel, width),
        [(shape((2, 4, 2, 4, half // 2, 2 * rows)), (2, 4, 1, 4, half // 2, 2 * rows), lambda i: (0, 0, i, 0, 0, 0))],
        [info, (own, one, lambda i: (i, 0, 0)), (peer, one, lambda i: (i, 0, 0))],
        grid=(2,),
        scalars=1,
        nbytes=8 * rows * model,
        name="flip",
    )

    quarter = HD // 4
    frequency = (ROPE_BASE ** (-np.arange(quarter, dtype=np.float64) / quarter)).astype(np.float32)
    angle_r = positions[0].astype(F32)[:, None] * frequency[None, :]
    angle_c = positions[1].astype(F32)[:, None] * frequency[None, :]
    cos_r, sin_r, cos_c, sin_c = jnp.cos(angle_r), jnp.sin(angle_r), jnp.cos(angle_c), jnp.sin(angle_c)
    cos_t = jnp.concatenate([cos_r, cos_r, cos_c, cos_c], axis=1)
    sin_t = jnp.concatenate([-sin_r, sin_r, -sin_c, sin_c], axis=1)

    lin_shape = shape((rows, 4 * cols), F32)
    one_matrix = (1, width, cols)

    def by_matrix(w_j):
        if not isinstance(w_j, list):
            return [(w_j, one_matrix, lambda m: (m, 0, 0))]
        return [
            (w_j[0], one_matrix, lambda m: (jnp.minimum(m, 1), 0, 0)),
            (w_j[1], one_matrix, lambda m: (jnp.maximum(m - 2, 0), 0, 0)),
        ]

    lin = []
    for first, pairs in ((0, 3), (3, 1)):
        span = 2 * pairs * width
        group = shards[2 * first : 2 * (first + pairs)]
        columns = functools.partial(lambda c, m: (m // 3, 0, c), first // pairs)
        acc = ((rows, cols), lambda m: (0, m))
        lin = call(
            functools.partial(linear_kernel, [len(w_j) if isinstance(w_j, list) else 1 for w_j in group]),
            [(lin_shape, *acc)] * 2,
            [(own, (1, rows, span), columns), (peer, (1, rows, span), columns)]
            + [item for w_j in group for item in by_matrix(w_j)]
            + [(value, *acc) for value in lin],
            grid=(4,),
            flops=2 * 2 * rows * 2 * pairs * width * 4 * cols,
            nbytes=2 * pairs * width * 8 * cols + 8 * rows * 2 * pairs * width,
            name="linear",
            after=[] if first else [turned, cos_t, sin_t],
        )
    lin_own, lin_send = lin
    lin_peer = shift(lin_send, dc=1)
    (y_own,) = call(
        attend_kernel,
        [shape((rows, 4 * cols))],
        [lengths, lin_own, lin_peer, cos_t, sin_t],
        scalars=1,
        flops=HEADS * 10 * rows * rows * HD * 2,
        nbytes=10 * rows * 4 * cols,
        name="attend",
    )
    y_peer = shift(y_own, dc=1)

    quarter = half // 2
    piece = shape((4, 8, quarter, 128))

    def terms(steps):
        part = len(steps) / 4
        picks = [functools.partial(lambda step, _: (0, step, 0, 0, 0, 0), step) for step in steps]
        return call(
            functools.partial(terms_kernel, len(steps)),
            [piece] * (2 * len(steps)),
            [(turned, (2, 1, 2, 4, quarter, 2 * rows), pick) for pick in picks] + [y_own, y_peer],
            flops=int(part * 2 * 2 * rows * (model // 2) * 4 * cols),
            nbytes=int(part * (4 * model * cols + 8 * rows * model)),
            name="terms",
        )

    far = terms([2])
    far = [along(far[0], first=1), along(far[1], first=-1)]
    back = terms([3])
    back = [along(back[0], first=-1), along(back[1], first=1)]
    near = terms([1, 0])

    per_u = ((1, 8, quarter, 128), lambda u: (u, 0, 0, 0))
    joined = sum_call(
        join_kernel,
        "join",
        [(piece, *per_u)] * 2,
        [(near[0], *per_u), (far[0], *per_u), (near[1], *per_u), (far[1], *per_u)],
        grid=(4,),
    )
    ahead = [along(joined[0], first=1), along(joined[1], first=-1)]

    def first_three(w_j):
        if not isinstance(w_j, list):
            return [(w_j, (3, width, cols), lambda _: (0, 0, 0))]
        return [w_j[0], (w_j[1], one_matrix, lambda _: (0, 0, 0))]

    g_own, g_send = call(
        functools.partial(normed_grad_kernel, width, [len(first_three(w_j)) for w_j in shards]),
        [shape((rows, model // 2), F32), shape((rows, model // 2))],
        [y_own, y_peer] + [item for w_j in shards for item in first_three(w_j)],
        flops=2 * rows * model * 3 * cols,
        nbytes=4 * model * cols + 4 * rows * model,
        name="normed_grad",
        after=[joined[0]],
    )

    per_n = ((4, 2, quarter, 128), lambda n: (0, n, 0, 0))
    mixed = shape((8, 2, quarter, 128))
    out_n = ((2, 2, quarter, 128), lambda n: (n, 0, 0, 0))
    halfway = sum_call(
        sides_kernel,
        "sides",
        [(mixed, *out_n)] * 4,
        [(value, *per_n) for value in (near[2], back[0], ahead[0], near[3], back[1], ahead[1])],
        grid=(4,),
        after=[g_send],
    )
    g_peer = shift(gate(g_send, [halfway[0]]), dc=1)
    g_rows = ((some, model // 2), lambda i: (i, 0))
    grad_tokens, mark = call(
        functools.partial(token_grad_kernel, width),
        [(shape((rows, model)), (some, model), lambda i: (i, 0)), (shape((8, 128), F32), (8, 128), lambda i: (0, 0))],
        [info, (tokens, (some, model), lambda i: (i, 0)), (g_own, *g_rows), (g_peer, *g_rows)],
        grid=(4,),
        scalars=1,
        scratch=[pltpu.VMEM((some, model), F32)],
        flops=16 * rows * model,
        nbytes=8 * rows * model,
        name="token_grad",
    )

    rest = [along(halfway[d], second=d) for d in range(1, 4)]
    (by_z,) = sum_call(
        seconds_kernel,
        "seconds",
        [(mixed, *out_n)],
        [(value, *out_n) for value in [halfway[0]] + rest],
        grid=(4,),
        after=[mark],
    )
    (spread,) = sum_call(last_kernel, "last", [shape((NZ, 2, quarter, 128))], [exchange(by_z)])
    here = exchange(spread)
    there = permute(here, lambda x, y, z, core: (x + 2, y, z, core))
    dims = (4, shard_rows, cols)
    weight_grads = []
    for blocks, h in ((here, x_hi), (there, 1 - x_hi)):
        blocks = gate(blocks, weight_grads) if weight_grads else blocks
        for c, value in ((core, blocks), (1 - core, shift(blocks, dc=1))):
            weight_grads = [place(jnp.stack([2 * c + h]).astype(jnp.int32), value, dims, weight_grads)]
    (weight_grads,) = weight_grads
    return (grad_tokens, weight_grads)


def solution(mesh):
    return jax.shard_map(
        per_device,
        mesh=mesh,
        in_specs=(
            P(("dp", "fsdp"), None),
            P(("dp", "fsdp"), None),
            P(("dp", "fsdp"), None),
            P(None, ("dp", "fsdp")),
            P(None, "fsdp", None),
        ),
        out_specs=(P(("dp", "fsdp"), None), P(None, "fsdp", None)),
        check_vma=False,
    )
```
